128 devices in a mesh: dom: 64 (over y, x, z), rep: 2 (over core).
Axes of the slice: x: 4, y: 4, z: 4, core: 2. Of those that a mesh axis runs over, the one named last changes fastest.
Arguments:
- node_state: bfloat16 [32768, 384], P(('rep', 'dom')), parts along dimension 0, may hold values from -6 to 6
- edge_state: bfloat16 [131072, 384], P(('rep', 'dom')), parts along dimension 0, may hold values from -6 to 6
- edge_source: int32 [131072], P(('rep', 'dom')), parts along dimension 0, may hold values from 0 to 383
- contact_block: int32 [2048], P(('rep', 'dom')), parts along dimension 0, may hold values from 0 to 1
- contact_host: int32 [2048, 1], P(('rep', 'dom')), parts along dimension 0, may hold values from 0 to 63; in each aligned block of 16 rows (0 to 15, 16 to 31, ...) at most 2 rows name the same one
- contact_remote: int32 [2048], P(('rep', 'dom')), parts along dimension 0, may hold values from 0 to 1
- w_edge_in: bfloat16 [2304, 384], P('rep'), parts along dimension 0, may hold values from -0.1875 to 0.1875
- w_edge_out: bfloat16 [768, 384], P('rep'), parts along dimension 0, may hold values from -0.3125 to 0.3125
- w_node_in: bfloat16 [2304, 384], P('rep'), parts along dimension 0, may hold values from -0.1875 to 0.1875
- w_node_out: bfloat16 [768, 384], P('rep'), parts along dimension 0, may hold values from -0.3125 to 0.3125
- w_contact_in: bfloat16 [1536, 384], P('rep'), parts along dimension 0, may hold values from -0.21875 to 0.21875
- w_contact_out: bfloat16 [768, 384], P('rep'), parts along dimension 0, may hold values from -0.3125 to 0.3125
- node_cot: bfloat16 [32768, 384], P(('rep', 'dom')), parts along dimension 0, may hold values from -6 to 6
- edge_cot: bfloat16 [131072, 384], P(('rep', 'dom')), parts along dimension 0, may hold values from -6 to 6
Outputs:
- node_out: bfloat16 [32768, 384], P(('rep', 'dom')), parts along dimension 0
- edge_out: bfloat16 [131072, 384], P(('rep', 'dom')), parts along dimension 0
- node_grad: bfloat16 [32768, 384], P(('rep', 'dom')), parts along dimension 0
- edge_grad: bfloat16 [131072, 384], P(('rep', 'dom')), parts along dimension 0
- grad_edge_in: float32 [2304, 384], P('rep'), parts along dimension 0
- grad_edge_out: float32 [768, 384], P('rep'), parts along dimension 0
- grad_node_in: float32 [2304, 384], P('rep'), parts along dimension 0
- grad_node_out: float32 [768, 384], P('rep'), parts along dimension 0
- grad_contact_in: float32 [1536, 384], P('rep'), parts along dimension 0
- grad_contact_out: float32 [768, 384], P('rep'), parts along dimension 0
The draws below stay inside these ranges and needn't reach their ends.
There are 2 independent parts, one for each index of `rep`. The reference program is written for one: setup_inputs(seed, part) draws one part's arguments, and reference() takes and returns one part's arrays. A program takes and returns all parts, laid end to end along the dimension named above; each array names one. Nothing has to cross between parts.
Inputs may be any that keep to these rules, and one draw needn't show every extreme that they name: `contact_host`: the 16 rows of one partition name any one host partition at most 2 times, and 2 times in some partition.
All inputs are finite; a program needn't handle non-finite values.
Results may differ from the reference program's by a relative error of at most 0.0082.
Values may be sent and summed in bfloat16 or wider, within the bound.
A program may use at most 128 MiB of HBM per device.

```python
import math
import jax
import jax.numpy as jnp
import numpy as np
from jax import lax

L = 384
BLOCK = 128
EPN = 4
RIM = 64
CAP = 2
NODE_DEV = 256
C_DEV = 16
NODES = 16384
EDGES = 65536
CONTACTS = 1024
N_DOM = 64


def touch_ends(values, own_key, low, largest):
    dims = values.shape
    spot = [jax.random.randint(jax.random.fold_in(own_key, axis), (), 0, dims[axis]) for axis in range(len(dims))]
    values = values.at[tuple(spot)].set(low)
    longest = dims.index(max(dims))
    spot[longest] = (spot[longest] + 1) % dims[longest]
    return values.at[tuple(spot)].set(largest)


def block_scale(rng, shape, cuts, smallest, high):
    loudness, own = 1.0, jax.random.fold_in(rng, 6)
    for dim, parts in cuts:
        heights = jnp.exp(jax.random.uniform(jax.random.fold_in(own, dim), (parts,), jnp.float32, smallest / len(cuts), high / len(cuts)))
        loudness = loudness * jnp.repeat(heights, shape[dim] // parts).reshape([-1 if axis == dim else 1 for axis in range(len(shape))])
    return loudness


def deal_out(own_key, own, number, rows, amount, top, limit, skew):
    order = jax.random.permutation(own_key, amount)
    heavy_load, usual = portions_of(amount, rows * top, limit, skew, True), portions_of(amount, rows * top, limit, skew, False)
    places = jnp.arange(amount)

    def named(lengths, rotation):
        used = int((lengths > 0).sum())
        fixed = max(1, used // 4)
        passed = fixed + (places - fixed + rotation * (used - fixed)) % max(1, amount - fixed)
        return jnp.zeros((amount,), jnp.int32).at[order[jnp.where(places < fixed, places, passed)]].set(jnp.asarray(lengths, jnp.int32))

    lengths = jnp.where(number % 4 == 0, named(heavy_load, number // 4), named(usual, number - number // 4 - 1))
    mixed = jax.random.permutation(jax.random.fold_in(own, 3), amount)
    source_of, taker = mixed[0:amount // 2 * 2:2], mixed[1:amount // 2 * 2:2]
    margin = jnp.minimum(lengths[source_of] - 1, limit - lengths[taker]) // 2
    margin = jnp.where((source_of == order[0]) | (taker == order[0]) | (lengths[taker] == 0), 0, jnp.maximum(margin, 0))
    passed = jax.random.randint(jax.random.fold_in(own, 4), (amount // 2,), 0, 1 << 20) % (margin + 1)
    lengths = lengths.at[source_of].add(-passed).at[taker].add(passed)
    items = jnp.searchsorted(jnp.cumsum(lengths), jnp.arange(rows * top), side="right").astype(jnp.int32)
    grid = items.reshape(top, rows).T
    grid = grid[jax.random.permutation(jax.random.fold_in(own, 1), rows)]
    rotation = jax.random.randint(jax.random.fold_in(own, 2), (rows, 1), 0, top)
    return jnp.take_along_axis(grid, (jnp.arange(top)[None, :] + rotation) % top, axis=1)


def portions_of(number_of, total, most, slope, full):
    weights = [(1 << 20) // math.isqrt(standing ** slope) + 1 for standing in range(1, number_of + 1)]
    largest = most if full else min(most, max(-(-total // number_of), total * weights[0] // sum(weights)))
    least = 1 if total - largest >= number_of - 1 else 0
    holding, surplus = [largest] + [least] * (number_of - 1), total - largest - least * (number_of - 1)
    while surplus > 0:
        free = [i for i in range(1, number_of) if holding[i] < largest] or [i for i in range(1, number_of) if holding[i] < most]
        whole, left = sum([weights[i] for i in free]), surplus
        for i in free:
            more = min(most - holding[i], max(1, left * weights[i] // whole), surplus)
            holding[i] = holding[i] + more
            surplus = surplus - more
    return np.array(holding)


def gaussian(key, extent, scale, limit, pieces=(), kind=jnp.bfloat16):
    loudness = block_scale(key, extent, pieces, -0.22, 0.18) if pieces else 1.0
    array = jax.random.normal(key, extent, jnp.float32) * scale * loudness
    return jnp.minimum(jnp.maximum(array, -limit), limit).astype(kind)


def setup_inputs(seed: int = 0, part: int = 0) -> dict:
    keys = jax.random.split(jax.random.key(seed), 15)
    own_keys = jax.random.split(jax.random.fold_in(keys[14], part), 15)
    node_state = gaussian(own_keys[0], (NODES, L), 1.0, 6.0, ((0, 64),))
    edge_state = gaussian(own_keys[1], (EDGES, L), 1.0, 6.0, ((0, 64),))
    edge_source = touch_ends(jax.random.randint(own_keys[2], (EDGES,), 0, NODE_DEV + 2 * RIM), jax.random.fold_in(own_keys[2], 1), 0, (NODE_DEV + 2 * RIM) - 1).astype(jnp.int32)
    contact_block = touch_ends(jax.random.randint(own_keys[3], (CONTACTS,), 0, NODE_DEV // BLOCK), jax.random.fold_in(own_keys[3], 1), 0, (NODE_DEV // BLOCK) - 1).astype(jnp.int32)
    contact_host_keys = jax.random.split(jax.random.fold_in(own_keys[4], 1), CONTACTS // C_DEV)
    contact_host_turns = jax.random.permutation(jax.random.fold_in(own_keys[4], 3), CONTACTS // C_DEV)
    contact_host = jax.vmap(lambda own, number: deal_out(jax.random.fold_in(own_keys[4], 2), own, number, C_DEV, N_DOM, 1, CAP, 2))(contact_host_keys, contact_host_turns).reshape((CONTACTS, 1))
    contact_remote = touch_ends(jax.random.randint(own_keys[5], (CONTACTS,), 0, NODE_DEV // BLOCK), jax.random.fold_in(own_keys[5], 1), 0, (NODE_DEV // BLOCK) - 1).astype(jnp.int32)
    w_edge_in = gaussian(own_keys[6], (3 * L, L), (3 * L) ** -0.5, 0.1875)
    w_edge_out = gaussian(own_keys[7], (L, L), L ** -0.5, 0.3125)
    w_node_in = gaussian(own_keys[8], (3 * L, L), (3 * L) ** -0.5, 0.1875)
    w_node_out = gaussian(own_keys[9], (L, L), L ** -0.5, 0.3125)
    w_contact_in = gaussian(own_keys[10], (2 * L, L), (2 * L) ** -0.5, 0.21875)
    w_contact_out = gaussian(own_keys[11], (L, L), L ** -0.5, 0.3125)
    node_cot = gaussian(own_keys[12], (NODES, L), 1.0, 6.0, ((0, 64),))
    edge_cot = gaussian(own_keys[13], (EDGES, L), 1.0, 6.0, ((0, 64),))
    return dict(node_state=node_state, edge_state=edge_state, edge_source=edge_source, contact_block=contact_block, contact_host=contact_host, contact_remote=contact_remote, w_edge_in=w_edge_in, w_edge_out=w_edge_out, w_node_in=w_node_in, w_node_out=w_node_out, w_contact_in=w_contact_in, w_contact_out=w_contact_out, node_cot=node_cot, edge_cot=edge_cot)


norm_eps = 1e-05

def layer_norm(values):
    center = values - lax.optimization_barrier(jnp.mean(values, axis=-1, keepdims=True))
    scale = lax.rsqrt(lax.optimization_barrier(jnp.mean(center * center, axis=-1, keepdims=True)) + norm_eps)
    return center * scale

def layer_norm_back(values, upstream):
    center = values - lax.optimization_barrier(jnp.mean(values, axis=-1, keepdims=True))
    scale = lax.rsqrt(lax.optimization_barrier(jnp.mean(center * center, axis=-1, keepdims=True)) + norm_eps)
    normed = center * scale
    first = lax.optimization_barrier(jnp.mean(upstream, axis=-1, keepdims=True))
    second = lax.optimization_barrier(jnp.mean(upstream * normed, axis=-1, keepdims=True))
    return scale * (upstream - first - normed * second)

def forward_mlp(inputs, w_first, w_second):
    hidden_pre = jnp.dot(inputs, w_first, preferred_element_type=jnp.float32)
    hidden = jax.nn.silu(hidden_pre).astype(jnp.bfloat16)
    linear = jnp.dot(hidden, w_second, preferred_element_type=jnp.float32)
    return (hidden_pre, hidden, linear, layer_norm(linear))

def backward_mlp(inputs, hidden_pre, hidden, linear, w_second, upstream):
    d_linear = layer_norm_back(linear, upstream).astype(jnp.bfloat16)
    grad_second = jnp.dot(hidden.T, d_linear, preferred_element_type=jnp.float32)
    d_hidden = jnp.dot(d_linear, w_second.T, preferred_element_type=jnp.float32)
    sigma = jax.nn.sigmoid(hidden_pre)
    d_pre = (d_hidden * sigma * (1.0 + hidden_pre * (1.0 - sigma))).astype(jnp.bfloat16)
    grad_first = jnp.dot(inputs.T, d_pre, preferred_element_type=jnp.float32)
    return (d_pre, grad_first, grad_second)

def reference(node_state, edge_state, edge_source, contact_block, contact_host, contact_remote, w_edge_in, w_edge_out, w_node_in, w_node_out, w_contact_in, w_contact_out, node_cot, edge_cot):
    latent = node_state.shape[1]
    padded = jnp.pad(node_state, ((RIM, RIM), (0, 0)))
    edge_ids = jnp.arange(EDGES, dtype=jnp.int32)
    source_index = edge_ids // (EPN * NODE_DEV) * NODE_DEV + edge_source
    source_rows = padded[source_index]
    target_rows = jnp.repeat(node_state, EPN, axis=0)
    edge_input = jnp.concatenate([edge_state, source_rows, target_rows], axis=1)
    e_pre, e_hidden, e_linear, e_normed = forward_mlp(edge_input, w_edge_in, w_edge_out)
    edge_out = (edge_state.astype(jnp.float32) + e_normed).astype(jnp.bfloat16)
    mesh_sum = edge_out.astype(jnp.float32).reshape(NODES, EPN, latent).sum(axis=1).astype(jnp.bfloat16)
    offsets = jnp.arange(BLOCK, dtype=jnp.int32)
    receiver = jnp.arange(CONTACTS, dtype=jnp.int32) // C_DEV
    own_index = ((receiver * NODE_DEV + contact_block * BLOCK)[:, None] + offsets[None, :]).reshape(-1)
    remote_index = ((contact_host[:, 0] * NODE_DEV + contact_remote * BLOCK)[:, None] + offsets[None, :]).reshape(-1)
    contact_input = jnp.concatenate([node_state[own_index], node_state[remote_index]], axis=1)
    c_pre, c_hidden, c_linear, c_normed = forward_mlp(contact_input, w_contact_in, w_contact_out)
    message = c_normed.astype(jnp.bfloat16)
    contact_sum = jax.ops.segment_sum(message.astype(jnp.float32), own_index, NODES).astype(jnp.bfloat16)
    node_input = jnp.concatenate([node_state, mesh_sum, contact_sum], axis=1)
    n_pre, n_hidden, n_linear, n_normed = forward_mlp(node_input, w_node_in, w_node_out)
    node_out = (node_state.astype(jnp.float32) + n_normed).astype(jnp.bfloat16)
    d_node_pre, grad_node_in, grad_node_out = backward_mlp(node_input, n_pre, n_hidden, n_linear, w_node_out, node_cot.astype(jnp.float32))
    dx_node = jnp.dot(d_node_pre, w_node_in.T, preferred_element_type=jnp.float32)
    grad_h = node_cot.astype(jnp.float32) + dx_node[:, :latent]
    d_mesh = dx_node[:, latent:2 * latent].astype(jnp.bfloat16)
    d_contact = dx_node[:, 2 * latent:].astype(jnp.bfloat16)
    d_edge = edge_cot.astype(jnp.float32) + jnp.repeat(d_mesh.astype(jnp.float32), EPN, axis=0)
    d_edge_pre, grad_edge_in, grad_edge_out = backward_mlp(edge_input, e_pre, e_hidden, e_linear, w_edge_out, d_edge)
    dx_edge = jnp.dot(d_edge_pre, w_edge_in.T, preferred_element_type=jnp.float32)
    edge_grad = (d_edge + dx_edge[:, :latent]).astype(jnp.bfloat16)
    grad_h = grad_h + dx_edge[:, 2 * latent:].reshape(NODES, EPN, latent).sum(axis=1)
    spread = jax.ops.segment_sum(dx_edge[:, latent:2 * latent], source_index, NODES + 2 * RIM)
    grad_h = grad_h + spread[RIM:RIM + NODES]
    d_message = d_contact[own_index].astype(jnp.float32)
    d_contact_pre, grad_contact_in, grad_contact_out = backward_mlp(contact_input, c_pre, c_hidden, c_linear, w_contact_out, d_message)
    d_own = jnp.dot(d_contact_pre, w_contact_in[:latent].T, preferred_element_type=jnp.float32)
    d_remote = jnp.dot(d_contact_pre, w_contact_in[latent:].T, preferred_element_type=jnp.float32).astype(jnp.bfloat16)
    grad_h = grad_h + jax.ops.segment_sum(d_own, own_index, NODES)
    grad_h = grad_h + jax.ops.segment_sum(d_remote.astype(jnp.float32), remote_index, NODES)
    node_grad = grad_h.astype(jnp.bfloat16)
    return (node_out, edge_out, node_grad, edge_grad, grad_edge_in, grad_edge_out, grad_node_in, grad_node_out, grad_contact_in, grad_contact_out)
```

```python
import functools

import jax
import jax.numpy as jnp
from jax import lax
from jax.experimental import pallas as pl
from jax.experimental.pallas import tpu as pltpu
from jax.sharding import PartitionSpec as P

L = 384
BLOCK = 128
EPN = 4
RIM = 64
NODES = 256
EDGES = 1024
ROWS = 16
TILE = 256
COLORS = 3
COLS = 128
SIDE = 4
DOM = 64
EPS = 1e-05
BF = jnp.bfloat16
F32 = jnp.float32
MESH = pl.DeviceIdType.MESH

EDGE_IN, EDGE_OUT, NODE_IN, NODE_OUT, CONTACT_IN, CONTACT_OUT = 0, 1152, 1536, 2688, 3072, 3840
GROWS = 4352
QUARTER = GROWS // 4
PIECE = QUARTER // 4

ORDERS = (("z", "x", "y"), ("x", "y", "z"), ("y", "z", "x"))
STRIDE = {"y": 16, "x": 4, "z": 1}
AXES = ("y", "x", "z")
N_CHUNK = 4
CHUNK = ROWS // N_CHUNK


def mm(a, b):
    return lax.dot_general(a, b, (((1,), (0,)), ((), ())), preferred_element_type=F32)


def mm_nt(a, b):
    return lax.dot_general(a, b, (((1,), (1,)), ((), ())), preferred_element_type=F32)


def mm_tn(a, b):
    return lax.dot_general(a, b, (((0,), (0,)), ((), ())), preferred_element_type=F32)


def row_mean(v):
    return jnp.sum(v, axis=-1, keepdims=True) * (1.0 / L)


def norm(y):
    center = y - row_mean(y)
    scale = lax.rsqrt(row_mean(center * center) + EPS)
    return center * scale, scale


def norm_back(u, scale, g):
    return scale * (g - row_mean(g) - u * row_mean(g * u))


def silu_parts(z):
    s = jax.nn.sigmoid(z)
    return (z * s).astype(BF), s * (1.0 + z * (1.0 - s))


def body(
    x_ref, src_ref, meta_ref, ncot_ref,
    es_hbm, ecot_hbm, wei_hbm, weo_hbm, wni_hbm, wno_hbm, wci_hbm, wco_hbm,
    node_out, edge_out, node_grad, edge_grad, grads_hbm,
    es, ecot, wei, weo, wni, wno, wci, wco,
    plane, sbuf, rbuf, dz_all, r2, r3, r3src,
    g1, g2src, g2, g3, gout,
    halo, rim_out, rim_in, xext, onehot,
    meta_v, meta_s, table_v, table_s,
    src_rows, tgt_rows, e_u, e_r, e_h, e_a, e_dy, e_dz, mesh_sum,
    c_u, c_r, c_h, c_a, c_dy, p_own, csum, dzown, tsum, nbuf, dcon, dmesh,
    local_sem, meta_ss, meta_rs, halo_ss, halo_rs, rim_ss, rim_rs,
    f1_ss, f1_rs, f2_ss, f2_rs, f2b_ss, f2b_rs, f3_ss, f3_rs,
    b1_ss, b1_rs, b1b_ss, b1b_rs, b2_ss, b2_rs, b3_ss, b3_rs,
    g1_ss, g1_rs, g2_ss, g2_rs, g3_ss, g3_rs, g4_ss, g4_rs, g4b_ss, g4b_rs,
    g5_ss, g5_rs, g5b_ss, g5b_rs,
):
    me = lax.axis_index("dom")
    coord = {"y": lax.div(me, 16), "x": lax.rem(lax.div(me, 4), 4), "z": lax.rem(me, 4)}

    def around(axis, off):
        return lax.rem(coord[axis] + off, SIDE)

    def peer(axis, off):
        return me + (around(axis, off) - coord[axis]) * STRIDE[axis]

    up, down = lax.rem(me + 1, DOM), lax.rem(me + DOM - 1, DOM)

    def remote(src, dst, ss, rs, dev):
        return pltpu.make_async_remote_copy(
            src_ref=src, dst_ref=dst, send_sem=ss, recv_sem=rs,
            device_id={"dom": dev}, device_id_type=MESH,
        )

    def arrived(dst, ss, rs, dev):
        remote(dst, dst, ss, rs, dev).wait_recv()

    pending = []

    def send(*args):
        copy = remote(*args)
        copy.start()
        pending.append(copy)

    def flush():
        for copy in pending:
            copy.wait_send()
        pending.clear()

    loads = [
        pltpu.make_async_copy(src, dst, local_sem.at[i])
        for i, (src, dst) in enumerate(
            [(wci_hbm, wci), (es_hbm, es), (wei_hbm, wei), (weo_hbm, weo), (wco_hbm, wco),
             (wni_hbm, wni), (wno_hbm, wno), (ecot_hbm, ecot)]
        )
    ]
    for load in loads:
        load.start()

    barrier = pltpu.get_barrier_semaphore()
    for axis in AXES:
        for off in (1, 2, 3):
            pl.semaphore_signal(barrier, inc=1, device_id={"dom": peer(axis, off)}, device_id_type=MESH)
    pl.semaphore_signal(barrier, inc=1, device_id={"dom": up}, device_id_type=MESH)
    pl.semaphore_signal(barrier, inc=1, device_id={"dom": down}, device_id_type=MESH)

    x = x_ref[...]
    for k, (a1, a2, a3) in enumerate(ORDERS):
        own = (coord[a2] * SIDE + coord[a1]) * 2
        for b in range(2):
            plane[k, own + b] = x_ref[b * BLOCK:(b + 1) * BLOCK, k * COLS:(k + 1) * COLS]
    pl.semaphore_wait(barrier, 11)

    for k, (a1, a2, a3) in enumerate(ORDERS):
        own = (coord[a2] * SIDE + coord[a1]) * 2
        for off in (1, 2, 3):
            part = plane.at[k, pl.ds(own, 2)]
            send(part, part, f1_ss.at[k, off - 1], f1_rs.at[k, off - 1], peer(a1, off))
    send(x_ref.at[pl.ds(NODES - RIM, RIM)], halo.at[0], halo_ss.at[0], halo_rs.at[0], up)
    send(x_ref.at[pl.ds(0, RIM)], halo.at[1], halo_ss.at[1], halo_rs.at[1], down)
    for i, axis in enumerate(AXES):
        meta_v[i, 0] = meta_ref[...]
        for off in (1, 2, 3):
            send(meta_ref, meta_v.at[i, SIDE - off], meta_ss.at[i, off - 1], meta_rs.at[i, off - 1], peer(axis, off))

    lanes = lax.broadcasted_iota(jnp.int32, (BLOCK, L), 1)
    idx = jnp.concatenate([src_ref[...].astype(F32)] * 16, axis=0).T
    for j in range(EDGES // BLOCK):
        col = idx[:, j:j + 1].astype(jnp.int32)
        onehot[j * BLOCK:(j + 1) * BLOCK, :] = jnp.where(col == lanes, 1.0, 0.0).astype(BF)
    for k in range(COLORS):
        for j in range(SIDE):
            dz_all[k, j, ROWS] = jnp.zeros((BLOCK, COLS), BF)
    csum[...] = jnp.zeros_like(csum)
    dzown[...] = jnp.zeros_like(dzown)
    loads[0].wait()
    p_own[...] = mm(x, wci[0:L]).reshape(2, BLOCK, L)

    for k, (a1, a2, a3) in enumerate(ORDERS):
        for off in (1, 2, 3):
            got = (coord[a2] * SIDE + around(a1, SIDE - off)) * 2
            arrived(plane.at[k, pl.ds(got, 2)], f1_ss.at[k, off - 1], f1_rs.at[k, off - 1], peer(a1, off))
        part = plane.at[k, pl.ds(coord[a2] * 8, 8)]
        send(part, part, f2_ss.at[k, 0], f2_rs.at[k, 0], peer(a2, 1))
        send(part, part, f2_ss.at[k, 1], f2_rs.at[k, 1], peer(a2, 3))

    arrived(halo.at[0], halo_ss.at[0], halo_rs.at[0], up)
    arrived(halo.at[1], halo_ss.at[1], halo_rs.at[1], down)
    has_low = (me > 0).astype(F32)
    has_high = (me < DOM - 1).astype(F32)
    xext[0:RIM] = (halo[0].astype(F32) * has_low).astype(BF)
    xext[RIM:RIM + NODES] = x
    xext[RIM + NODES:] = (halo[1].astype(F32) * has_high).astype(BF)

    for load in loads[1:4]:
        load.wait()

    quarter = TILE // EPN
    fan = jnp.where(
        lax.div(lax.broadcasted_iota(jnp.int32, (TILE, quarter), 0), EPN)
        == lax.broadcasted_iota(jnp.int32, (TILE, quarter), 1), 1.0, 0.0,
    ).astype(BF)

    def edge_forward(t):
        rows = pl.ds(pl.multiple_of(t * TILE, TILE), TILE)
        nodes = pl.ds(pl.multiple_of(t * quarter, quarter), quarter)
        state = es[rows]
        src = mm(onehot[rows], xext[...]).astype(BF)
        tgt = mm(fan, x_ref[nodes]).astype(BF)
        z = mm(state, wei[0:L]) + mm(src, wei[L:2 * L]) + mm(tgt, wei[2 * L:])
        a, h = silu_parts(z)
        u, r = norm(mm(a, weo[...]))
        out = (state.astype(F32) + u).astype(BF)
        edge_out[rows] = out
        mesh_sum[nodes] = mm_tn(fan, out).astype(BF)
        e_a[rows] = a
        e_h[rows] = h
        e_u[rows] = u
        e_r[rows] = r

    pl.loop(0, 2)(edge_forward)

    for k, (a1, a2, a3) in enumerate(ORDERS):
        low = pl.ds(around(a2, 3) * 8, 8)
        high = pl.ds(around(a2, 1) * 8, 8)
        arrived(plane.at[k, low], f2_ss.at[k, 0], f2_rs.at[k, 0], peer(a2, 1))
        part = plane.at[k, pl.ds(around(a2, 3) * 8, 4)]
        send(part, part, f2b_ss.at[k, 0], f2b_rs.at[k, 0], peer(a2, 1))
        arrived(plane.at[k, high], f2_ss.at[k, 1], f2_rs.at[k, 1], peer(a2, 3))
        part = plane.at[k, pl.ds(around(a2, 1) * 8 + 4, 4)]
        send(part, part, f2b_ss.at[k, 1], f2b_rs.at[k, 1], peer(a2, 3))

    for i, axis in enumerate(AXES):
        for off in (1, 2, 3):
            arrived(meta_v.at[i, SIDE - off], meta_ss.at[i, off - 1], meta_rs.at[i, off - 1], peer(axis, off))
    lane = lax.broadcasted_iota(jnp.int32, (1, 128), 1)
    mine = [coord[a3] * 32 for a1, a2, a3 in ORDERS]
    sought = lax.rem(lane, 32) + jnp.where(lane < 32, mine[0], jnp.where(lane < 64, mine[1], mine[2]))
    place = lax.broadcasted_iota(jnp.int32, (ROWS, 128), 1)
    for j in range(SIDE):
        asked = [meta_v[AXES.index(a3), j, 8:8 + ROWS] for a1, a2, a3 in ORDERS]
        asked = jnp.where(place < 32, asked[0], jnp.where(place < 64, asked[1], asked[2]))
        first = second = jnp.full((1, 128), ROWS, jnp.int32)
        for c in reversed(range(ROWS)):
            hit = asked[c:c + 1] == sought
            second = jnp.where(hit, first, second)
            first = jnp.where(hit, c, first)
        table_v[2 * j:2 * j + 1] = first
        table_v[2 * j + 1:2 * j + 2] = second
    to_smem = [
        pltpu.make_async_copy(meta_v, meta_s, local_sem.at[8]),
        pltpu.make_async_copy(table_v, table_s, local_sem.at[9]),
    ]
    for copy in to_smem:
        copy.start()

    pl.loop(2, 4)(edge_forward)

    for copy in to_smem:
        copy.wait()
    for k, (a1, a2, a3) in enumerate(ORDERS):
        opposite = around(a2, 2) * 8
        arrived(plane.at[k, pl.ds(opposite, 4)], f2b_ss.at[k, 0], f2b_rs.at[k, 0], peer(a2, 1))
        arrived(plane.at[k, pl.ds(opposite + 4, 4)], f2b_ss.at[k, 1], f2b_rs.at[k, 1], peer(a2, 3))

    for q in range(N_CHUNK):
        for j in (2, 1, 3, 0):
            for k, (a1, a2, a3) in enumerate(ORDERS):
                i = AXES.index(a3)
                for c in range(CHUNK):
                    slot = meta_s[i, j, k, q * CHUNK + c]
                    if j:
                        sbuf[k, j - 1, q * CHUNK + c] = plane[k, slot]
                    else:
                        rbuf[q][k, 0, c] = plane[k, slot]
                if j:
                    send(
                        sbuf.at[k, j - 1, pl.ds(q * CHUNK, CHUNK)], rbuf[q].at[k, SIDE - j],
                        f3_ss.at[q, k, j - 1], f3_rs.at[q, k, j - 1], peer(a3, j),
                    )

    loads[4].wait()
    for q in range(N_CHUNK):
        for k, (a1, a2, a3) in enumerate(ORDERS):
            for j in (1, 2, 3):
                arrived(rbuf[q].at[k, SIDE - j], f3_ss.at[q, k, j - 1], f3_rs.at[q, k, j - 1], peer(a3, j))

        @pl.loop(0, CHUNK // 2)
        def _(p):
            parts, owns, weights = [], [], []
            for s in range(2):
                c = q * CHUNK + 2 * p + s
                cols = []
                for k, (a1, a2, a3) in enumerate(ORDERS):
                    where = lax.rem(meta_s[0, 0, 3 + k, c] - coord[a3] + SIDE, SIDE)
                    cols.append(rbuf[q][k, where, 2 * p + s])
                parts.append(jnp.concatenate(cols, axis=1))
                block = meta_s[0, 0, 6, c]
                owns.append(p_own[block])
                weights.append(block.astype(F32))
            rows = pl.ds(pl.multiple_of(q * CHUNK * BLOCK + p * TILE, TILE), TILE)
            z = mm(jnp.concatenate(parts, axis=0), wci[L:]) + jnp.concatenate(owns, axis=0)
            a, h = silu_parts(z)
            u, r = norm(mm(a, wco[...]))
            c_a[rows] = a
            c_h[rows] = h
            c_u[rows] = u
            c_r[rows] = r
            message = u.astype(BF).astype(F32)
            for s in range(2):
                m = message[s * BLOCK:(s + 1) * BLOCK]
                csum[1] += m * weights[s]
                csum[0] += m * (1.0 - weights[s])

    loads[5].wait()
    loads[6].wait()
    nbuf[:, 0:L] = x
    nbuf[:, L:2 * L] = mesh_sum[...]
    nbuf[:, 2 * L:] = csum[...].reshape(NODES, L).astype(BF)
    a, h = silu_parts(mm(nbuf[...], wni[...]))
    u, r = norm(mm(a, wno[...]))
    node_out[...] = (x.astype(F32) + u).astype(BF)
    ncot = ncot_ref[...].astype(F32)
    n_dy = norm_back(u, r, ncot).astype(BF)
    n_dz = (mm_nt(n_dy, wno[...]) * h).astype(BF)
    dcon[...] = mm_nt(n_dz, wni[2 * L:]).astype(BF).reshape(2, BLOCK, L)

    @pl.loop(0, ROWS // 2)
    def _(t):
        rows = pl.ds(pl.multiple_of(t * TILE, TILE), TILE)
        blocks = [meta_s[0, 0, 6, 2 * t + s] for s in range(2)]
        g = jnp.concatenate([dcon[b] for b in blocks], axis=0).astype(F32)
        dy = norm_back(c_u[rows], c_r[rows], g).astype(BF)
        c_dy[rows] = dy
        dz = (mm_nt(dy, wco[...]) * c_h[rows]).astype(BF)
        for s in range(2):
            part = dz[s * BLOCK:(s + 1) * BLOCK]
            weight = blocks[s].astype(F32)
            dzown[1] += part.astype(F32) * weight
            dzown[0] += part.astype(F32) * (1.0 - weight)
            for k in range(COLORS):
                dz_all[k, 0, 2 * t + s] = part[:, k * COLS:(k + 1) * COLS]
        for k, (a1, a2, a3) in enumerate(ORDERS):
            pair = pl.ds(2 * t, 2)
            remote(dz_all.at[k, 0, pair], dz_all.at[k, 3, pair], b1_ss.at[k, 0, t], b1_rs.at[k, 0, t], peer(a3, 1)).start()
            remote(dz_all.at[k, 0, pair], dz_all.at[k, 1, pair], b1_ss.at[k, 1, t], b1_rs.at[k, 1, t], peer(a3, 3)).start()

    def put(row, value):
        value = value.astype(BF)
        count = value.shape[0]
        for k in range(COLORS):
            sbuf_rows = value[:, k * COLS:(k + 1) * COLS].reshape(count // BLOCK, BLOCK, COLS)
            for i in range(count // BLOCK):
                g = row // BLOCK + i
                gsend(k, g)[...] = sbuf_rows[i]

    flush()

    def gsend(k, g):
        return sbuf.at[k, g // ROWS, g % ROWS]

    dmesh[...] = mm_nt(n_dz, wni[L:2 * L]).astype(BF)
    loads[7].wait()

    def edge_backward(t):
        rows = pl.ds(pl.multiple_of(t * TILE, TILE), TILE)
        nodes = pl.ds(pl.multiple_of(t * quarter, quarter), quarter)
        g = ecot[rows].astype(F32) + mm(fan, dmesh[nodes])
        dy = norm_back(e_u[rows], e_r[rows], g).astype(BF)
        dz = (mm_nt(dy, weo[...]) * e_h[rows]).astype(BF)
        edge_grad[rows] = (g + mm_nt(dz, wei[0:L])).astype(BF)
        tsum[nodes] = mm_tn(fan, dz).astype(BF)
        e_dy[rows] = dy
        e_dz[rows] = dz

    @pl.loop(0, 4)
    def _(t):
        edge_backward(t)
        for k, (a1, a2, a3) in enumerate(ORDERS):
            pair = pl.ds(2 * t, 2)
            arrived(dz_all.at[k, 3, pair], b1_ss.at[k, 0, t], b1_rs.at[k, 0, t], peer(a3, 1))
            remote(dz_all.at[k, 3, pair], dz_all.at[k, 2, pair], b1b_ss.at[k, t], b1b_rs.at[k, t], peer(a3, 1)).start()
            late = t + 4
            pair = pl.ds(2 * late, 2)
            arrived(dz_all.at[k, 1, pair], b1_ss.at[k, 1, late], b1_rs.at[k, 1, late], peer(a3, 3))
            remote(dz_all.at[k, 1, pair], dz_all.at[k, 2, pair], b1b_ss.at[k, late], b1b_rs.at[k, late], peer(a3, 3)).start()

    spread = mm_tn(onehot[...], e_dz[...])
    spread_low = spread.astype(BF)
    rim_out[0] = spread_low[0:RIM]
    rim_out[1] = spread_low[RIM + NODES:]
    send(rim_out.at[0], rim_in.at[0], rim_ss.at[0], rim_rs.at[0], down)
    send(rim_out.at[1], rim_in.at[1], rim_ss.at[1], rim_rs.at[1], up)
    put(EDGE_IN + L, mm_tn(xext[...], spread_low))
    put(EDGE_IN, mm_tn(es[...], e_dz[...]))
    put(EDGE_IN + 2 * L, mm_tn(x, tsum[...]))
    put(EDGE_OUT, mm_tn(e_a[...], e_dy[...]))

    @pl.loop(0, 4)
    def _(t):
        late = t + 4
        for k, (a1, a2, a3) in enumerate(ORDERS):
            arrived(dz_all.at[k, 3, pl.ds(2 * late, 2)], b1_ss.at[k, 0, late], b1_rs.at[k, 0, late], peer(a3, 1))
            arrived(dz_all.at[k, 1, pl.ds(2 * t, 2)], b1_ss.at[k, 1, t], b1_rs.at[k, 1, t], peer(a3, 3))
            arrived(dz_all.at[k, 2, pl.ds(2 * t, 2)], b1b_ss.at[k, t], b1b_rs.at[k, t], peer(a3, 1))
            arrived(dz_all.at[k, 2, pl.ds(2 * late, 2)], b1b_ss.at[k, late], b1b_rs.at[k, late], peer(a3, 3))

    @pl.loop(0, 2 * 16)
    def _(s):
        for k in range(COLORS):
            total = jnp.zeros((BLOCK, COLS), F32)
            for j in range(SIDE):
                for i in range(2):
                    total += dz_all[k, j, table_s[2 * j + i, k * 32 + s]].astype(F32)
            plane[k, s] = total.astype(BF)

    for k, (a1, a2, a3) in enumerate(ORDERS):
        for off in (2, 1, 3):
            send(
                plane.at[k, pl.ds(around(a2, off) * 8, 8)], r2.at[k, off - 1],
                b2_ss.at[k, off - 1], b2_rs.at[k, off - 1], peer(a2, off),
            )
    put(CONTACT_OUT, mm_tn(c_a[...], c_dy[...]))
    put(CONTACT_IN, mm_tn(x, dzown[...].reshape(NODES, L).astype(BF)))
    put(NODE_OUT, mm_tn(a, n_dy))
    for i in range(3):
        put(NODE_IN + i * L, mm_tn(nbuf[:, i * L:(i + 1) * L], n_dz))
    grad = ncot + mm_nt(n_dz, wni[0:L]) + mm_nt(tsum[...], wei[2 * L:])
    grad += mm_nt(dzown[...].reshape(NODES, L).astype(BF), wci[0:L])

    for k, (a1, a2, a3) in enumerate(ORDERS):
        for off in (1, 2, 3):
            arrived(r2.at[k, off - 1], b2_ss.at[k, off - 1], b2_rs.at[k, off - 1], peer(a2, off))

        @pl.loop(0, 8)
        def _(s):
            total = plane[k, coord[a2] * 8 + s].astype(F32)
            for o in range(3):
                total += r2[k, o, s].astype(F32)
            r3src[k, s] = total.astype(BF)

        for off in (1, 2, 3):
            send(
                r3src.at[k, pl.ds(around(a1, off) * 2, 2)], r3.at[k, off - 1],
                b3_ss.at[k, off - 1], b3_rs.at[k, off - 1], peer(a1, off),
            )
    arrived(rim_in.at[0], rim_ss.at[0], rim_rs.at[0], down)
    arrived(rim_in.at[1], rim_ss.at[1], rim_rs.at[1], up)
    first = spread[RIM:2 * RIM] + rim_in[1].astype(F32) * has_low
    last = spread[NODES:NODES + RIM] + rim_in[0].astype(F32) * has_high
    own_spread = jnp.concatenate([first, spread[2 * RIM:NODES], last], axis=0).astype(BF)
    grad += mm_nt(own_spread, wei[L:2 * L])
    cols = []
    for k, (a1, a2, a3) in enumerate(ORDERS):
        halves = [r3src[k, coord[a1] * 2 + b].astype(F32) for b in range(2)]
        for off in (1, 2, 3):
            arrived(r3.at[k, off - 1], b3_ss.at[k, off - 1], b3_rs.at[k, off - 1], peer(a1, off))
            halves = [halves[b] + r3[k, off - 1, b].astype(F32) for b in range(2)]
        cols.append(jnp.concatenate(halves, axis=0).astype(BF))
    s_rem = jnp.concatenate(cols, axis=1)
    put(CONTACT_IN + L, mm_tn(x, s_rem))
    node_grad[...] = (grad + mm_nt(s_rem, wci[L:])).astype(BF)

    def rows_of(k, quarter_index):
        return gflat.at[k, pl.ds(quarter_index * QUARTER, QUARTER)]

    gflat = sbuf.reshape(COLORS, 3 * ROWS * BLOCK, COLS)
    for k, (a1, a2, a3) in enumerate(ORDERS):
        for off in (2, 1, 3):
            send(rows_of(k, around(a3, off)), g1.at[k, off - 1], g1_ss.at[k, off - 1], g1_rs.at[k, off - 1], peer(a3, off))
    for k, (a1, a2, a3) in enumerate(ORDERS):
        for off in (1, 2, 3):
            arrived(g1.at[k, off - 1], g1_ss.at[k, off - 1], g1_rs.at[k, off - 1], peer(a3, off))

        @pl.loop(0, 4)
        def _(t):
            rows = pl.ds(pl.multiple_of(t * PIECE, 16), PIECE)
            total = gflat[k, pl.ds(pl.multiple_of(coord[a3] * QUARTER + t * PIECE, 16), PIECE)].astype(F32)
            for o in range(3):
                total += g1[k, o, rows].astype(F32)
            g2src[k, t] = total.astype(BF)

        for off in (2, 1, 3):
            send(g2src.at[k, around(a2, off)], g2.at[k, off - 1], g2_ss.at[k, off - 1], g2_rs.at[k, off - 1], peer(a2, off))
    for k, (a1, a2, a3) in enumerate(ORDERS):
        for off in (1, 2, 3):
            arrived(g2.at[k, off - 1], g2_ss.at[k, off - 1], g2_rs.at[k, off - 1], peer(a2, off))
        total = g2src[k, coord[a2]].astype(F32)
        for o in range(3):
            total += g2[k, o].astype(F32)
        g3[k, coord[a1]] = total.astype(BF)
        for off in (2, 1, 3):
            part = g3.at[k, coord[a1]]
            send(part, part, g3_ss.at[k, off - 1], g3_rs.at[k, off - 1], peer(a1, off))
    for k, (a1, a2, a3) in enumerate(ORDERS):
        for off in (1, 2, 3):
            arrived(g3.at[k, around(a1, SIDE - off)], g3_ss.at[k, off - 1], g3_rs.at[k, off - 1], peer(a1, off))
        total = g3[k, 0].astype(F32)
        for o in range(1, SIDE):
            total += g3[k, o].astype(F32)
        gout[k, coord[a3], coord[a2]] = total.astype(BF)
        part = gout.at[k, coord[a3], coord[a2]]
        for off in (2, 1, 3):
            send(part, part, g4_ss.at[k, off - 1], g4_rs.at[k, off - 1], peer(a2, off))
    for k, (a1, a2, a3) in enumerate(ORDERS):
        for off in (1, 2, 3):
            arrived(
                gout.at[k, coord[a3], around(a2, SIDE - off)],
                g4_ss.at[k, off - 1], g4_rs.at[k, off - 1], peer(a2, off),
            )
        part = gout.at[k, coord[a3]]
        send(part, part, g5_ss.at[k, 0], g5_rs.at[k, 0], peer(a3, 1))
        send(part, part, g5_ss.at[k, 1], g5_rs.at[k, 1], peer(a3, 3))
    for k, (a1, a2, a3) in enumerate(ORDERS):
        arrived(gout.at[k, around(a3, 3)], g5_ss.at[k, 0], g5_rs.at[k, 0], peer(a3, 1))
        part = gout.at[k, around(a3, 3), pl.ds(0, 2)]
        send(part, part, g5b_ss.at[k, 0], g5b_rs.at[k, 0], peer(a3, 1))
        arrived(gout.at[k, around(a3, 1)], g5_ss.at[k, 1], g5_rs.at[k, 1], peer(a3, 3))
        part = gout.at[k, around(a3, 1), pl.ds(2, 2)]
        send(part, part, g5b_ss.at[k, 1], g5b_rs.at[k, 1], peer(a3, 3))
    for k, (a1, a2, a3) in enumerate(ORDERS):
        arrived(gout.at[k, around(a3, 2), pl.ds(0, 2)], g5b_ss.at[k, 0], g5b_rs.at[k, 0], peer(a3, 1))
        arrived(gout.at[k, around(a3, 2), pl.ds(2, 2)], g5b_ss.at[k, 1], g5b_rs.at[k, 1], peer(a3, 3))
    out = pltpu.make_async_copy(gout, grads_hbm, local_sem.at[10])
    out.start()

    @pl.loop(0, 8)
    def _(t):
        for k, (a1, a2, a3) in enumerate(ORDERS):
            part = dz_all.at[k, 0, pl.ds(2 * t, 2)]
            remote(part, part, b1_ss.at[k, 0, t], b1_rs.at[k, 0, t], peer(a3, 1)).wait_send()
            remote(part, part, b1_ss.at[k, 1, t], b1_rs.at[k, 1, t], peer(a3, 3)).wait_send()
            remote(part, part, b1b_ss.at[k, t], b1b_rs.at[k, t], peer(a3, 1)).wait_send()

    flush()
    out.wait()


def dma(*shape):
    return pltpu.SemaphoreType.DMA(shape)


def vm(shape, dtype):
    return pltpu.VMEM(shape, dtype)


def fused(x, src, meta, ncot, es, ecot, wei, weo, wni, wno, wci, wco):
    tile = (BLOCK, COLS)
    scratch = [
        vm((EDGES, L), BF), vm((EDGES, L), BF), vm((3 * L, L), BF), vm((L, L), BF), vm((3 * L, L), BF),
        vm((L, L), BF), vm((2 * L, L), BF), vm((L, L), BF),
        vm((COLORS, 32) + tile, BF),
        vm((COLORS, 3, ROWS) + tile, BF),
        [vm((COLORS, SIDE, CHUNK) + tile, BF) for _ in range(N_CHUNK)],
        vm((COLORS, SIDE, ROWS + 1) + tile, BF),
        vm((COLORS, 3, 8) + tile, BF), vm((COLORS, 3, 2) + tile, BF), vm((COLORS, 8) + tile, BF),
        vm((COLORS, 3, QUARTER, COLS), BF), vm((COLORS, SIDE, PIECE, COLS), BF), vm((COLORS, 3, PIECE, COLS), BF),
        vm((COLORS, SIDE, PIECE, COLS), BF), vm((COLORS, SIDE, SIDE, PIECE, COLS), BF),
        vm((2, RIM, L), BF), vm((2, RIM, L), BF), vm((2, RIM, L), BF), vm((NODES + 2 * RIM, L), BF), vm((EDGES, L), BF),
        vm((3, SIDE, 24, 128), jnp.int32), pltpu.SMEM((3, SIDE, 24, 128), jnp.int32),
        vm((8, 128), jnp.int32), pltpu.SMEM((8, 128), jnp.int32),
        vm((16, 128), BF), vm((16, 128), BF), vm((EDGES, L), F32), vm((EDGES, 1), F32), vm((EDGES, L), F32), vm((EDGES, L), BF),
        vm((EDGES, L), BF), vm((EDGES, L), BF), vm((NODES, L), BF),
        vm((ROWS * BLOCK, L), F32), vm((ROWS * BLOCK, 1), F32), vm((ROWS * BLOCK, L), F32), vm((ROWS * BLOCK, L), BF),
        vm((ROWS * BLOCK, L), BF), vm((2, BLOCK, L), F32), vm((2, BLOCK, L), F32), vm((2, BLOCK, L), F32),
        vm((NODES, L), BF), vm((NODES, 3 * L), BF), vm((2, BLOCK, L), BF), vm((NODES, L), BF),
        dma(11), dma(3, 3), dma(3, 3), dma(2), dma(2), dma(2), dma(2),
        dma(3, 3), dma(3, 3), dma(3, 2), dma(3, 2), dma(3, 2), dma(3, 2), dma(N_CHUNK, 3, 3), dma(N_CHUNK, 3, 3),
        dma(3, 2, 8), dma(3, 2, 8), dma(3, 8), dma(3, 8), dma(3, 3), dma(3, 3), dma(3, 3), dma(3, 3),
        dma(3, 3), dma(3, 3), dma(3, 3), dma(3, 3), dma(3, 3), dma(3, 3), dma(3, 3), dma(3, 3), dma(3, 2), dma(3, 2),
        dma(3, 2), dma(3, 2), dma(3, 2), dma(3, 2),
    ]
    here = pl.BlockSpec(memory_space=pltpu.VMEM)
    there = pl.BlockSpec(memory_space=pl.ANY)
    return pl.pallas_call(
        body,
        out_shape=(
            jax.ShapeDtypeStruct((NODES, L), BF), jax.ShapeDtypeStruct((EDGES, L), BF),
            jax.ShapeDtypeStruct((NODES, L), BF), jax.ShapeDtypeStruct((EDGES, L), BF),
            jax.ShapeDtypeStruct((COLORS, SIDE, SIDE, PIECE, COLS), BF),
        ),
        in_specs=[here] * 4 + [there] * 8,
        out_specs=[here] * 4 + [there],
        scratch_shapes=scratch,
        compiler_params=pltpu.CompilerParams(
            collective_id=0, has_side_effects=True, vmem_limit_bytes=63 * 1024 * 1024
        ),
        name="layer",
    )(x, src, meta, ncot, es, ecot, wei, weo, wni, wno, wci, wco)


def on_device(
    node_state, edge_state, edge_source, contact_block, contact_host, contact_remote,
    w_edge_in, w_edge_out, w_node_in, w_node_out, w_contact_in, w_contact_out, node_cot, edge_cot,
):
    host = contact_host[:, 0]
    hy, hx, hz = host // 16, host // 4 % 4, host % 4
    at = {"y": hy, "x": hx, "z": hz}
    lines = [(at[a2] * SIDE + at[a1]) * 2 + contact_remote for a1, a2, a3 in ORDERS]
    lines += [at[a3] for a1, a2, a3 in ORDERS]
    lines += [contact_block, contact_block]
    meta = jnp.pad(jnp.stack(lines), ((0, 0), (0, 128 - ROWS)))
    asked = [jnp.broadcast_to((lines[3 + k] * 32 + lines[k])[:, None], (ROWS, 32)) for k in (0, 1, 2, 2)]
    meta = jnp.concatenate([meta, jnp.concatenate(asked, axis=1)], axis=0)
    node_out, edge_out, node_grad, edge_grad, packed = fused(
        node_state, edge_source.reshape(8, 128), meta, node_cot, edge_state, edge_cot,
        w_edge_in, w_edge_out, w_node_in, w_node_out, w_contact_in, w_contact_out,
    )
    packed = packed.reshape(COLORS, GROWS, COLS)

    def grad(row, count):
        return jnp.concatenate([packed[k, row:row + count] for k in range(COLORS)], axis=1).astype(F32)

    return (
        node_out, edge_out, node_grad, edge_grad,
        grad(EDGE_IN, 3 * L), grad(EDGE_OUT, L), grad(NODE_IN, 3 * L), grad(NODE_OUT, L),
        grad(CONTACT_IN, 2 * L), grad(CONTACT_OUT, L),
    )


def solution(mesh):
    rows = P(("rep", "dom"), None)
    flat = P(("rep", "dom"))
    weight = P("rep", None)
    return jax.shard_map(
        on_device,
        mesh=mesh,
        in_specs=(rows, rows, flat, flat, rows, flat) + (weight,) * 6 + (rows, rows),
        out_specs=(rows,) * 4 + (weight,) * 6,
        check_vma=False,
    )
```

```python
import functools

import jax
import jax.numpy as jnp
from jax import lax
from jax.experimental import pallas as pl
from jax.experimental.pallas import tpu as pltpu
from jax.sharding import PartitionSpec as P

L = 384
BLOCK = 128
EPN = 4
RIM = 64
NODES = 256
EDGES = 1024
ROWS = 16
TILE = 256
COLORS = 3
COLS = 128
SIDE = 4
DOM = 64
EPS = 1e-05
BF = jnp.bfloat16
F32 = jnp.float32
MESH = pl.DeviceIdType.MESH

GROUPS = (1536, 1280, 1536)
NODE_G, CONTACT_G, EDGE_G = 0, 1, 2

ORDERS = (("z", "x", "y"), ("x", "y", "z"), ("y", "z", "x"))
STRIDE = {"y": 16, "x": 4, "z": 1}
AXES = ("y", "x", "z")
N_CHUNK = 4
S_META, S_HALO, S_RIM, S_F1, S_F2, S_F2B, S_H, S_F3, S_B1, S_B1B, S_B2, S_B3, S_G = range(13)
R_META, R_HALO, R_RIM, R_F1, R_F2, R_F2B, R_H, R_F3, R_B1, R_B1B, R_B2, R_B3, R_G = (
    0, 1, 2, 3, 6, 9, 10, 14, 18, 26, 27, 28, 29
)
CHUNK = ROWS // N_CHUNK
HALF = BLOCK // 2


def mm(a, b):
    return lax.dot_general(a, b, (((1,), (0,)), ((), ())), preferred_element_type=F32)


def mm_nt(a, b):
    return lax.dot_general(a, b, (((1,), (1,)), ((), ())), preferred_element_type=F32)


def mm_tn(a, b):
    return lax.dot_general(a, b, (((0,), (0,)), ((), ())), preferred_element_type=F32)


def row_mean(v):
    return jnp.sum(v, axis=-1, keepdims=True) * (1.0 / L)


def norm(y):
    center = y - row_mean(y)
    scale = lax.rsqrt(row_mean(center * center) + EPS)
    return center * scale, scale


def norm_back(u, scale, g):
    return scale * (g - row_mean(g) - u * row_mean(g * u))


def silu_parts(z):
    s = jax.nn.sigmoid(z)
    return (z * s).astype(BF), s * (1.0 + z * (1.0 - s))


def body(
    x_ref, src_ref, ncot_ref, block_ref, host_ref, remote_ref,
    es_hbm, ecot_hbm, wei_hbm, weo_hbm, wni_hbm, wno_hbm, wci_hbm, wco_hbm,
    node_out_hbm, edge_out_hbm, node_grad_hbm, edge_grad_hbm, node_hbm, contact_hbm, edge_hbm,
    es, ecot, wei, weo, wni, wno, wci, wco,
    plane, hs, hr, sbuf, rbuf, dz_all, r2, r3, r3src,
    gsend, g1, g2src, g2, g3, gout, node_out, edge_out, node_grad, edge_grad,
    halo, rim_out, rim_in, xext, onehot,
    meta_v, meta_s, table_v, table_s,
    e_u, e_r, e_h, e_a, e_dy, e_dz, mesh_sum,
    c_x, c_u, c_r, c_h, c_a, c_dy, p_own, csum, dzown, tsum, nbuf, dcon, dmesh,
    local_sem, ss, rs,
):
    me = lax.axis_index("dom")
    coord = {"y": lax.div(me, 16), "x": lax.rem(lax.div(me, 4), 4), "z": lax.rem(me, 4)}

    def around(axis, off):
        return lax.rem(coord[axis] + off, SIDE)

    def peer(axis, off):
        return me + (around(axis, off) - coord[axis]) * STRIDE[axis]

    up, down = lax.rem(me + 1, DOM), lax.rem(me + DOM - 1, DOM)

    def remote(src, dst, to, at, dev):
        return pltpu.make_async_remote_copy(
            src_ref=src, dst_ref=dst, send_sem=ss.at[to], recv_sem=rs.at[at],
            device_id={"dom": dev}, device_id_type=MESH,
        )

    def arrived(ref, sem):
        remote(ref, ref, 0, sem, up).wait_recv()

    def sent(ref, sem):
        remote(ref, ref, sem, 0, up).wait_send()

    def send(*args):
        remote(*args).start()

    loads = [
        pltpu.make_async_copy(src, dst, local_sem.at[i])
        for i, (src, dst) in enumerate(
            [(wci_hbm, wci), (es_hbm, es), (wei_hbm, wei), (weo_hbm, weo), (wco_hbm, wco),
             (wni_hbm, wni), (wno_hbm, wno), (ecot_hbm, ecot)]
        )
    ]
    for load in loads:
        load.start()

    outs = []

    def write(src, dst, i):
        out = pltpu.make_async_copy(src, dst, local_sem.at[i])
        out.start()
        outs.append(out)

    barrier = pltpu.get_barrier_semaphore()
    for axis in AXES:
        for off in (1, 2, 3):
            pl.semaphore_signal(barrier, inc=1, device_id={"dom": peer(axis, off)}, device_id_type=MESH)
    pl.semaphore_signal(barrier, inc=1, device_id={"dom": up}, device_id_type=MESH)
    pl.semaphore_signal(barrier, inc=1, device_id={"dom": down}, device_id_type=MESH)

    x = x_ref[...]
    place = lax.broadcasted_iota(jnp.int32, (1, 128), 1)
    for c in range(ROWS):
        host = host_ref[c]
        at = {"y": lax.div(host, 16), "x": lax.rem(lax.div(host, 4), 4), "z": lax.rem(host, 4)}
        code = [((at[a3] * SIDE + at[a2]) * SIDE + at[a1]) * 2 + remote_ref[c] for a1, a2, a3 in ORDERS]
        line = jnp.where(place < 32, code[0], jnp.where(place < 64, code[1], code[2]))
        line = jnp.where(place < 96, line, block_ref[c])
        for i in range(3):
            meta_v[i, 0, c:c + 1] = line
    for k, (a1, a2, a3) in enumerate(ORDERS):
        own = (coord[a2] * SIDE + coord[a1]) * 2
        for b in range(2):
            plane[k, own + b] = x_ref[b * BLOCK:(b + 1) * BLOCK, k * COLS:(k + 1) * COLS]
    pl.semaphore_wait(barrier, 11)

    for k, (a1, a2, a3) in enumerate(ORDERS):
        own = (coord[a2] * SIDE + coord[a1]) * 2
        for off in (1, 2, 3):
            part = plane.at[k, pl.ds(own, 2)]
            send(part, part, S_F1, R_F1 + k, peer(a1, off))
    send(x_ref.at[pl.ds(NODES - RIM, RIM)], halo.at[0], S_HALO, R_HALO, up)
    send(x_ref.at[pl.ds(0, RIM)], halo.at[1], S_HALO, R_HALO, down)
    for i, axis in enumerate(AXES):
        for off in (1, 2, 3):
            send(meta_v.at[i, 0], meta_v.at[i, SIDE - off], S_META, R_META, peer(axis, off))

    lanes = lax.broadcasted_iota(jnp.int32, (BLOCK, L), 1)
    idx = jnp.concatenate([src_ref[...].astype(F32)] * 16, axis=0).T
    for j in range(EDGES // BLOCK):
        col = idx[:, j:j + 1].astype(jnp.int32)
        onehot[j * BLOCK:(j + 1) * BLOCK, :] = jnp.where(col == lanes, 1.0, 0.0).astype(BF)
    for k in range(COLORS):
        for j in range(SIDE):
            dz_all[k, j, ROWS] = jnp.zeros((BLOCK, COLS), BF)
    csum[...] = jnp.zeros_like(csum)
    dzown[...] = jnp.zeros_like(dzown)
    loads[0].wait()
    p_own[...] = mm(x, wci[0:L]).reshape(2, BLOCK, L)

    for k, (a1, a2, a3) in enumerate(ORDERS):
        arrived(plane.at[k, pl.ds(0, 6)], R_F1 + k)
        part = plane.at[k, pl.ds(coord[a2] * 8, 8)]
        send(part, part, S_F2, R_F2 + k, peer(a2, 1))
        send(part, part, S_F2, R_F2 + k, peer(a2, 3))

    arrived(halo, R_HALO)
    has_low = (me > 0).astype(F32)
    has_high = (me < DOM - 1).astype(F32)
    xext[0:RIM] = (halo[0].astype(F32) * has_low).astype(BF)
    xext[RIM:RIM + NODES] = x
    xext[RIM + NODES:] = (halo[1].astype(F32) * has_high).astype(BF)

    arrived(meta_v.at[:, pl.ds(1, 3)], R_META)
    mine = [coord[a3] * 32 for a1, a2, a3 in ORDERS]
    sought = lax.rem(place, 32) + jnp.where(place < 32, mine[0], jnp.where(place < 64, mine[1], mine[2]))
    wide = lax.broadcasted_iota(jnp.int32, (ROWS, 128), 1)
    for j in range(SIDE):
        asked = [meta_v[AXES.index(a3), j] for a1, a2, a3 in ORDERS]
        asked = jnp.where(wide < 32, asked[0], jnp.where(wide < 64, asked[1], asked[2]))
        first = second = jnp.full((1, 128), ROWS, jnp.int32)
        for c in reversed(range(ROWS)):
            hit = asked[c:c + 1] == sought
            second = jnp.where(hit, first, second)
            first = jnp.where(hit, c, first)
        table_v[2 * j:2 * j + 1] = first
        table_v[2 * j + 1:2 * j + 2] = second
    to_smem = [
        pltpu.make_async_copy(meta_v, meta_s, local_sem.at[8]),
        pltpu.make_async_copy(table_v, table_s, local_sem.at[9]),
    ]
    for copy in to_smem:
        copy.start()

    for load in loads[1:4]:
        load.wait()

    quarter = TILE // EPN
    fan = jnp.where(
        lax.div(lax.broadcasted_iota(jnp.int32, (TILE, quarter), 0), EPN)
        == lax.broadcasted_iota(jnp.int32, (TILE, quarter), 1), 1.0, 0.0,
    ).astype(BF)

    def edge_forward(t):
        rows = pl.ds(pl.multiple_of(t * TILE, TILE), TILE)
        nodes = pl.ds(pl.multiple_of(t * quarter, quarter), quarter)
        state = es[rows]
        src = mm(onehot[rows], xext[...]).astype(BF)
        tgt = mm(fan, x_ref[nodes]).astype(BF)
        z = mm(state, wei[0:L]) + mm(src, wei[L:2 * L]) + mm(tgt, wei[2 * L:])
        a, h = silu_parts(z)
        u, r = norm(mm(a, weo[...]))
        out = (state.astype(F32) + u).astype(BF)
        edge_out[rows] = out
        mesh_sum[nodes] = mm_tn(fan, out).astype(BF)
        e_a[rows] = a
        e_h[rows] = h
        e_u[rows] = u.astype(BF)
        e_r[rows] = r

    for k, (a1, a2, a3) in enumerate(ORDERS):
        arrived(plane.at[k, pl.ds(0, 16)], R_F2 + k)
        part = plane.at[k, pl.ds(around(a2, 3) * 8, 4)]
        send(part, part, S_F2B, R_F2B, peer(a2, 1))
        part = plane.at[k, pl.ds(around(a2, 1) * 8 + 4, 4)]
        send(part, part, S_F2B, R_F2B, peer(a2, 3))

    edge_forward(0)

    for copy in to_smem:
        copy.wait()
    arrived(plane.at[:, pl.ds(0, 8)], R_F2B)

    def request(k, j, c):
        code = meta_s[AXES.index(ORDERS[k][2]), j, c, k * 32]
        return lax.rem(code, 32), lax.div(code, 32)

    for q in range(N_CHUNK):
        for k, (a1, a2, a3) in enumerate(ORDERS):
            for c in range(CHUNK):
                slot, _ = request(k, 2, q * CHUNK + c)
                hs[k, 0, q * CHUNK + c] = plane[k, slot, 0:HALF]
                hs[k, 1, q * CHUNK + c] = plane[k, slot, HALF:]
            part = pl.ds(q * CHUNK, CHUNK)
            send(hs.at[k, 0, part], hr[q].at[k, 0], S_H, R_H + q, peer(a3, 3))
            send(hs.at[k, 1, part], hr[q].at[k, 1], S_H, R_H + q, peer(a3, 1))
    for q in range(N_CHUNK):
        arrived(hr[q], R_H + q)
        for k, (a1, a2, a3) in enumerate(ORDERS):
            for c in range(CHUNK):
                row = q * CHUNK + c
                slot, where = request(k, 3, row)
                own = where == coord[a3]
                sbuf[k, 0, row, 0:HALF] = jnp.where(own, plane[k, slot, 0:HALF], hr[q][k, 0, c])
                sbuf[k, 0, row, HALF:] = plane[k, slot, HALF:]
                slot, where = request(k, 1, row)
                own = where == coord[a3]
                sbuf[k, 1, row, 0:HALF] = plane[k, slot, 0:HALF]
                sbuf[k, 1, row, HALF:] = jnp.where(own, plane[k, slot, HALF:], hr[q][k, 1, c])
            part = pl.ds(q * CHUNK, CHUNK)
            send(sbuf.at[k, 0, part], rbuf[q].at[k, 1], S_F3, R_F3 + q, peer(a3, 3))
            send(sbuf.at[k, 1, part], rbuf[q].at[k, 2], S_F3, R_F3 + q, peer(a3, 1))
        for k in range(COLORS):
            for c in range(CHUNK):
                rbuf[q][k, 0, c] = plane[k, request(k, 0, q * CHUNK + c)[0]]
        if q < 3:
            edge_forward(q + 1)

    loads[4].wait()
    for q in range(N_CHUNK):
        arrived(rbuf[q].at[:, pl.ds(1, 2)], R_F3 + q)

        @pl.loop(0, CHUNK // 2)
        def _(p):
            parts, owns, weights = [], [], []
            for s in range(2):
                c = q * CHUNK + 2 * p + s
                cols = []
                for k, (a1, a2, a3) in enumerate(ORDERS):
                    away = lax.rem(request(k, 0, c)[1] - coord[a3] + SIDE, SIDE)
                    cols.append(jnp.concatenate([
                        rbuf[q][k, lax.div(away + 1, 2), 2 * p + s, 0:HALF],
                        rbuf[q][k, jnp.minimum(away, 2), 2 * p + s, HALF:],
                    ], axis=0))
                parts.append(jnp.concatenate(cols, axis=1))
                block = meta_s[0, 0, c, 96]
                owns.append(p_own[block])
                weights.append(block.astype(F32))
            rows = pl.ds(pl.multiple_of(q * CHUNK * BLOCK + p * TILE, TILE), TILE)
            remote_rows = jnp.concatenate(parts, axis=0)
            c_x[rows] = remote_rows
            z = mm(remote_rows, wci[L:]) + jnp.concatenate(owns, axis=0)
            a, h = silu_parts(z)
            u, r = norm(mm(a, wco[...]))
            c_a[rows] = a
            c_h[rows] = h
            message = u.astype(BF)
            c_u[rows] = message
            c_r[rows] = r
            message = message.astype(F32)
            for s in range(2):
                m = message[s * BLOCK:(s + 1) * BLOCK]
                csum[1] += m * weights[s]
                csum[0] += m * (1.0 - weights[s])

    loads[5].wait()
    loads[6].wait()
    nbuf[:, 0:L] = x
    nbuf[:, L:2 * L] = mesh_sum[...]
    nbuf[:, 2 * L:] = csum[...].reshape(NODES, L).astype(BF)
    a, h = silu_parts(mm(nbuf[...], wni[...]))
    u, r = norm(mm(a, wno[...]))
    node_out[...] = (x.astype(F32) + u).astype(BF)
    write(node_out, node_out_hbm, 13)
    write(edge_out, edge_out_hbm, 14)
    ncot = ncot_ref[...].astype(F32)
    n_dy = norm_back(u, r, ncot).astype(BF)
    n_dz = (mm_nt(n_dy, wno[...]) * h).astype(BF)
    dcon[...] = mm_nt(n_dz, wni[2 * L:]).astype(BF).reshape(2, BLOCK, L)

    @pl.loop(0, ROWS // 2)
    def _(t):
        rows = pl.ds(pl.multiple_of(t * TILE, TILE), TILE)
        blocks = [meta_s[0, 0, 2 * t + s, 96] for s in range(2)]
        g = jnp.concatenate([dcon[b] for b in blocks], axis=0).astype(F32)
        dy = norm_back(c_u[rows].astype(F32), c_r[rows], g).astype(BF)
        c_dy[rows] = dy
        dz = (mm_nt(dy, wco[...]) * c_h[rows]).astype(BF)
        for s in range(2):
            part = dz[s * BLOCK:(s + 1) * BLOCK]
            weight = blocks[s].astype(F32)
            dzown[1] += part.astype(F32) * weight
            dzown[0] += part.astype(F32) * (1.0 - weight)
            for k in range(COLORS):
                dz_all[k, 0, 2 * t + s] = part[:, k * COLS:(k + 1) * COLS]
        for k, (a1, a2, a3) in enumerate(ORDERS):
            pair = pl.ds(2 * t, 2)
            send(dz_all.at[k, 0, pair], dz_all.at[k, 3, pair], S_B1, R_B1 + t, peer(a3, 1))
            send(dz_all.at[k, 0, pair], dz_all.at[k, 1, pair], S_B1, R_B1 + t, peer(a3, 3))

    def put(group, row, value):
        value = value.astype(BF)
        for k in range(COLORS):
            gsend[group][k, row:row + L] = value[:, k * COLS:(k + 1) * COLS]

    def sums_1(n):
        size = GROUPS[n] // 4
        for k, (a1, a2, a3) in enumerate(ORDERS):
            for off in (2, 1, 3):
                send(
                    gsend[n].at[k, pl.ds(around(a3, off) * size, size)], g1[n].at[k, off - 1],
                    S_G + 6 * n + 0, R_G + 6 * n + 0, peer(a3, off),
                )

    def sums_2(n):
        size = GROUPS[n] // 4
        piece = size // 4
        arrived(g1[n], R_G + 6 * n)
        for k, (a1, a2, a3) in enumerate(ORDERS):
            @pl.loop(0, 4)
            def _(t):
                rows = pl.ds(pl.multiple_of(t * piece, 16), piece)
                total = gsend[n][k, pl.ds(pl.multiple_of(coord[a3] * size + t * piece, 16), piece)].astype(F32)
                for o in range(3):
                    total += g1[n][k, o, rows].astype(F32)
                g2src[n][k, t] = total.astype(BF)

            for off in (2, 1, 3):
                send(
                    g2src[n].at[k, around(a2, off)], g2[n].at[k, off - 1],
                    S_G + 6 * n + 1, R_G + 6 * n + 1, peer(a2, off),
                )

    def sums_3(n):
        arrived(g2[n], R_G + 6 * n + 1)
        for k, (a1, a2, a3) in enumerate(ORDERS):
            total = g2src[n][k, coord[a2]].astype(F32)
            for o in range(3):
                total += g2[n][k, o].astype(F32)
            g3[n][k, coord[a1]] = total.astype(BF)
            part = g3[n].at[k, coord[a1]]
            for off in (2, 1, 3):
                send(part, part, S_G + 6 * n + 2, R_G + 6 * n + 2, peer(a1, off))

    def sums_4(n):
        arrived(g2[n], R_G + 6 * n + 2)
        for k, (a1, a2, a3) in enumerate(ORDERS):
            total = g3[n][k, 0].astype(F32)
            for o in range(1, SIDE):
                total += g3[n][k, o].astype(F32)
            gout[n][k, coord[a3], coord[a2]] = total.astype(BF)
            part = gout[n].at[k, coord[a3], coord[a2]]
            for off in (2, 1, 3):
                send(part, part, S_G + 6 * n + 3, R_G + 6 * n + 3, peer(a2, off))

    def sums_5(n):
        arrived(g2[n], R_G + 6 * n + 3)
        for k, (a1, a2, a3) in enumerate(ORDERS):
            part = gout[n].at[k, coord[a3]]
            send(part, part, S_G + 6 * n + 4, R_G + 6 * n + 4, peer(a3, 1))
            send(part, part, S_G + 6 * n + 4, R_G + 6 * n + 4, peer(a3, 3))

    def sums_6(n):
        arrived(gout[n].at[:, pl.ds(0, 2)], R_G + 6 * n + 4)
        for k, (a1, a2, a3) in enumerate(ORDERS):
            part = gout[n].at[k, around(a3, 3), pl.ds(0, 2)]
            send(part, part, S_G + 6 * n + 5, R_G + 6 * n + 5, peer(a3, 1))
            part = gout[n].at[k, around(a3, 1), pl.ds(2, 2)]
            send(part, part, S_G + 6 * n + 5, R_G + 6 * n + 5, peer(a3, 3))

    def sums_7(n):
        arrived(gout[n].at[:, 0], R_G + 6 * n + 5)
        write(gout[n], (node_hbm, contact_hbm, edge_hbm)[n], 10 + n)

    for k in range(COLORS):
        gsend[CONTACT_G][k, 3 * L:] = jnp.zeros((GROUPS[CONTACT_G] - 3 * L, COLS), BF)
    put(NODE_G, 3 * L, mm_tn(a, n_dy))
    for i in range(3):
        put(NODE_G, i * L, mm_tn(nbuf[:, i * L:(i + 1) * L], n_dz))
    sums_1(NODE_G)
    own_low = dzown[...].reshape(NODES, L).astype(BF)
    put(CONTACT_G, 0, mm_tn(x, own_low))
    hidden = jnp.concatenate(
        [dz_all[k, 0, 0:ROWS].reshape(ROWS * BLOCK, COLS) for k in range(COLORS)], axis=1
    )
    put(CONTACT_G, L, mm_tn(c_x[...], hidden))
    put(CONTACT_G, 2 * L, mm_tn(c_a[...], c_dy[...]))
    sums_1(CONTACT_G)

    dmesh[...] = mm_nt(n_dz, wni[L:2 * L]).astype(BF)
    loads[7].wait()

    def edge_backward(t):
        rows = pl.ds(pl.multiple_of(t * TILE, TILE), TILE)
        nodes = pl.ds(pl.multiple_of(t * quarter, quarter), quarter)
        g = ecot[rows].astype(F32) + mm(fan, dmesh[nodes])
        dy = norm_back(e_u[rows].astype(F32), e_r[rows], g).astype(BF)
        dz = (mm_nt(dy, weo[...]) * e_h[rows]).astype(BF)
        edge_grad[rows] = (g + mm_nt(dz, wei[0:L])).astype(BF)
        tsum[nodes] = mm_tn(fan, dz).astype(BF)
        e_dy[rows] = dy
        e_dz[rows] = dz

    @pl.loop(0, 4)
    def _(t):
        edge_backward(t)
        for tile in (2 * t, 2 * t + 1):
            arrived(dz_all.at[:, pl.ds(0, 2), pl.ds(0, 2)], R_B1 + tile)
            for k, (a1, a2, a3) in enumerate(ORDERS):
                even, odd = pl.ds(2 * tile, 1), pl.ds(2 * tile + 1, 1)
                send(dz_all.at[k, 3, even], dz_all.at[k, 2, even], S_B1B, R_B1B, peer(a3, 1))
                send(dz_all.at[k, 1, odd], dz_all.at[k, 2, odd], S_B1B, R_B1B, peer(a3, 3))

    write(edge_grad, edge_grad_hbm, 15)
    spread = mm_tn(onehot[...], e_dz[...])
    spread_low = spread.astype(BF)
    rim_out[0] = spread_low[0:RIM]
    rim_out[1] = spread_low[RIM + NODES:]
    send(rim_out.at[0], rim_in.at[0], S_RIM, R_RIM, down)
    send(rim_out.at[1], rim_in.at[1], S_RIM, R_RIM, up)
    put(EDGE_G, L, mm_tn(xext[...], spread_low))
    put(EDGE_G, 0, mm_tn(es[...], e_dz[...]))
    put(EDGE_G, 2 * L, mm_tn(x, tsum[...]))
    put(EDGE_G, 3 * L, mm_tn(e_a[...], e_dy[...]))
    sums_1(EDGE_G)

    arrived(dz_all.at[:, 2, pl.ds(0, ROWS)], R_B1B)
    sent(plane.at[:, pl.ds(0, 16)], S_F2)
    sent(plane.at[:, pl.ds(0, 8)], S_F2B)
    sent(r3, S_F1)

    for off in (2, 1, 3, 0):
        group = [around(a2, off) * 8 for a1, a2, a3 in ORDERS]

        @pl.loop(0, 8)
        def _(s):
            for k in range(COLORS):
                total = jnp.zeros((BLOCK, COLS), F32)
                for j in range(SIDE):
                    for i in range(2):
                        total += dz_all[k, j, table_s[2 * j + i, k * 32 + group[k] + s]].astype(F32)
                plane[k, group[k] + s] = total.astype(BF)

        if off:
            for k, (a1, a2, a3) in enumerate(ORDERS):
                send(
                    plane.at[k, pl.ds(group[k], 8)], r2.at[k, off - 1],
                    S_B2, R_B2, peer(a2, off),
                )
    sums_2(NODE_G)
    sums_2(CONTACT_G)
    grad = ncot + mm_nt(n_dz, wni[0:L]) + mm_nt(tsum[...], wei[2 * L:]) + mm_nt(own_low, wci[0:L])

    arrived(r2, R_B2)
    for k, (a1, a2, a3) in enumerate(ORDERS):
        @pl.loop(0, 8)
        def _(s):
            total = plane[k, coord[a2] * 8 + s].astype(F32)
            for o in range(3):
                total += r2[k, o, s].astype(F32)
            r3src[k, s] = total.astype(BF)

        for off in (1, 2, 3):
            send(
                r3src.at[k, pl.ds(around(a1, off) * 2, 2)], r3.at[k, off - 1],
                S_B3, R_B3, peer(a1, off),
            )
    sums_3(NODE_G)
    sums_3(CONTACT_G)
    sums_2(EDGE_G)
    sums_4(NODE_G)
    sums_4(CONTACT_G)
    sums_3(EDGE_G)
    arrived(rim_in, R_RIM)
    first = spread[RIM:2 * RIM] + rim_in[1].astype(F32) * has_low
    last = spread[NODES:NODES + RIM] + rim_in[0].astype(F32) * has_high
    own_spread = jnp.concatenate([first, spread[2 * RIM:NODES], last], axis=0).astype(BF)
    grad += mm_nt(own_spread, wei[L:2 * L])
    arrived(r3, R_B3)
    cols = []
    for k, (a1, a2, a3) in enumerate(ORDERS):
        halves = [r3src[k, coord[a1] * 2 + b].astype(F32) for b in range(2)]
        for off in (1, 2, 3):
            halves = [halves[b] + r3[k, off - 1, b].astype(F32) for b in range(2)]
        cols.append(jnp.concatenate(halves, axis=0).astype(BF))
    s_rem = jnp.concatenate(cols, axis=1)
    node_grad[...] = (grad + mm_nt(s_rem, wci[L:])).astype(BF)
    write(node_grad, node_grad_hbm, 16)

    sums_5(NODE_G)
    sums_4(EDGE_G)
    sums_5(CONTACT_G)
    sums_6(NODE_G)
    sums_5(EDGE_G)
    sums_6(CONTACT_G)
    sums_7(NODE_G)
    sums_6(EDGE_G)
    sums_7(CONTACT_G)
    sums_7(EDGE_G)

    for ref, sem in (
        (meta_v.at[:, pl.ds(1, 3)], S_META), (halo, S_HALO), (rim_in, S_RIM), (hs, S_H), (sbuf, S_F3), (sbuf, S_B1),
        (dz_all.at[:, 2, pl.ds(0, ROWS)], S_B1B), (r2, S_B2), (r3, S_B3),
    ):
        sent(ref, sem)
    for n in range(3):
        refs = (g1[n], g2[n], g2[n], g2[n], gout[n].at[:, pl.ds(0, 2)], gout[n].at[:, 0])
        for i, ref in enumerate(refs):
            sent(ref, S_G + 6 * n + i)
    for out in outs:
        out.wait()


def dma(*shape):
    return pltpu.SemaphoreType.DMA(shape)


def vm(shape, dtype):
    return pltpu.VMEM(shape, dtype)


def fused(x, src, ncot, block, host, remote, es, ecot, wei, weo, wni, wno, wci, wco):
    tile = (BLOCK, COLS)
    pieces = [rows // 16 for rows in GROUPS]
    scratch = [
        vm((EDGES, L), BF), vm((EDGES, L), BF), vm((3 * L, L), BF), vm((L, L), BF), vm((3 * L, L), BF),
        vm((L, L), BF), vm((2 * L, L), BF), vm((L, L), BF),
        vm((COLORS, 32) + tile, BF),
        vm((COLORS, 2, ROWS, HALF, COLS), BF),
        [vm((COLORS, 2, CHUNK, HALF, COLS), BF) for _ in range(N_CHUNK)],
        vm((COLORS, 2, ROWS) + tile, BF),
        [vm((COLORS, 3, CHUNK) + tile, BF) for _ in range(N_CHUNK)],
        vm((COLORS, SIDE, ROWS + 1) + tile, BF),
        vm((COLORS, 3, 8) + tile, BF), vm((COLORS, 3, 2) + tile, BF), vm((COLORS, 8) + tile, BF),
        [vm((COLORS, rows, COLS), BF) for rows in GROUPS],
        [vm((COLORS, 3, rows // 4, COLS), BF) for rows in GROUPS],
        [vm((COLORS, SIDE, piece, COLS), BF) for piece in pieces],
        [vm((COLORS, 3, piece, COLS), BF) for piece in pieces],
        [vm((COLORS, SIDE, piece, COLS), BF) for piece in pieces],
        [vm((COLORS, SIDE, SIDE, piece, COLS), BF) for piece in pieces],
        vm((NODES, L), BF), vm((EDGES, L), BF), vm((NODES, L), BF), vm((EDGES, L), BF),
        vm((2, RIM, L), BF), vm((2, RIM, L), BF), vm((2, RIM, L), BF), vm((NODES + 2 * RIM, L), BF), vm((EDGES, L), BF),
        vm((3, SIDE, ROWS, 128), jnp.int32), pltpu.SMEM((3, SIDE, ROWS, 128), jnp.int32),
        vm((8, 128), jnp.int32), pltpu.SMEM((8, 128), jnp.int32),
        vm((EDGES, L), BF), vm((EDGES, 1), F32), vm((EDGES, L), F32), vm((EDGES, L), BF),
        vm((EDGES, L), BF), vm((EDGES, L), BF), vm((NODES, L), BF),
        vm((ROWS * BLOCK, L), BF), vm((ROWS * BLOCK, L), BF), vm((ROWS * BLOCK, 1), F32), vm((ROWS * BLOCK, L), F32),
        vm((ROWS * BLOCK, L), BF),
        vm((ROWS * BLOCK, L), BF), vm((2, BLOCK, L), F32), vm((2, BLOCK, L), F32), vm((2, BLOCK, L), F32),
        vm((NODES, L), BF), vm((NODES, 3 * L), BF), vm((2, BLOCK, L), BF), vm((NODES, L), BF),
        dma(17), dma(S_G + 18), dma(R_G + 18),
    ]
    here = pl.BlockSpec(memory_space=pltpu.VMEM)
    there = pl.BlockSpec(memory_space=pl.ANY)
    scalars = pl.BlockSpec(memory_space=pltpu.SMEM)
    return pl.pallas_call(
        body,
        out_shape=(
            jax.ShapeDtypeStruct((NODES, L), BF), jax.ShapeDtypeStruct((EDGES, L), BF),
            jax.ShapeDtypeStruct((NODES, L), BF), jax.ShapeDtypeStruct((EDGES, L), BF),
        ) + tuple(jax.ShapeDtypeStruct((COLORS, SIDE, SIDE, piece, COLS), BF) for piece in pieces),
        in_specs=[here] * 3 + [scalars] * 3 + [there] * 8,
        out_specs=[there] * 7,
        scratch_shapes=scratch,
        compiler_params=pltpu.CompilerParams(
            collective_id=0, has_side_effects=True, vmem_limit_bytes=63 * 1024 * 1024
        ),
        name="layer",
    )(x, src, ncot, block, host, remote, es, ecot, wei, weo, wni, wno, wci, wco)


def finish_body(*refs):
    plain_in, packed_in = refs[0:4], refs[4:7]
    plain_out, wide_out = refs[7:11], refs[11:17]
    plain, packed, wide, in_sem, out_sem = refs[17:21], refs[21:24], refs[24:27], refs[27], refs[28]
    loads = [pltpu.make_async_copy(packed_in[n], packed[n], in_sem.at[n]) for n in range(3)]
    loads += [pltpu.make_async_copy(plain_in[i], plain[i], in_sem.at[3 + i]) for i in range(4)]
    for load in loads:
        load.start()
    stores = []

    def store(src, dst):
        copy = pltpu.make_async_copy(src, dst, out_sem.at[len(stores)])
        copy.start()
        stores.append(copy)

    for n, first in enumerate((3 * L, 2 * L, 3 * L)):
        loads[n].wait()
        for k in range(COLORS):
            wide[n][:, k * COLS:(k + 1) * COLS] = packed[n][k].astype(F32)
        store(wide[n].at[pl.ds(0, first)], wide_out[2 * n])
        store(wide[n].at[pl.ds(first, L)], wide_out[2 * n + 1])
    for i in range(4):
        loads[3 + i].wait()
        store(plain[i], plain_out[i])
    for copy in stores:
        copy.wait()


def finish(plain, packed):
    packed = [p.reshape(COLORS, rows, COLS) for p, rows in zip(packed, GROUPS)]
    there = pl.BlockSpec(memory_space=pl.ANY)
    shapes = [jax.ShapeDtypeStruct(p.shape, p.dtype) for p in plain]
    shapes += [jax.ShapeDtypeStruct((n * L, L), F32) for n in (3, 1, 2, 1, 3, 1)]
    return pl.pallas_call(
        finish_body,
        out_shape=shapes,
        in_specs=[there] * 7,
        out_specs=[there] * 10,
        scratch_shapes=[
            *[vm(p.shape, p.dtype) for p in plain],
            *[vm((COLORS, rows, COLS), BF) for rows in GROUPS],
            *[vm((rows, L), F32) for rows in GROUPS],
            dma(7), dma(10),
        ],
        compiler_params=pltpu.CompilerParams(vmem_limit_bytes=63 * 1024 * 1024),
        name="finish",
    )(*plain, *packed)


def on_device(
    node_state, edge_state, edge_source, contact_block, contact_host, contact_remote,
    w_edge_in, w_edge_out, w_node_in, w_node_out, w_contact_in, w_contact_out, node_cot, edge_cot,
):
    results = fused(
        node_state, edge_source.reshape(8, 128), node_cot, contact_block, contact_host.reshape(ROWS), contact_remote,
        edge_state, edge_cot, w_edge_in, w_edge_out, w_node_in, w_node_out, w_contact_in, w_contact_out,
    )
    out = finish(results[:4], results[4:])
    node_in, node_last, contact_in, contact_last, edge_in, edge_last = out[4:]
    return tuple(out[:4]) + (edge_in, edge_last, node_in, node_last, contact_in, contact_last)


def solution(mesh):
    rows = P(("rep", "dom"), None)
    flat = P(("rep", "dom"))
    weight = P("rep", None)
    return jax.shard_map(
        on_device,
        mesh=mesh,
        in_specs=(rows, rows, flat, flat, rows, flat) + (weight,) * 6 + (rows, rows),
        out_specs=(rows,) * 4 + (weight,) * 6,
        check_vma=False,
    )
```

```python
import functools

import jax
import jax.numpy as jnp
from jax import lax
from jax.experimental import pallas as pl
from jax.experimental.pallas import tpu as pltpu
from jax.sharding import PartitionSpec as P

L = 384
BLOCK = 128
EPN = 4
RIM = 64
NODES = 256
EDGES = 1024
ROWS = 16
TILE = 256
COLORS = 3
COLS = 128
SIDE = 4
DOM = 64
EPS = 1e-05
BF = jnp.bfloat16
F32 = jnp.float32
MESH = pl.DeviceIdType.MESH

GROUPS = (1536, 1280, 1536)
NODE_G, CONTACT_G, EDGE_G = 0, 1, 2

ORDERS = (("z", "x", "y"), ("x", "y", "z"), ("y", "z", "x"))
STRIDE = {"y": 16, "x": 4, "z": 1}
AXES = ("y", "x", "z")
N_CHUNK = 4
S_META, S_HALO, S_RIM, S_F1, S_F2, S_F2B, S_H, S_F3, S_B1, S_B1B, S_B2H, S_B2, S_B3, S_G = range(14)
R_META, R_HALO, R_RIM, R_F1, R_F2, R_F2B, R_H, R_F3, R_B1, R_B1B, R_B2H, R_B2, R_B3, R_G = (
    0, 1, 2, 3, 6, 9, 10, 14, 18, 26, 27, 28, 29, 30
)
CHUNK = ROWS // N_CHUNK
HALF = BLOCK // 2


def mm(a, b):
    return lax.dot_general(a, b, (((1,), (0,)), ((), ())), preferred_element_type=F32)


def mm_nt(a, b):
    return lax.dot_general(a, b, (((1,), (1,)), ((), ())), preferred_element_type=F32)


def mm_tn(a, b):
    return lax.dot_general(a, b, (((0,), (0,)), ((), ())), preferred_element_type=F32)


def row_mean(v):
    return jnp.sum(v, axis=-1, keepdims=True) * (1.0 / L)


def norm(y):
    center = y - row_mean(y)
    scale = lax.rsqrt(row_mean(center * center) + EPS)
    return center * scale, scale


def norm_back(u, scale, g):
    return scale * (g - row_mean(g) - u * row_mean(g * u))


def silu_parts(z):
    s = jax.nn.sigmoid(z)
    return (z * s).astype(BF), s * (1.0 + z * (1.0 - s))


def body(
    x_ref, src_ref, ncot_ref, block_ref, host_ref, remote_ref,
    es_hbm, ecot_hbm, wei_hbm, weo_hbm, wni_hbm, wno_hbm, wci_hbm, wco_hbm,
    node_out_hbm, edge_out_hbm, node_grad_hbm, edge_grad_hbm, node_hbm, contact_hbm, edge_hbm,
    es, ecot, wei, weo, wni, wno, wci, wco,
    plane, hs, hr, sbuf, rbuf, dz_all, r2h, r2, r3, r3src,
    gsend, g1h, g1, g2src, g2, g3, gout, node_out, edge_out, node_grad, edge_grad,
    halo, rim_out, rim_in, xext, onehot,
    meta_v, meta_s, table_v, table_s,
    e_u, e_r, e_h, e_a, e_dy, e_dz, mesh_sum,
    c_x, c_u, c_r, c_h, c_a, c_dy, p_own, csum, dzown, tsum, nbuf, dcon, dmesh,
    local_sem, ss, rs,
):
    me = lax.axis_index("dom")
    coord = {"y": lax.div(me, 16), "x": lax.rem(lax.div(me, 4), 4), "z": lax.rem(me, 4)}

    def around(axis, off):
        return lax.rem(coord[axis] + off, SIDE)

    def peer(axis, off):
        return me + (around(axis, off) - coord[axis]) * STRIDE[axis]

    up, down = lax.rem(me + 1, DOM), lax.rem(me + DOM - 1, DOM)

    def remote(src, dst, to, at, dev):
        return pltpu.make_async_remote_copy(
            src_ref=src, dst_ref=dst, send_sem=ss.at[to], recv_sem=rs.at[at],
            device_id={"dom": dev}, device_id_type=MESH,
        )

    def arrived(ref, sem):
        remote(ref, ref, 0, sem, up).wait_recv()

    def sent(ref, sem):
        remote(ref, ref, sem, 0, up).wait_send()

    def send(*args):
        remote(*args).start()

    loads = [
        pltpu.make_async_copy(src, dst, local_sem.at[i])
        for i, (src, dst) in enumerate(
            [(wci_hbm, wci), (es_hbm, es), (wei_hbm, wei), (weo_hbm, weo), (wco_hbm, wco),
             (wni_hbm, wni), (wno_hbm, wno), (ecot_hbm, ecot)]
        )
    ]
    for load in loads:
        load.start()

    outs = []

    def write(src, dst, i):
        out = pltpu.make_async_copy(src, dst, local_sem.at[i])
        out.start()
        outs.append(out)

    barrier = pltpu.get_barrier_semaphore()
    for axis in AXES:
        for off in (1, 2, 3):
            pl.semaphore_signal(barrier, inc=1, device_id={"dom": peer(axis, off)}, device_id_type=MESH)
    pl.semaphore_signal(barrier, inc=1, device_id={"dom": up}, device_id_type=MESH)
    pl.semaphore_signal(barrier, inc=1, device_id={"dom": down}, device_id_type=MESH)

    x = x_ref[...]
    place = lax.broadcasted_iota(jnp.int32, (1, 128), 1)
    for c in range(ROWS):
        host = host_ref[c]
        at = {"y": lax.div(host, 16), "x": lax.rem(lax.div(host, 4), 4), "z": lax.rem(host, 4)}
        code = [((at[a3] * SIDE + at[a2]) * SIDE + at[a1]) * 2 + remote_ref[c] for a1, a2, a3 in ORDERS]
        line = jnp.where(place < 32, code[0], jnp.where(place < 64, code[1], code[2]))
        line = jnp.where(place < 96, line, block_ref[c])
        for i in range(3):
            meta_v[i, 0, c:c + 1] = line
    for k, (a1, a2, a3) in enumerate(ORDERS):
        own = (coord[a2] * SIDE + coord[a1]) * 2
        for b in range(2):
            plane[k, own + b] = x_ref[b * BLOCK:(b + 1) * BLOCK, k * COLS:(k + 1) * COLS]
    pl.semaphore_wait(barrier, 11)

    for k, (a1, a2, a3) in enumerate(ORDERS):
        own = (coord[a2] * SIDE + coord[a1]) * 2
        for off in (1, 2, 3):
            part = plane.at[k, pl.ds(own, 2)]
            send(part, part, S_F1, R_F1 + k, peer(a1, off))
    send(x_ref.at[pl.ds(NODES - RIM, RIM)], halo.at[0], S_HALO, R_HALO, up)
    send(x_ref.at[pl.ds(0, RIM)], halo.at[1], S_HALO, R_HALO, down)
    for i, axis in enumerate(AXES):
        for off in (1, 2, 3):
            send(meta_v.at[i, 0], meta_v.at[i, SIDE - off], S_META, R_META, peer(axis, off))

    lanes = lax.broadcasted_iota(jnp.int32, (BLOCK, L), 1)
    idx = jnp.concatenate([src_ref[...].astype(F32)] * 16, axis=0).T
    for j in range(EDGES // BLOCK):
        col = idx[:, j:j + 1].astype(jnp.int32)
        onehot[j * BLOCK:(j + 1) * BLOCK, :] = jnp.where(col == lanes, 1.0, 0.0).astype(BF)
    for k in range(COLORS):
        for j in range(SIDE):
            dz_all[k, j, ROWS] = jnp.zeros((BLOCK, COLS), BF)
    csum[...] = jnp.zeros_like(csum)
    dzown[...] = jnp.zeros_like(dzown)
    loads[0].wait()
    p_own[...] = mm(x, wci[0:L]).reshape(2, BLOCK, L)

    for k, (a1, a2, a3) in enumerate(ORDERS):
        arrived(plane.at[k, pl.ds(0, 6)], R_F1 + k)
        part = plane.at[k, pl.ds(coord[a2] * 8, 8)]
        send(part, part, S_F2, R_F2 + k, peer(a2, 1))
        send(part, part, S_F2, R_F2 + k, peer(a2, 3))

    arrived(halo, R_HALO)
    has_low = (me > 0).astype(F32)
    has_high = (me < DOM - 1).astype(F32)
    xext[0:RIM] = (halo[0].astype(F32) * has_low).astype(BF)
    xext[RIM:RIM + NODES] = x
    xext[RIM + NODES:] = (halo[1].astype(F32) * has_high).astype(BF)

    arrived(meta_v.at[:, pl.ds(1, 3)], R_META)
    mine = [coord[a3] * 32 for a1, a2, a3 in ORDERS]
    sought = lax.rem(place, 32) + jnp.where(place < 32, mine[0], jnp.where(place < 64, mine[1], mine[2]))
    wide = lax.broadcasted_iota(jnp.int32, (ROWS, 128), 1)
    for j in range(SIDE):
        asked = [meta_v[AXES.index(a3), j] for a1, a2, a3 in ORDERS]
        asked = jnp.where(wide < 32, asked[0], jnp.where(wide < 64, asked[1], asked[2]))
        first = second = jnp.full((1, 128), ROWS, jnp.int32)
        for c in reversed(range(ROWS)):
            hit = asked[c:c + 1] == sought
            second = jnp.where(hit, first, second)
            first = jnp.where(hit, c, first)
        table_v[2 * j:2 * j + 1] = first
        table_v[2 * j + 1:2 * j + 2] = second
    to_smem = [
        pltpu.make_async_copy(meta_v, meta_s, local_sem.at[8]),
        pltpu.make_async_copy(table_v, table_s, local_sem.at[9]),
    ]
    for copy in to_smem:
        copy.start()

    for load in loads[1:4]:
        load.wait()

    quarter = TILE // EPN
    fan = jnp.where(
        lax.div(lax.broadcasted_iota(jnp.int32, (TILE, quarter), 0), EPN)
        == lax.broadcasted_iota(jnp.int32, (TILE, quarter), 1), 1.0, 0.0,
    ).astype(BF)

    def edge_forward(t):
        rows = pl.ds(pl.multiple_of(t * TILE, TILE), TILE)
        nodes = pl.ds(pl.multiple_of(t * quarter, quarter), quarter)
        state = es[rows]
        src = mm(onehot[rows], xext[...]).astype(BF)
        tgt = mm(fan, x_ref[nodes]).astype(BF)
        z = mm(state, wei[0:L]) + mm(src, wei[L:2 * L]) + mm(tgt, wei[2 * L:])
        a, h = silu_parts(z)
        u, r = norm(mm(a, weo[...]))
        out = (state.astype(F32) + u).astype(BF)
        edge_out[rows] = out
        mesh_sum[nodes] = mm_tn(fan, out).astype(BF)
        e_a[rows] = a
        e_h[rows] = h
        e_u[rows] = u.astype(BF)
        e_r[rows] = r

    for k, (a1, a2, a3) in enumerate(ORDERS):
        arrived(plane.at[k, pl.ds(0, 16)], R_F2 + k)
        part = plane.at[k, pl.ds(around(a2, 3) * 8, 4)]
        send(part, part, S_F2B, R_F2B, peer(a2, 1))
        part = plane.at[k, pl.ds(around(a2, 1) * 8 + 4, 4)]
        send(part, part, S_F2B, R_F2B, peer(a2, 3))

    edge_forward(0)

    for copy in to_smem:
        copy.wait()
    arrived(plane.at[:, pl.ds(0, 8)], R_F2B)

    def request(k, j, c):
        code = meta_s[AXES.index(ORDERS[k][2]), j, c, k * 32]
        return lax.rem(code, 32), lax.div(code, 32)

    for q in range(N_CHUNK):
        for k, (a1, a2, a3) in enumerate(ORDERS):
            for c in range(CHUNK):
                slot, _ = request(k, 2, q * CHUNK + c)
                hs[k, 0, q * CHUNK + c] = plane[k, slot, 0:HALF]
                hs[k, 1, q * CHUNK + c] = plane[k, slot, HALF:]
            part = pl.ds(q * CHUNK, CHUNK)
            send(hs.at[k, 0, part], hr[q].at[k, 0], S_H, R_H + q, peer(a3, 3))
            send(hs.at[k, 1, part], hr[q].at[k, 1], S_H, R_H + q, peer(a3, 1))
    for q in range(N_CHUNK):
        arrived(hr[q], R_H + q)
        for k, (a1, a2, a3) in enumerate(ORDERS):
            for c in range(CHUNK):
                row = q * CHUNK + c
                slot, where = request(k, 3, row)
                own = where == coord[a3]
                sbuf[k, 0, row, 0:HALF] = jnp.where(own, plane[k, slot, 0:HALF], hr[q][k, 0, c])
                sbuf[k, 0, row, HALF:] = plane[k, slot, HALF:]
                slot, where = request(k, 1, row)
                own = where == coord[a3]
                sbuf[k, 1, row, 0:HALF] = plane[k, slot, 0:HALF]
                sbuf[k, 1, row, HALF:] = jnp.where(own, plane[k, slot, HALF:], hr[q][k, 1, c])
            part = pl.ds(q * CHUNK, CHUNK)
            send(sbuf.at[k, 0, part], rbuf[q].at[k, 1], S_F3, R_F3 + q, peer(a3, 3))
            send(sbuf.at[k, 1, part], rbuf[q].at[k, 2], S_F3, R_F3 + q, peer(a3, 1))
        for k in range(COLORS):
            for c in range(CHUNK):
                rbuf[q][k, 0, c] = plane[k, request(k, 0, q * CHUNK + c)[0]]
        if q < 3:
            edge_forward(q + 1)

    loads[4].wait()
    for q in range(N_CHUNK):
        arrived(rbuf[q].at[:, pl.ds(1, 2)], R_F3 + q)

        @pl.loop(0, CHUNK // 2)
        def _(p):
            parts, owns, weights = [], [], []
            for s in range(2):
                c = q * CHUNK + 2 * p + s
                cols = []
                for k, (a1, a2, a3) in enumerate(ORDERS):
                    away = lax.rem(request(k, 0, c)[1] - coord[a3] + SIDE, SIDE)
                    cols.append(jnp.concatenate([
                        rbuf[q][k, lax.div(away + 1, 2), 2 * p + s, 0:HALF],
                        rbuf[q][k, jnp.minimum(away, 2), 2 * p + s, HALF:],
                    ], axis=0))
                parts.append(jnp.concatenate(cols, axis=1))
                block = meta_s[0, 0, c, 96]
                owns.append(p_own[block])
                weights.append(block.astype(F32))
            rows = pl.ds(pl.multiple_of(q * CHUNK * BLOCK + p * TILE, TILE), TILE)
            remote_rows = jnp.concatenate(parts, axis=0)
            c_x[rows] = remote_rows
            z = mm(remote_rows, wci[L:]) + jnp.concatenate(owns, axis=0)
            a, h = silu_parts(z)
            u, r = norm(mm(a, wco[...]))
            c_a[rows] = a
            c_h[rows] = h
            message = u.astype(BF)
            c_u[rows] = message
            c_r[rows] = r
            message = message.astype(F32)
            for s in range(2):
                m = message[s * BLOCK:(s + 1) * BLOCK]
                csum[1] += m * weights[s]
                csum[0] += m * (1.0 - weights[s])

    loads[5].wait()
    loads[6].wait()
    nbuf[:, 0:L] = x
    nbuf[:, L:2 * L] = mesh_sum[...]
    nbuf[:, 2 * L:] = csum[...].reshape(NODES, L).astype(BF)
    a, h = silu_parts(mm(nbuf[...], wni[...]))
    u, r = norm(mm(a, wno[...]))
    node_out[...] = (x.astype(F32) + u).astype(BF)
    write(node_out, node_out_hbm, 10)
    write(edge_out, edge_out_hbm, 11)
    ncot = ncot_ref[...].astype(F32)
    n_dy = norm_back(u, r, ncot).astype(BF)
    n_dz = (mm_nt(n_dy, wno[...]) * h).astype(BF)
    dcon[...] = mm_nt(n_dz, wni[2 * L:]).astype(BF).reshape(2, BLOCK, L)

    @pl.loop(0, ROWS // 2)
    def _(t):
        rows = pl.ds(pl.multiple_of(t * TILE, TILE), TILE)
        blocks = [meta_s[0, 0, 2 * t + s, 96] for s in range(2)]
        g = jnp.concatenate([dcon[b] for b in blocks], axis=0).astype(F32)
        dy = norm_back(c_u[rows].astype(F32), c_r[rows], g).astype(BF)
        c_dy[rows] = dy
        dz = (mm_nt(dy, wco[...]) * c_h[rows]).astype(BF)
        for s in range(2):
            part = dz[s * BLOCK:(s + 1) * BLOCK]
            weight = blocks[s].astype(F32)
            dzown[1] += part.astype(F32) * weight
            dzown[0] += part.astype(F32) * (1.0 - weight)
            for k in range(COLORS):
                dz_all[k, 0, 2 * t + s] = part[:, k * COLS:(k + 1) * COLS]
        for k, (a1, a2, a3) in enumerate(ORDERS):
            pair = pl.ds(2 * t, 2)
            send(dz_all.at[k, 0, pair], dz_all.at[k, 3, pair], S_B1, R_B1 + t, peer(a3, 1))
            send(dz_all.at[k, 0, pair], dz_all.at[k, 1, pair], S_B1, R_B1 + t, peer(a3, 3))

    def put(group, row, value):
        value = value.astype(BF)
        for k in range(COLORS):
            gsend[group][k, row:row + L] = value[:, k * COLS:(k + 1) * COLS]

    def sums_1(n):
        size = GROUPS[n] // 4
        half = size // 2
        for k, (a1, a2, a3) in enumerate(ORDERS):
            far = around(a3, 2) * size
            send(gsend[n].at[k, pl.ds(far, half)], g1h[n].at[k, 0], S_G + 7 * n, R_G + 7 * n, peer(a3, 1))
            send(gsend[n].at[k, pl.ds(far + half, half)], g1h[n].at[k, 1], S_G + 7 * n, R_G + 7 * n, peer(a3, 3))

    def sums_1b(n):
        size = GROUPS[n] // 4
        half = size // 2
        arrived(g1h[n], R_G + 7 * n)
        for k, (a1, a2, a3) in enumerate(ORDERS):
            for i, off in enumerate((1, 3)):
                start = around(a3, off) * size
                rows = pl.ds(pl.multiple_of(start + i * half, 16), half)
                total = gsend[n][k, rows].astype(F32) + g1h[n][k, i].astype(F32)
                gsend[n][k, rows] = total.astype(BF)
                send(
                    gsend[n].at[k, pl.ds(start, size)], g1[n].at[k, i],
                    S_G + 7 * n + 1, R_G + 7 * n + 1, peer(a3, off),
                )

    def sums_2(n):
        size = GROUPS[n] // 4
        piece = size // 4
        arrived(g1[n], R_G + 7 * n + 1)
        for k, (a1, a2, a3) in enumerate(ORDERS):
            @pl.loop(0, 4)
            def _(t):
                rows = pl.ds(pl.multiple_of(t * piece, 16), piece)
                total = gsend[n][k, pl.ds(pl.multiple_of(coord[a3] * size + t * piece, 16), piece)].astype(F32)
                for o in range(2):
                    total += g1[n][k, o, rows].astype(F32)
                g2src[n][k, t] = total.astype(BF)

            for off in (2, 1, 3):
                send(
                    g2src[n].at[k, around(a2, off)], g2[n].at[k, off - 1],
                    S_G + 7 * n + 2, R_G + 7 * n + 2, peer(a2, off),
                )

    def sums_3(n):
        arrived(g2[n], R_G + 7 * n + 2)
        for k, (a1, a2, a3) in enumerate(ORDERS):
            total = g2src[n][k, coord[a2]].astype(F32)
            for o in range(3):
                total += g2[n][k, o].astype(F32)
            g3[n][k, coord[a1]] = total.astype(BF)
            part = g3[n].at[k, coord[a1]]
            for off in (2, 1, 3):
                send(part, part, S_G + 7 * n + 3, R_G + 7 * n + 3, peer(a1, off))

    def sums_4(n):
        arrived(g2[n], R_G + 7 * n + 3)
        for k, (a1, a2, a3) in enumerate(ORDERS):
            total = g3[n][k, 0].astype(F32)
            for o in range(1, SIDE):
                total += g3[n][k, o].astype(F32)
            gout[n][k, coord[a3], coord[a2]] = total.astype(BF)
            part = gout[n].at[k, coord[a3], coord[a2]]
            for off in (2, 1, 3):
                send(part, part, S_G + 7 * n + 4, R_G + 7 * n + 4, peer(a2, off))

    def sums_5(n):
        arrived(g2[n], R_G + 7 * n + 4)
        for k, (a1, a2, a3) in enumerate(ORDERS):
            part = gout[n].at[k, coord[a3]]
            send(part, part, S_G + 7 * n + 5, R_G + 7 * n + 5, peer(a3, 1))
            send(part, part, S_G + 7 * n + 5, R_G + 7 * n + 5, peer(a3, 3))

    def keep(n, off):
        for k, (a1, a2, a3) in enumerate(ORDERS):
            at = around(a3, off)
            write(gout[n].at[k, at], (node_hbm, contact_hbm, edge_hbm)[n].at[k, at], 14 + (n * 3 + k) * 4 + off)

    def sums_6(n):
        arrived(gout[n].at[:, pl.ds(0, 2)], R_G + 7 * n + 5)
        for k, (a1, a2, a3) in enumerate(ORDERS):
            part = gout[n].at[k, around(a3, 3), pl.ds(0, 2)]
            send(part, part, S_G + 7 * n + 6, R_G + 7 * n + 6, peer(a3, 1))
            part = gout[n].at[k, around(a3, 1), pl.ds(2, 2)]
            send(part, part, S_G + 7 * n + 6, R_G + 7 * n + 6, peer(a3, 3))
        for off in (0, 1, 3):
            keep(n, off)

    def sums_7(n):
        arrived(gout[n].at[:, 0], R_G + 7 * n + 6)
        keep(n, 2)

    for k in range(COLORS):
        gsend[CONTACT_G][k, 3 * L:] = jnp.zeros((GROUPS[CONTACT_G] - 3 * L, COLS), BF)
    put(NODE_G, 3 * L, mm_tn(a, n_dy))
    for i in range(3):
        put(NODE_G, i * L, mm_tn(nbuf[:, i * L:(i + 1) * L], n_dz))
    sums_1(NODE_G)
    own_low = dzown[...].reshape(NODES, L).astype(BF)
    put(CONTACT_G, 0, mm_tn(x, own_low))
    hidden = jnp.concatenate(
        [dz_all[k, 0, 0:ROWS].reshape(ROWS * BLOCK, COLS) for k in range(COLORS)], axis=1
    )
    put(CONTACT_G, L, mm_tn(c_x[...], hidden))
    put(CONTACT_G, 2 * L, mm_tn(c_a[...], c_dy[...]))
    sums_1(CONTACT_G)
    sums_1b(NODE_G)

    dmesh[...] = mm_nt(n_dz, wni[L:2 * L]).astype(BF)
    loads[7].wait()

    def edge_backward(t):
        rows = pl.ds(pl.multiple_of(t * TILE, TILE), TILE)
        nodes = pl.ds(pl.multiple_of(t * quarter, quarter), quarter)
        g = ecot[rows].astype(F32) + mm(fan, dmesh[nodes])
        dy = norm_back(e_u[rows].astype(F32), e_r[rows], g).astype(BF)
        dz = (mm_nt(dy, weo[...]) * e_h[rows]).astype(BF)
        edge_grad[rows] = (g + mm_nt(dz, wei[0:L])).astype(BF)
        tsum[nodes] = mm_tn(fan, dz).astype(BF)
        e_dy[rows] = dy
        e_dz[rows] = dz

    def pass_on(tile):
        arrived(dz_all.at[:, pl.ds(0, 2), pl.ds(0, 2)], R_B1 + tile)
        for k, (a1, a2, a3) in enumerate(ORDERS):
            even, odd = pl.ds(2 * tile, 1), pl.ds(2 * tile + 1, 1)
            send(dz_all.at[k, 3, even], dz_all.at[k, 2, even], S_B1B, R_B1B, peer(a3, 1))
            send(dz_all.at[k, 1, odd], dz_all.at[k, 2, odd], S_B1B, R_B1B, peer(a3, 3))

    @pl.loop(0, 4)
    def _(t):
        edge_backward(t)

        @pl.when(t > 0)
        def _():
            pass_on(2 * t - 1)

        pass_on(2 * t)

    write(edge_grad, edge_grad_hbm, 12)
    sums_1b(CONTACT_G)
    spread = mm_tn(onehot[...], e_dz[...])
    spread_low = spread.astype(BF)
    rim_out[0] = spread_low[0:RIM]
    rim_out[1] = spread_low[RIM + NODES:]
    send(rim_out.at[0], rim_in.at[0], S_RIM, R_RIM, down)
    send(rim_out.at[1], rim_in.at[1], S_RIM, R_RIM, up)
    pass_on(7)
    put(EDGE_G, L, mm_tn(xext[...], spread_low))
    put(EDGE_G, 0, mm_tn(es[...], e_dz[...]))
    put(EDGE_G, 2 * L, mm_tn(x, tsum[...]))
    put(EDGE_G, 3 * L, mm_tn(e_a[...], e_dy[...]))
    sums_1(EDGE_G)
    sums_2(NODE_G)

    arrived(dz_all.at[:, 2, pl.ds(0, ROWS)], R_B1B)
    sent(plane.at[:, pl.ds(0, 16)], S_F2)
    sent(plane.at[:, pl.ds(0, 8)], S_F2B)
    sent(r3, S_F1)

    def slot_sum(k, s):
        total = jnp.zeros((BLOCK, COLS), F32)
        for j in range(SIDE):
            for i in range(2):
                total += dz_all[k, j, table_s[2 * j + i, k * 32 + s]].astype(F32)
        return total

    own, near, far, last = [[around(a2, off) * 8 for a1, a2, a3 in ORDERS] for off in range(4)]

    @pl.loop(0, 8)
    def _(s):
        for k in range(COLORS):
            plane[k, far[k] + s] = slot_sum(k, far[k] + s).astype(BF)

    for k, (a1, a2, a3) in enumerate(ORDERS):
        send(plane.at[k, pl.ds(far[k], 4)], r2h.at[k, 0], S_B2H, R_B2H, peer(a2, 1))
        send(plane.at[k, pl.ds(far[k] + 4, 4)], r2h.at[k, 1], S_B2H, R_B2H, peer(a2, 3))
    sums_1b(EDGE_G)
    sums_2(CONTACT_G)

    @pl.loop(0, 4)
    def _(s):
        for k in range(COLORS):
            plane[k, near[k] + 4 + s] = slot_sum(k, near[k] + 4 + s).astype(BF)
            plane[k, last[k] + s] = slot_sum(k, last[k] + s).astype(BF)

    arrived(r2h, R_B2H)

    @pl.loop(0, 4)
    def _(s):
        for k in range(COLORS):
            plane[k, near[k] + s] = (slot_sum(k, near[k] + s) + r2h[k, 0, s].astype(F32)).astype(BF)
            plane[k, last[k] + 4 + s] = (slot_sum(k, last[k] + 4 + s) + r2h[k, 1, s].astype(F32)).astype(BF)

    for k, (a1, a2, a3) in enumerate(ORDERS):
        send(plane.at[k, pl.ds(near[k], 8)], r2.at[k, 0], S_B2, R_B2, peer(a2, 1))
        send(plane.at[k, pl.ds(last[k], 8)], r2.at[k, 1], S_B2, R_B2, peer(a2, 3))
    sums_3(NODE_G)

    @pl.loop(0, 8)
    def _(s):
        for k in range(COLORS):
            plane[k, own[k] + s] = slot_sum(k, own[k] + s).astype(BF)

    sums_2(EDGE_G)
    sums_4(NODE_G)
    sums_3(CONTACT_G)
    grad = ncot + mm_nt(n_dz, wni[0:L]) + mm_nt(tsum[...], wei[2 * L:]) + mm_nt(own_low, wci[0:L])

    arrived(r2, R_B2)
    for k, (a1, a2, a3) in enumerate(ORDERS):
        @pl.loop(0, 8)
        def _(s):
            total = plane[k, coord[a2] * 8 + s].astype(F32)
            for o in range(2):
                total += r2[k, o, s].astype(F32)
            r3src[k, s] = total.astype(BF)

        for off in (1, 2, 3):
            send(
                r3src.at[k, pl.ds(around(a1, off) * 2, 2)], r3.at[k, off - 1],
                S_B3, R_B3, peer(a1, off),
            )
    sums_3(EDGE_G)
    sums_5(NODE_G)
    sums_4(CONTACT_G)
    arrived(rim_in, R_RIM)
    first = spread[RIM:2 * RIM] + rim_in[1].astype(F32) * has_low
    last = spread[NODES:NODES + RIM] + rim_in[0].astype(F32) * has_high
    own_spread = jnp.concatenate([first, spread[2 * RIM:NODES], last], axis=0).astype(BF)
    grad += mm_nt(own_spread, wei[L:2 * L])
    arrived(r3, R_B3)
    cols = []
    for k, (a1, a2, a3) in enumerate(ORDERS):
        halves = [r3src[k, coord[a1] * 2 + b].astype(F32) for b in range(2)]
        for off in (1, 2, 3):
            halves = [halves[b] + r3[k, off - 1, b].astype(F32) for b in range(2)]
        cols.append(jnp.concatenate(halves, axis=0).astype(BF))
    s_rem = jnp.concatenate(cols, axis=1)
    node_grad[...] = (grad + mm_nt(s_rem, wci[L:])).astype(BF)
    write(node_grad, node_grad_hbm, 13)

    sums_4(EDGE_G)
    sums_6(NODE_G)
    sums_5(CONTACT_G)
    sums_5(EDGE_G)
    sums_6(CONTACT_G)
    sums_7(NODE_G)
    sums_6(EDGE_G)
    sums_7(CONTACT_G)
    sums_7(EDGE_G)

    for ref, sem in (
        (meta_v.at[:, pl.ds(1, 3)], S_META), (halo, S_HALO), (rim_in, S_RIM), (hs, S_H), (sbuf, S_F3), (sbuf, S_B1),
        (dz_all.at[:, 2, pl.ds(0, ROWS)], S_B1B), (r2h, S_B2H), (r2, S_B2), (r3, S_B3),
    ):
        sent(ref, sem)
    for n in range(3):
        refs = (g1h[n], g1[n], g2[n], g2[n], g2[n], gout[n].at[:, pl.ds(0, 2)], gout[n].at[:, 0])
        for i, ref in enumerate(refs):
            sent(ref, S_G + 7 * n + i)
    for out in outs:
        out.wait()


def dma(*shape):
    return pltpu.SemaphoreType.DMA(shape)


def vm(shape, dtype):
    return pltpu.VMEM(shape, dtype)


def fused(x, src, ncot, block, host, remote, es, ecot, wei, weo, wni, wno, wci, wco):
    tile = (BLOCK, COLS)
    pieces = [rows // 16 for rows in GROUPS]
    scratch = [
        vm((EDGES, L), BF), vm((EDGES, L), BF), vm((3 * L, L), BF), vm((L, L), BF), vm((3 * L, L), BF),
        vm((L, L), BF), vm((2 * L, L), BF), vm((L, L), BF),
        vm((COLORS, 32) + tile, BF),
        vm((COLORS, 2, ROWS, HALF, COLS), BF),
        [vm((COLORS, 2, CHUNK, HALF, COLS), BF) for _ in range(N_CHUNK)],
        vm((COLORS, 2, ROWS) + tile, BF),
        [vm((COLORS, 3, CHUNK) + tile, BF) for _ in range(N_CHUNK)],
        vm((COLORS, SIDE, ROWS + 1) + tile, BF),
        vm((COLORS, 2, 4) + tile, BF), vm((COLORS, 2, 8) + tile, BF), vm((COLORS, 3, 2) + tile, BF), vm((COLORS, 8) + tile, BF),
        [vm((COLORS, rows, COLS), BF) for rows in GROUPS],
        [vm((COLORS, 2, rows // 8, COLS), BF) for rows in GROUPS],
        [vm((COLORS, 2, rows // 4, COLS), BF) for rows in GROUPS],
        [vm((COLORS, SIDE, piece, COLS), BF) for piece in pieces],
        [vm((COLORS, 3, piece, COLS), BF) for piece in pieces],
        [vm((COLORS, SIDE, piece, COLS), BF) for piece in pieces],
        [vm((COLORS, SIDE, SIDE, piece, COLS), BF) for piece in pieces],
        vm((NODES, L), BF), vm((EDGES, L), BF), vm((NODES, L), BF), vm((EDGES, L), BF),
        vm((2, RIM, L), BF), vm((2, RIM, L), BF), vm((2, RIM, L), BF), vm((NODES + 2 * RIM, L), BF), vm((EDGES, L), BF),
        vm((3, SIDE, ROWS, 128), jnp.int32), pltpu.SMEM((3, SIDE, ROWS, 128), jnp.int32),
        vm((8, 128), jnp.int32), pltpu.SMEM((8, 128), jnp.int32),
        vm((EDGES, L), BF), vm((EDGES, 1), F32), vm((EDGES, L), F32), vm((EDGES, L), BF),
        vm((EDGES, L), BF), vm((EDGES, L), BF), vm((NODES, L), BF),
        vm((ROWS * BLOCK, L), BF), vm((ROWS * BLOCK, L), BF), vm((ROWS * BLOCK, 1), F32), vm((ROWS * BLOCK, L), F32),
        vm((ROWS * BLOCK, L), BF),
        vm((ROWS * BLOCK, L), BF), vm((2, BLOCK, L), F32), vm((2, BLOCK, L), F32), vm((2, BLOCK, L), F32),
        vm((NODES, L), BF), vm((NODES, 3 * L), BF), vm((2, BLOCK, L), BF), vm((NODES, L), BF),
        dma(50), dma(S_G + 21), dma(R_G + 21),
    ]
    here = pl.BlockSpec(memory_space=pltpu.VMEM)
    there = pl.BlockSpec(memory_space=pl.ANY)
    scalars = pl.BlockSpec(memory_space=pltpu.SMEM)
    return pl.pallas_call(
        body,
        out_shape=(
            jax.ShapeDtypeStruct((NODES, L), BF), jax.ShapeDtypeStruct((EDGES, L), BF),
            jax.ShapeDtypeStruct((NODES, L), BF), jax.ShapeDtypeStruct((EDGES, L), BF),
        ) + tuple(jax.ShapeDtypeStruct((COLORS, SIDE, SIDE, piece, COLS), BF) for piece in pieces),
        in_specs=[here] * 3 + [scalars] * 3 + [there] * 8,
        out_specs=[there] * 7,
        scratch_shapes=scratch,
        compiler_params=pltpu.CompilerParams(
            collective_id=0, has_side_effects=True, vmem_limit_bytes=63 * 1024 * 1024
        ),
        name="layer",
    )(x, src, ncot, block, host, remote, es, ecot, wei, weo, wni, wno, wci, wco)


def finish_body(*refs):
    plain_in, packed_in = refs[0:4], refs[4:7]
    plain_out, wide_out = refs[7:11], refs[11:17]
    plain, packed, wide, in_sem, out_sem = refs[17:21], refs[21:24], refs[24:27], refs[27], refs[28]
    chunks = []
    for n, count in enumerate((3, 2, 3)):
        chunks += [(n, i * L, 2 * n + i // count, i % count * L) for i in range(count + 1)]
    loads = [
        pltpu.make_async_copy(packed_in[n].at[:, pl.ds(row, L)], packed[n].at[:, pl.ds(row, L)], in_sem.at[i])
        for i, (n, row, _, _) in enumerate(chunks)
    ]
    loads += [pltpu.make_async_copy(plain_in[i], plain[i], in_sem.at[len(chunks) + i]) for i in range(4)]
    for load in loads:
        load.start()
    stores = []

    def store(src, dst):
        copy = pltpu.make_async_copy(src, dst, out_sem.at[len(stores)])
        copy.start()
        stores.append(copy)

    for i, (n, row, which, there) in enumerate(chunks):
        loads[i].wait()
        for k in range(COLORS):
            wide[n][row:row + L, k * COLS:(k + 1) * COLS] = packed[n][k, row:row + L].astype(F32)
        store(wide[n].at[pl.ds(row, L)], wide_out[which].at[pl.ds(there, L)])
    for i in range(4):
        loads[len(chunks) + i].wait()
        store(plain[i], plain_out[i])
    for copy in stores:
        copy.wait()


def finish(plain, packed):
    packed = [p.reshape(COLORS, rows, COLS) for p, rows in zip(packed, GROUPS)]
    there = pl.BlockSpec(memory_space=pl.ANY)
    shapes = [jax.ShapeDtypeStruct(p.shape, p.dtype) for p in plain]
    shapes += [jax.ShapeDtypeStruct((n * L, L), F32) for n in (3, 1, 2, 1, 3, 1)]
    return pl.pallas_call(
        finish_body,
        out_shape=shapes,
        in_specs=[there] * 7,
        out_specs=[there] * 10,
        scratch_shapes=[
            *[vm(p.shape, p.dtype) for p in plain],
            *[vm((COLORS, rows, COLS), BF) for rows in GROUPS],
            *[vm((rows, L), F32) for rows in GROUPS],
            dma(15), dma(15),
        ],
        compiler_params=pltpu.CompilerParams(vmem_limit_bytes=63 * 1024 * 1024),
        name="finish",
    )(*plain, *packed)


def on_device(
    node_state, edge_state, edge_source, contact_block, contact_host, contact_remote,
    w_edge_in, w_edge_out, w_node_in, w_node_out, w_contact_in, w_contact_out, node_cot, edge_cot,
):
    results = fused(
        node_state, edge_source.reshape(8, 128), node_cot, contact_block, contact_host.reshape(ROWS), contact_remote,
        edge_state, edge_cot, w_edge_in, w_edge_out, w_node_in, w_node_out, w_contact_in, w_contact_out,
    )
    out = finish(results[:4], results[4:])
    node_in, node_last, contact_in, contact_last, edge_in, edge_last = out[4:]
    return tuple(out[:4]) + (edge_in, edge_last, node_in, node_last, contact_in, contact_last)


def solution(mesh):
    rows = P(("rep", "dom"), None)
    flat = P(("rep", "dom"))
    weight = P("rep", None)
    return jax.shard_map(
        on_device,
        mesh=mesh,
        in_specs=(rows, rows, flat, flat, rows, flat) + (weight,) * 6 + (rows, rows),
        out_specs=(rows,) * 4 + (weight,) * 6,
        check_vma=False,
    )
```

```python
import functools

import jax
import jax.numpy as jnp
from jax import lax
from jax.experimental import pallas as pl
from jax.experimental.pallas import tpu as pltpu
from jax.sharding import PartitionSpec as P

L = 384
BLOCK = 128
EPN = 4
RIM = 64
NODES = 256
EDGES = 1024
ROWS = 16
TILE = 256
COLORS = 3
COLS = 128
SIDE = 4
DOM = 64
EPS = 1e-05
BF = jnp.bfloat16
F32 = jnp.float32
MESH = pl.DeviceIdType.MESH

GROUPS = (1536, 1280, 1536)
NODE_G, CONTACT_G, EDGE_G = 0, 1, 2

ORDERS = (("z", "x", "y"), ("x", "y", "z"), ("y", "z", "x"))
STRIDE = {"y": 16, "x": 4, "z": 1}
AXES = ("y", "x", "z")
N_CHUNK = 4
S_META, S_HALO, S_RIM, S_F1, S_F2, S_F2B, S_H, S_F3, S_B1, S_B1B, S_B2H, S_B2, S_B3, S_G = range(14)
R_META, R_HALO, R_RIM, R_F1, R_F2, R_F2B, R_H, R_F3, R_B1, R_B1B, R_B2H, R_B2, R_B3, R_G = (
    0, 1, 2, 3, 6, 9, 10, 14, 18, 26, 27, 28, 29, 30
)
CHUNK = ROWS // N_CHUNK
HALF = BLOCK // 2


def mm(a, b):
    return lax.dot_general(a, b, (((1,), (0,)), ((), ())), preferred_element_type=F32)


def mm_nt(a, b):
    return lax.dot_general(a, b, (((1,), (1,)), ((), ())), preferred_element_type=F32)


def mm_tn(a, b):
    return lax.dot_general(a, b, (((0,), (0,)), ((), ())), preferred_element_type=F32)


def row_mean(v):
    return jnp.sum(v, axis=-1, keepdims=True) * (1.0 / L)


def norm(y):
    center = y - row_mean(y)
    scale = lax.rsqrt(row_mean(center * center) + EPS)
    return center * scale, scale


def norm_back(u, scale, g):
    return scale * (g - row_mean(g) - u * row_mean(g * u))


def silu_parts(z):
    s = jax.nn.sigmoid(z)
    return (z * s).astype(BF), s * (1.0 + z * (1.0 - s))


def body(
    x_ref, src_ref, ncot_ref, block_ref, host_ref, remote_ref,
    es_hbm, ecot_hbm, wei_hbm, weo_hbm, wni_hbm, wno_hbm, wci_hbm, wco_hbm,
    node_out_hbm, edge_out_hbm, node_grad_hbm, edge_grad_hbm, node_hbm, contact_hbm, edge_hbm,
    es, ecot, wei, weo, wni, wno, wci, wco,
    plane, hs, hr, sbuf, rbuf, dz_near, dz_far, r2h, r2, r3, r3src,
    gsend, g1h, g1, g2src, g2, g3, gout, node_out, edge_out, node_grad, edge_grad,
    halo, rim_out, rim_in, xext, onehot,
    meta_v, meta_s, table_v, table_s,
    e_u, e_r, e_h, e_a, e_dy, e_dz, mesh_sum,
    c_x, c_u, c_r, c_h, c_a, c_dy, p_own, csum, dzown, tsum, nbuf, dcon, dmesh,
    local_sem, ss, rs,
):
    me = lax.axis_index("dom")
    coord = {"y": lax.div(me, 16), "x": lax.rem(lax.div(me, 4), 4), "z": lax.rem(me, 4)}

    def around(axis, off):
        return lax.rem(coord[axis] + off, SIDE)

    def peer(axis, off):
        return me + (around(axis, off) - coord[axis]) * STRIDE[axis]

    up, down = lax.rem(me + 1, DOM), lax.rem(me + DOM - 1, DOM)

    def remote(src, dst, to, at, dev):
        return pltpu.make_async_remote_copy(
            src_ref=src, dst_ref=dst, send_sem=ss.at[to], recv_sem=rs.at[at],
            device_id={"dom": dev}, device_id_type=MESH,
        )

    def arrived(ref, sem):
        remote(ref, ref, 0, sem, up).wait_recv()

    def sent(ref, sem):
        remote(ref, ref, sem, 0, up).wait_send()

    def send(*args):
        remote(*args).start()

    loads = [
        pltpu.make_async_copy(src, dst, local_sem.at[i])
        for i, (src, dst) in enumerate(
            [(wci_hbm, wci), (es_hbm, es), (wei_hbm, wei), (weo_hbm, weo), (wco_hbm, wco),
             (wni_hbm, wni), (wno_hbm, wno), (ecot_hbm, ecot)]
        )
    ]
    for load in loads:
        load.start()

    outs = []

    def write(src, dst, i):
        out = pltpu.make_async_copy(src, dst, local_sem.at[i])
        out.start()
        outs.append(out)

    barrier = pltpu.get_barrier_semaphore()
    for axis in AXES:
        for off in (1, 2, 3):
            pl.semaphore_signal(barrier, inc=1, device_id={"dom": peer(axis, off)}, device_id_type=MESH)
    pl.semaphore_signal(barrier, inc=1, device_id={"dom": up}, device_id_type=MESH)
    pl.semaphore_signal(barrier, inc=1, device_id={"dom": down}, device_id_type=MESH)

    x = x_ref[...]
    place = lax.broadcasted_iota(jnp.int32, (1, 128), 1)
    for c in range(ROWS):
        host = host_ref[c]
        at = {"y": lax.div(host, 16), "x": lax.rem(lax.div(host, 4), 4), "z": lax.rem(host, 4)}
        code = [((at[a3] * SIDE + at[a2]) * SIDE + at[a1]) * 2 + remote_ref[c] for a1, a2, a3 in ORDERS]
        line = jnp.where(place < 32, code[0], jnp.where(place < 64, code[1], code[2]))
        line = jnp.where(place < 96, line, block_ref[c])
        for i in range(3):
            meta_v[i, 0, c:c + 1] = line
    for k, (a1, a2, a3) in enumerate(ORDERS):
        own = (coord[a2] * SIDE + coord[a1]) * 2
        for b in range(2):
            plane[k, own + b] = x_ref[b * BLOCK:(b + 1) * BLOCK, k * COLS:(k + 1) * COLS]
    pl.semaphore_wait(barrier, 11)

    for k, (a1, a2, a3) in enumerate(ORDERS):
        own = (coord[a2] * SIDE + coord[a1]) * 2
        for off in (1, 2, 3):
            part = plane.at[k, pl.ds(own, 2)]
            send(part, part, S_F1, R_F1 + k, peer(a1, off))
        part = plane.at[k, pl.ds(own, 2)]
        send(part, part, S_F2, R_F2 + k, peer(a2, 1))
        send(part, part, S_F2, R_F2 + k, peer(a2, 3))
    send(x_ref.at[pl.ds(NODES - RIM, RIM)], halo.at[0], S_HALO, R_HALO, up)
    send(x_ref.at[pl.ds(0, RIM)], halo.at[1], S_HALO, R_HALO, down)
    for i, axis in enumerate(AXES):
        for off in (1, 2, 3):
            send(meta_v.at[i, 0], meta_v.at[i, SIDE - off], S_META, R_META, peer(axis, off))

    lanes = lax.broadcasted_iota(jnp.int32, (BLOCK, L), 1)
    idx = jnp.concatenate([src_ref[...].astype(F32)] * 16, axis=0).T
    for j in range(EDGES // BLOCK):
        col = idx[:, j:j + 1].astype(jnp.int32)
        onehot[j * BLOCK:(j + 1) * BLOCK, :] = jnp.where(col == lanes, 1.0, 0.0).astype(BF)
    for k in range(COLORS):
        for j in range(3):
            dz_near[k, j, ROWS] = jnp.zeros((BLOCK, COLS), BF)
        dz_far[k, ROWS] = jnp.zeros((BLOCK, COLS), BF)
    csum[...] = jnp.zeros_like(csum)
    dzown[...] = jnp.zeros_like(dzown)
    loads[0].wait()
    p_own[...] = mm(x, wci[0:L]).reshape(2, BLOCK, L)

    for k, (a1, a2, a3) in enumerate(ORDERS):
        arrived(plane.at[k, pl.ds(0, 6)], R_F1 + k)
        for off in (1, 2, 3):
            part = plane.at[k, pl.ds((coord[a2] * SIDE + around(a1, off)) * 2, 2)]
            send(part, part, S_F2, R_F2 + k, peer(a2, 1))
            send(part, part, S_F2, R_F2 + k, peer(a2, 3))

    arrived(halo, R_HALO)
    has_low = (me > 0).astype(F32)
    has_high = (me < DOM - 1).astype(F32)
    xext[0:RIM] = (halo[0].astype(F32) * has_low).astype(BF)
    xext[RIM:RIM + NODES] = x
    xext[RIM + NODES:] = (halo[1].astype(F32) * has_high).astype(BF)

    arrived(meta_v.at[:, pl.ds(1, 3)], R_META)
    mine = [coord[a3] * 32 for a1, a2, a3 in ORDERS]
    sought = lax.rem(place, 32) + jnp.where(place < 32, mine[0], jnp.where(place < 64, mine[1], mine[2]))
    wide = lax.broadcasted_iota(jnp.int32, (ROWS, 128), 1)
    for j in range(SIDE):
        asked = [meta_v[AXES.index(a3), j] for a1, a2, a3 in ORDERS]
        asked = jnp.where(wide < 32, asked[0], jnp.where(wide < 64, asked[1], asked[2]))
        first = second = jnp.full((1, 128), ROWS, jnp.int32)
        for c in reversed(range(ROWS)):
            hit = asked[c:c + 1] == sought
            second = jnp.where(hit, first, second)
            first = jnp.where(hit, c, first)
        table_v[2 * j:2 * j + 1] = first
        table_v[2 * j + 1:2 * j + 2] = second
    to_smem = [
        pltpu.make_async_copy(meta_v, meta_s, local_sem.at[8]),
        pltpu.make_async_copy(table_v, table_s, local_sem.at[9]),
    ]
    for copy in to_smem:
        copy.start()

    for load in loads[1:4]:
        load.wait()

    quarter = TILE // EPN
    fan = jnp.where(
        lax.div(lax.broadcasted_iota(jnp.int32, (TILE, quarter), 0), EPN)
        == lax.broadcasted_iota(jnp.int32, (TILE, quarter), 1), 1.0, 0.0,
    ).astype(BF)

    def edge_forward(t):
        rows = pl.ds(pl.multiple_of(t * TILE, TILE), TILE)
        nodes = pl.ds(pl.multiple_of(t * quarter, quarter), quarter)
        state = es[rows]
        src = mm(onehot[rows], xext[...]).astype(BF)
        tgt = mm(fan, x_ref[nodes]).astype(BF)
        z = mm(state, wei[0:L]) + mm(src, wei[L:2 * L]) + mm(tgt, wei[2 * L:])
        a, h = silu_parts(z)
        u, r = norm(mm(a, weo[...]))
        out = (state.astype(F32) + u).astype(BF)
        edge_out[rows] = out
        mesh_sum[nodes] = mm_tn(fan, out).astype(BF)
        e_a[rows] = a
        e_h[rows] = h
        e_u[rows] = u.astype(BF)
        e_r[rows] = r

    for k, (a1, a2, a3) in enumerate(ORDERS):
        arrived(plane.at[k, pl.ds(0, 16)], R_F2 + k)
        part = plane.at[k, pl.ds(around(a2, 3) * 8, 4)]
        send(part, part, S_F2B, R_F2B, peer(a2, 1))
        part = plane.at[k, pl.ds(around(a2, 1) * 8 + 4, 4)]
        send(part, part, S_F2B, R_F2B, peer(a2, 3))

    edge_forward(0)

    for copy in to_smem:
        copy.wait()
    arrived(plane.at[:, pl.ds(0, 8)], R_F2B)

    def request(k, j, c):
        code = meta_s[AXES.index(ORDERS[k][2]), j, c, k * 32]
        return lax.rem(code, 32), lax.div(code, 32)

    for q in range(N_CHUNK):
        for k, (a1, a2, a3) in enumerate(ORDERS):
            for c in range(CHUNK):
                slot, _ = request(k, 2, q * CHUNK + c)
                hs[k, 0, q * CHUNK + c] = plane[k, slot, 0:HALF]
                hs[k, 1, q * CHUNK + c] = plane[k, slot, HALF:]
            part = pl.ds(q * CHUNK, CHUNK)
            send(hs.at[k, 0, part], hr[q].at[k, 0], S_H, R_H + q, peer(a3, 3))
            send(hs.at[k, 1, part], hr[q].at[k, 1], S_H, R_H + q, peer(a3, 1))
    for q in range(N_CHUNK):
        arrived(hr[q], R_H + q)
        for k, (a1, a2, a3) in enumerate(ORDERS):
            for c in range(CHUNK):
                row = q * CHUNK + c
                slot, where = request(k, 3, row)
                own = where == coord[a3]
                sbuf[k, 0, row, 0:HALF] = jnp.where(own, plane[k, slot, 0:HALF], hr[q][k, 0, c])
                sbuf[k, 0, row, HALF:] = plane[k, slot, HALF:]
                slot, where = request(k, 1, row)
                own = where == coord[a3]
                sbuf[k, 1, row, 0:HALF] = plane[k, slot, 0:HALF]
                sbuf[k, 1, row, HALF:] = jnp.where(own, plane[k, slot, HALF:], hr[q][k, 1, c])
            part = pl.ds(q * CHUNK, CHUNK)
            send(sbuf.at[k, 0, part], rbuf[q].at[k, 1], S_F3, R_F3 + q, peer(a3, 3))
            send(sbuf.at[k, 1, part], rbuf[q].at[k, 2], S_F3, R_F3 + q, peer(a3, 1))
        for k in range(COLORS):
            for c in range(CHUNK):
                rbuf[q][k, 0, c] = plane[k, request(k, 0, q * CHUNK + c)[0]]
        if q < 3:
            edge_forward(q + 1)

    loads[4].wait()
    for q in range(N_CHUNK):
        arrived(rbuf[q].at[:, pl.ds(1, 2)], R_F3 + q)

        @pl.loop(0, CHUNK // 2)
        def _(p):
            parts, owns, weights = [], [], []
            for s in range(2):
                c = q * CHUNK + 2 * p + s
                cols = []
                for k, (a1, a2, a3) in enumerate(ORDERS):
                    away = lax.rem(request(k, 0, c)[1] - coord[a3] + SIDE, SIDE)
                    cols.append(jnp.concatenate([
                        rbuf[q][k, lax.div(away + 1, 2), 2 * p + s, 0:HALF],
                        rbuf[q][k, jnp.minimum(away, 2), 2 * p + s, HALF:],
                    ], axis=0))
                parts.append(jnp.concatenate(cols, axis=1))
                block = meta_s[0, 0, c, 96]
                owns.append(p_own[block])
                weights.append(block.astype(F32))
            rows = pl.ds(pl.multiple_of(q * CHUNK * BLOCK + p * TILE, TILE), TILE)
            remote_rows = jnp.concatenate(parts, axis=0)
            c_x[rows] = remote_rows
            z = mm(remote_rows, wci[L:]) + jnp.concatenate(owns, axis=0)
            a, h = silu_parts(z)
            u, r = norm(mm(a, wco[...]))
            c_a[rows] = a
            c_h[rows] = h
            message = u.astype(BF)
            c_u[rows] = message
            c_r[rows] = r
            message = message.astype(F32)
            for s in range(2):
                m = message[s * BLOCK:(s + 1) * BLOCK]
                csum[1] += m * weights[s]
                csum[0] += m * (1.0 - weights[s])

    loads[5].wait()
    loads[6].wait()
    nbuf[:, 0:L] = x
    nbuf[:, L:2 * L] = mesh_sum[...]
    nbuf[:, 2 * L:] = csum[...].reshape(NODES, L).astype(BF)
    a, h = silu_parts(mm(nbuf[...], wni[...]))
    u, r = norm(mm(a, wno[...]))
    node_out[...] = (x.astype(F32) + u).astype(BF)
    write(node_out, node_out_hbm, 10)
    write(edge_out, edge_out_hbm, 11)
    ncot = ncot_ref[...].astype(F32)
    n_dy = norm_back(u, r, ncot).astype(BF)
    n_dz = (mm_nt(n_dy, wno[...]) * h).astype(BF)
    dcon[...] = mm_nt(n_dz, wni[2 * L:]).astype(BF).reshape(2, BLOCK, L)

    @pl.loop(0, ROWS // 2)
    def _(t):
        rows = pl.ds(pl.multiple_of(t * TILE, TILE), TILE)
        blocks = [meta_s[0, 0, 2 * t + s, 96] for s in range(2)]
        g = jnp.concatenate([dcon[b] for b in blocks], axis=0).astype(F32)
        dy = norm_back(c_u[rows].astype(F32), c_r[rows], g).astype(BF)
        c_dy[rows] = dy
        dz = (mm_nt(dy, wco[...]) * c_h[rows]).astype(BF)
        for s in range(2):
            part = dz[s * BLOCK:(s + 1) * BLOCK]
            weight = blocks[s].astype(F32)
            dzown[1] += part.astype(F32) * weight
            dzown[0] += part.astype(F32) * (1.0 - weight)
            for k in range(COLORS):
                dz_near[k, 0, 2 * t + s] = part[:, k * COLS:(k + 1) * COLS]

        @pl.when(lax.rem(t, 2) == 1)
        def _():
            four = pl.ds(2 * t - 2, 4)
            for k, (a1, a2, a3) in enumerate(ORDERS):
                chunk = lax.div(t, 2)
                send(dz_near.at[k, 0, four], dz_near.at[k, 2, four], S_B1, R_B1 + chunk, peer(a3, 1))
                send(dz_near.at[k, 0, four], dz_near.at[k, 1, four], S_B1, R_B1 + chunk, peer(a3, 3))

    def put(group, row, value):
        value = value.astype(BF)
        for k in range(COLORS):
            gsend[group][k, row:row + L] = value[:, k * COLS:(k + 1) * COLS]

    def sums_1(n):
        size = GROUPS[n] // 4
        half = size // 2
        for k, (a1, a2, a3) in enumerate(ORDERS):
            far = around(a3, 2) * size
            send(gsend[n].at[k, pl.ds(far, half)], g1h[n].at[k, 0], S_G + 7 * n, R_G + 7 * n, peer(a3, 1))
            send(gsend[n].at[k, pl.ds(far + half, half)], g1h[n].at[k, 1], S_G + 7 * n, R_G + 7 * n, peer(a3, 3))

    def sums_1b(n):
        size = GROUPS[n] // 4
        half = size // 2
        arrived(g1h[n], R_G + 7 * n)
        for k, (a1, a2, a3) in enumerate(ORDERS):
            for i, off in enumerate((1, 3)):
                start = around(a3, off) * size
                rows = pl.ds(pl.multiple_of(start + i * half, 16), half)
                total = gsend[n][k, rows].astype(F32) + g1h[n][k, i].astype(F32)
                gsend[n][k, rows] = total.astype(BF)
                send(
                    gsend[n].at[k, pl.ds(start, size)], g1[n].at[k, i],
                    S_G + 7 * n + 1, R_G + 7 * n + 1, peer(a3, off),
                )

    def sums_2(n):
        size = GROUPS[n] // 4
        piece = size // 4
        arrived(g1[n], R_G + 7 * n + 1)
        for k, (a1, a2, a3) in enumerate(ORDERS):
            @pl.loop(0, 4)
            def _(t):
                rows = pl.ds(pl.multiple_of(t * piece, 16), piece)
                total = gsend[n][k, pl.ds(pl.multiple_of(coord[a3] * size + t * piece, 16), piece)].astype(F32)
                for o in range(2):
                    total += g1[n][k, o, rows].astype(F32)
                g2src[n][k, t] = total.astype(BF)

            for off in (2, 1, 3):
                send(
                    g2src[n].at[k, around(a2, off)], g2[n].at[k, off - 1],
                    S_G + 7 * n + 2, R_G + 7 * n + 2, peer(a2, off),
                )

    def sums_3(n):
        arrived(g2[n], R_G + 7 * n + 2)
        for k, (a1, a2, a3) in enumerate(ORDERS):
            total = g2src[n][k, coord[a2]].astype(F32)
            for o in range(3):
                total += g2[n][k, o].astype(F32)
            g3[n][k, coord[a1]] = total.astype(BF)
            part = g3[n].at[k, coord[a1]]
            for off in (2, 1, 3):
                send(part, part, S_G + 7 * n + 3, R_G + 7 * n + 3, peer(a1, off))

    def sums_4(n):
        arrived(g2[n], R_G + 7 * n + 3)
        for k, (a1, a2, a3) in enumerate(ORDERS):
            total = g3[n][k, 0].astype(F32)
            for o in range(1, SIDE):
                total += g3[n][k, o].astype(F32)
            gout[n][k, coord[a3], coord[a2]] = total.astype(BF)
            part = gout[n].at[k, coord[a3], coord[a2]]
            for off in (2, 1, 3):
                send(part, part, S_G + 7 * n + 4, R_G + 7 * n + 4, peer(a2, off))

    def sums_5(n):
        arrived(g2[n], R_G + 7 * n + 4)
        for k, (a1, a2, a3) in enumerate(ORDERS):
            part = gout[n].at[k, coord[a3]]
            send(part, part, S_G + 7 * n + 5, R_G + 7 * n + 5, peer(a3, 1))
            send(part, part, S_G + 7 * n + 5, R_G + 7 * n + 5, peer(a3, 3))

    def keep(n, off):
        for k, (a1, a2, a3) in enumerate(ORDERS):
            at = around(a3, off)
            write(gout[n].at[k, at], (node_hbm, contact_hbm, edge_hbm)[n].at[k, at], 14 + (n * 3 + k) * 4 + off)

    def sums_6(n):
        arrived(gout[n].at[:, pl.ds(0, 2)], R_G + 7 * n + 5)
        for k, (a1, a2, a3) in enumerate(ORDERS):
            part = gout[n].at[k, around(a3, 3), pl.ds(0, 2)]
            send(part, part, S_G + 7 * n + 6, R_G + 7 * n + 6, peer(a3, 1))
            part = gout[n].at[k, around(a3, 1), pl.ds(2, 2)]
            send(part, part, S_G + 7 * n + 6, R_G + 7 * n + 6, peer(a3, 3))
        for off in (0, 1, 3):
            keep(n, off)

    def sums_7(n):
        arrived(gout[n].at[:, 0], R_G + 7 * n + 6)
        keep(n, 2)

    for k in range(COLORS):
        gsend[CONTACT_G][k, 3 * L:] = jnp.zeros((GROUPS[CONTACT_G] - 3 * L, COLS), BF)
    put(NODE_G, 3 * L, mm_tn(a, n_dy))
    for i in range(3):
        put(NODE_G, i * L, mm_tn(nbuf[:, i * L:(i + 1) * L], n_dz))
    sums_1(NODE_G)
    own_low = dzown[...].reshape(NODES, L).astype(BF)
    put(CONTACT_G, 0, mm_tn(x, own_low))
    hidden = jnp.concatenate(
        [dz_near[k, 0, 0:ROWS].reshape(ROWS * BLOCK, COLS) for k in range(COLORS)], axis=1
    )
    put(CONTACT_G, L, mm_tn(c_x[...], hidden))
    put(CONTACT_G, 2 * L, mm_tn(c_a[...], c_dy[...]))
    sums_1(CONTACT_G)
    sums_1b(NODE_G)

    dmesh[...] = mm_nt(n_dz, wni[L:2 * L]).astype(BF)
    loads[7].wait()

    def edge_backward(t):
        rows = pl.ds(pl.multiple_of(t * TILE, TILE), TILE)
        nodes = pl.ds(pl.multiple_of(t * quarter, quarter), quarter)
        g = ecot[rows].astype(F32) + mm(fan, dmesh[nodes])
        dy = norm_back(e_u[rows].astype(F32), e_r[rows], g).astype(BF)
        dz = (mm_nt(dy, weo[...]) * e_h[rows]).astype(BF)
        edge_grad[rows] = (g + mm_nt(dz, wei[0:L])).astype(BF)
        tsum[nodes] = mm_tn(fan, dz).astype(BF)
        e_dy[rows] = dy
        e_dz[rows] = dz

    def pass_on(chunk):
        arrived(dz_near.at[:, pl.ds(0, 2), pl.ds(0, 4)], R_B1 + chunk)
        for k, (a1, a2, a3) in enumerate(ORDERS):
            even, odd = pl.ds(4 * chunk, 2), pl.ds(4 * chunk + 2, 2)
            send(dz_near.at[k, 2, even], dz_far.at[k, even], S_B1B, R_B1B, peer(a3, 1))
            send(dz_near.at[k, 1, odd], dz_far.at[k, odd], S_B1B, R_B1B, peer(a3, 3))

    @pl.loop(0, 4)
    def _(t):
        edge_backward(t)

        @pl.when(t > 0)
        def _():
            pass_on(t - 1)

    write(edge_grad, edge_grad_hbm, 12)
    sums_1b(CONTACT_G)
    sums_2(NODE_G)
    spread = mm_tn(onehot[...], e_dz[...])
    spread_low = spread.astype(BF)
    rim_out[0] = spread_low[0:RIM]
    rim_out[1] = spread_low[RIM + NODES:]
    send(rim_out.at[0], rim_in.at[0], S_RIM, R_RIM, down)
    send(rim_out.at[1], rim_in.at[1], S_RIM, R_RIM, up)
    pass_on(3)
    put(EDGE_G, L, mm_tn(xext[...], spread_low))
    put(EDGE_G, 0, mm_tn(es[...], e_dz[...]))
    put(EDGE_G, 2 * L, mm_tn(x, tsum[...]))
    put(EDGE_G, 3 * L, mm_tn(e_a[...], e_dy[...]))
    sums_1(EDGE_G)
    sums_2(CONTACT_G)
    sums_3(NODE_G)

    sent(plane.at[:, pl.ds(0, 16)], S_F2)
    sent(plane.at[:, pl.ds(0, 8)], S_F2B)
    sent(r3, S_F1)

    @pl.loop(0, 2 * 16)
    def _(s):
        for k in range(COLORS):
            total = jnp.zeros((BLOCK, COLS), F32)
            for at, j in enumerate((0, 1, 3)):
                for i in range(2):
                    total += dz_near[k, at, table_s[2 * j + i, k * 32 + s]].astype(F32)
            plane[k, s] = total.astype(BF)

    sums_1b(EDGE_G)
    sums_3(CONTACT_G)
    sums_4(NODE_G)
    arrived(dz_far.at[:, pl.ds(0, ROWS)], R_B1B)

    def slot_sum(k, s):
        total = plane[k, s].astype(F32)
        for i in range(2):
            total += dz_far[k, table_s[4 + i, k * 32 + s]].astype(F32)
        return total

    own, near, far, last = [[around(a2, off) * 8 for a1, a2, a3 in ORDERS] for off in range(4)]

    @pl.loop(0, 8)
    def _(s):
        for k in range(COLORS):
            plane[k, far[k] + s] = slot_sum(k, far[k] + s).astype(BF)

    for k, (a1, a2, a3) in enumerate(ORDERS):
        send(plane.at[k, pl.ds(far[k], 4)], r2h.at[k, 0], S_B2H, R_B2H, peer(a2, 1))
        send(plane.at[k, pl.ds(far[k] + 4, 4)], r2h.at[k, 1], S_B2H, R_B2H, peer(a2, 3))
    sums_2(EDGE_G)
    sums_4(CONTACT_G)
    sums_5(NODE_G)

    @pl.loop(0, 4)
    def _(s):
        for k in range(COLORS):
            plane[k, near[k] + 4 + s] = slot_sum(k, near[k] + 4 + s).astype(BF)
            plane[k, last[k] + s] = slot_sum(k, last[k] + s).astype(BF)

    arrived(r2h, R_B2H)

    @pl.loop(0, 4)
    def _(s):
        for k in range(COLORS):
            plane[k, near[k] + s] = (slot_sum(k, near[k] + s) + r2h[k, 0, s].astype(F32)).astype(BF)
            plane[k, last[k] + 4 + s] = (slot_sum(k, last[k] + 4 + s) + r2h[k, 1, s].astype(F32)).astype(BF)

    for k, (a1, a2, a3) in enumerate(ORDERS):
        send(plane.at[k, pl.ds(near[k], 8)], r2.at[k, 0], S_B2, R_B2, peer(a2, 1))
        send(plane.at[k, pl.ds(last[k], 8)], r2.at[k, 1], S_B2, R_B2, peer(a2, 3))
    sums_3(EDGE_G)
    sums_5(CONTACT_G)
    sums_6(NODE_G)

    @pl.loop(0, 8)
    def _(s):
        for k in range(COLORS):
            plane[k, own[k] + s] = slot_sum(k, own[k] + s).astype(BF)

    grad = ncot + mm_nt(n_dz, wni[0:L]) + mm_nt(tsum[...], wei[2 * L:]) + mm_nt(own_low, wci[0:L])

    sums_4(EDGE_G)
    sums_6(CONTACT_G)
    arrived(r2, R_B2)
    for k, (a1, a2, a3) in enumerate(ORDERS):
        @pl.loop(0, 8)
        def _(s):
            total = plane[k, coord[a2] * 8 + s].astype(F32)
            for o in range(2):
                total += r2[k, o, s].astype(F32)
            r3src[k, s] = total.astype(BF)

        for off in (1, 2, 3):
            send(
                r3src.at[k, pl.ds(around(a1, off) * 2, 2)], r3.at[k, off - 1],
                S_B3, R_B3, peer(a1, off),
            )
    sums_5(EDGE_G)
    sums_7(NODE_G)
    arrived(rim_in, R_RIM)
    first = spread[RIM:2 * RIM] + rim_in[1].astype(F32) * has_low
    last = spread[NODES:NODES + RIM] + rim_in[0].astype(F32) * has_high
    own_spread = jnp.concatenate([first, spread[2 * RIM:NODES], last], axis=0).astype(BF)
    grad += mm_nt(own_spread, wei[L:2 * L])
    arrived(r3, R_B3)
    cols = []
    for k, (a1, a2, a3) in enumerate(ORDERS):
        halves = [r3src[k, coord[a1] * 2 + b].astype(F32) for b in range(2)]
        for off in (1, 2, 3):
            halves = [halves[b] + r3[k, off - 1, b].astype(F32) for b in range(2)]
        cols.append(jnp.concatenate(halves, axis=0).astype(BF))
    s_rem = jnp.concatenate(cols, axis=1)
    node_grad[...] = (grad + mm_nt(s_rem, wci[L:])).astype(BF)
    write(node_grad, node_grad_hbm, 13)
    sums_6(EDGE_G)
    sums_7(CONTACT_G)
    sums_7(EDGE_G)


    for ref, sem in (
        (meta_v.at[:, pl.ds(1, 3)], S_META), (halo, S_HALO), (rim_in, S_RIM), (hs, S_H), (sbuf, S_F3), (sbuf, S_B1),
        (dz_far.at[:, pl.ds(0, ROWS)], S_B1B), (r2h, S_B2H), (r2, S_B2), (r3, S_B3),
    ):
        sent(ref, sem)
    for n in range(3):
        refs = (g1h[n], g1[n], g2[n], g2[n], g2[n], gout[n].at[:, pl.ds(0, 2)], gout[n].at[:, 0])
        for i, ref in enumerate(refs):
            sent(ref, S_G + 7 * n + i)
    for out in outs:
        out.wait()


def dma(*shape):
    return pltpu.SemaphoreType.DMA(shape)


def vm(shape, dtype):
    return pltpu.VMEM(shape, dtype)


def fused(x, src, ncot, block, host, remote, es, ecot, wei, weo, wni, wno, wci, wco):
    tile = (BLOCK, COLS)
    pieces = [rows // 16 for rows in GROUPS]
    scratch = [
        vm((EDGES, L), BF), vm((EDGES, L), BF), vm((3 * L, L), BF), vm((L, L), BF), vm((3 * L, L), BF),
        vm((L, L), BF), vm((2 * L, L), BF), vm((L, L), BF),
        vm((COLORS, 32) + tile, BF),
        vm((COLORS, 2, ROWS, HALF, COLS), BF),
        [vm((COLORS, 2, CHUNK, HALF, COLS), BF) for _ in range(N_CHUNK)],
        vm((COLORS, 2, ROWS) + tile, BF),
        [vm((COLORS, 3, CHUNK) + tile, BF) for _ in range(N_CHUNK)],
        vm((COLORS, 3, ROWS + 1) + tile, BF), vm((COLORS, ROWS + 1) + tile, BF),
        vm((COLORS, 2, 4) + tile, BF), vm((COLORS, 2, 8) + tile, BF), vm((COLORS, 3, 2) + tile, BF), vm((COLORS, 8) + tile, BF),
        [vm((COLORS, rows, COLS), BF) for rows in GROUPS],
        [vm((COLORS, 2, rows // 8, COLS), BF) for rows in GROUPS],
        [vm((COLORS, 2, rows // 4, COLS), BF) for rows in GROUPS],
        [vm((COLORS, SIDE, piece, COLS), BF) for piece in pieces],
        [vm((COLORS, 3, piece, COLS), BF) for piece in pieces],
        [vm((COLORS, SIDE, piece, COLS), BF) for piece in pieces],
        [vm((COLORS, SIDE, SIDE, piece, COLS), BF) for piece in pieces],
        vm((NODES, L), BF), vm((EDGES, L), BF), vm((NODES, L), BF), vm((EDGES, L), BF),
        vm((2, RIM, L), BF), vm((2, RIM, L), BF), vm((2, RIM, L), BF), vm((NODES + 2 * RIM, L), BF), vm((EDGES, L), BF),
        vm((3, SIDE, ROWS, 128), jnp.int32), pltpu.SMEM((3, SIDE, ROWS, 128), jnp.int32),
        vm((8, 128), jnp.int32), pltpu.SMEM((8, 128), jnp.int32),
        vm((EDGES, L), BF), vm((EDGES, 1), F32), vm((EDGES, L), F32), vm((EDGES, L), BF),
        vm((EDGES, L), BF), vm((EDGES, L), BF), vm((NODES, L), BF),
        vm((ROWS * BLOCK, L), BF), vm((ROWS * BLOCK, L), BF), vm((ROWS * BLOCK, 1), F32), vm((ROWS * BLOCK, L), F32),
        vm((ROWS * BLOCK, L), BF),
        vm((ROWS * BLOCK, L), BF), vm((2, BLOCK, L), F32), vm((2, BLOCK, L), F32), vm((2, BLOCK, L), F32),
        vm((NODES, L), BF), vm((NODES, 3 * L), BF), vm((2, BLOCK, L), BF), vm((NODES, L), BF),
        dma(50), dma(S_G + 21), dma(R_G + 21),
    ]
    here = pl.BlockSpec(memory_space=pltpu.VMEM)
    there = pl.BlockSpec(memory_space=pl.ANY)
    scalars = pl.BlockSpec(memory_space=pltpu.SMEM)
    return pl.pallas_call(
        body,
        out_shape=(
            jax.ShapeDtypeStruct((NODES, L), BF), jax.ShapeDtypeStruct((EDGES, L), BF),
            jax.ShapeDtypeStruct((NODES, L), BF), jax.ShapeDtypeStruct((EDGES, L), BF),
        ) + tuple(jax.ShapeDtypeStruct((COLORS, SIDE, SIDE, piece, COLS), BF) for piece in pieces),
        in_specs=[here] * 3 + [scalars] * 3 + [there] * 8,
        out_specs=[there] * 7,
        scratch_shapes=scratch,
        compiler_params=pltpu.CompilerParams(
            collective_id=0, has_side_effects=True, vmem_limit_bytes=63 * 1024 * 1024
        ),
        name="layer",
    )(x, src, ncot, block, host, remote, es, ecot, wei, weo, wni, wno, wci, wco)


def finish_body(*refs):
    plain_in, packed_in = refs[0:4], refs[4:7]
    plain_out, wide_out = refs[7:11], refs[11:17]
    plain, packed, wide, in_sem, out_sem = refs[17:21], refs[21:24], refs[24:27], refs[27], refs[28]
    chunks = []
    for n, count in enumerate((3, 2, 3)):
        chunks += [(n, i * L, 2 * n + i // count, i % count * L) for i in range(count + 1)]
    loads = [
        pltpu.make_async_copy(packed_in[n].at[:, pl.ds(row, L)], packed[n].at[:, pl.ds(row, L)], in_sem.at[i])
        for i, (n, row, _, _) in enumerate(chunks)
    ]
    loads += [pltpu.make_async_copy(plain_in[i], plain[i], in_sem.at[len(chunks) + i]) for i in range(4)]
    for load in loads:
        load.start()
    stores = []

    def store(src, dst):
        copy = pltpu.make_async_copy(src, dst, out_sem.at[len(stores)])
        copy.start()
        stores.append(copy)

    for i, (n, row, which, there) in enumerate(chunks):
        loads[i].wait()
        for k in range(COLORS):
            wide[n][row:row + L, k * COLS:(k + 1) * COLS] = packed[n][k, row:row + L].astype(F32)
        store(wide[n].at[pl.ds(row, L)], wide_out[which].at[pl.ds(there, L)])
    for i in range(4):
        loads[len(chunks) + i].wait()
        store(plain[i], plain_out[i])
    for copy in stores:
        copy.wait()


def finish(plain, packed):
    packed = [p.reshape(COLORS, rows, COLS) for p, rows in zip(packed, GROUPS)]
    there = pl.BlockSpec(memory_space=pl.ANY)
    shapes = [jax.ShapeDtypeStruct(p.shape, p.dtype) for p in plain]
    shapes += [jax.ShapeDtypeStruct((n * L, L), F32) for n in (3, 1, 2, 1, 3, 1)]
    return pl.pallas_call(
        finish_body,
        out_shape=shapes,
        in_specs=[there] * 7,
        out_specs=[there] * 10,
        scratch_shapes=[
            *[vm(p.shape, p.dtype) for p in plain],
            *[vm((COLORS, rows, COLS), BF) for rows in GROUPS],
            *[vm((rows, L), F32) for rows in GROUPS],
            dma(15), dma(15),
        ],
        compiler_params=pltpu.CompilerParams(vmem_limit_bytes=63 * 1024 * 1024),
        name="finish",
    )(*plain, *packed)


def on_device(
    node_state, edge_state, edge_source, contact_block, contact_host, contact_remote,
    w_edge_in, w_edge_out, w_node_in, w_node_out, w_contact_in, w_contact_out, node_cot, edge_cot,
):
    results = fused(
        node_state, edge_source.reshape(8, 128), node_cot, contact_block, contact_host.reshape(ROWS), contact_remote,
        edge_state, edge_cot, w_edge_in, w_edge_out, w_node_in, w_node_out, w_contact_in, w_contact_out,
    )
    out = finish(results[:4], results[4:])
    node_in, node_last, contact_in, contact_last, edge_in, edge_last = out[4:]
    return tuple(out[:4]) + (edge_in, edge_last, node_in, node_last, contact_in, contact_last)


def solution(mesh):
    rows = P(("rep", "dom"), None)
    flat = P(("rep", "dom"))
    weight = P("rep", None)
    return jax.shard_map(
        on_device,
        mesh=mesh,
        in_specs=(rows, rows, flat, flat, rows, flat) + (weight,) * 6 + (rows, rows),
        out_specs=(rows,) * 4 + (weight,) * 6,
        check_vma=False,
    )
```

```python
import functools

import jax
import jax.numpy as jnp
from jax import lax
from jax.experimental import pallas as pl
from jax.experimental.pallas import tpu as pltpu
from jax.sharding import PartitionSpec as P

L = 384
BLOCK = 128
EPN = 4
RIM = 64
NODES = 256
EDGES = 1024
ROWS = 16
TILE = 256
COLORS = 3
COLS = 128
SIDE = 4
DOM = 64
EPS = 1e-05
BF = jnp.bfloat16
F32 = jnp.float32
MESH = pl.DeviceIdType.MESH

GROUPS = (1536, 1280, 1536)
NODE_G, CONTACT_G, EDGE_G = 0, 1, 2

ORDERS = (("z", "x", "y"), ("x", "y", "z"), ("y", "z", "x"))
STRIDE = {"y": 16, "x": 4, "z": 1}
AXES = ("y", "x", "z")
N_CHUNK = 4
S_META, S_HALO, S_RIM, S_F1, S_F2, S_F2B, S_H, S_F3, S_B1, S_B1B, S_B2H, S_B2, S_B3, S_G = range(14)
R_META, R_HALO, R_RIM, R_F1, R_F2, R_F2B, R_H, R_F3, R_B1, R_B1B, R_B2H, R_B2, R_B3, R_G = (
    0, 1, 2, 3, 6, 9, 10, 14, 18, 26, 27, 28, 29, 30
)
CHUNK = ROWS // N_CHUNK
HALF = BLOCK // 2


def mm(a, b):
    return lax.dot_general(a, b, (((1,), (0,)), ((), ())), preferred_element_type=F32)


def mm_nt(a, b):
    return lax.dot_general(a, b, (((1,), (1,)), ((), ())), preferred_element_type=F32)


def mm_tn(a, b):
    return lax.dot_general(a, b, (((0,), (0,)), ((), ())), preferred_element_type=F32)


def row_mean(v):
    return jnp.sum(v, axis=-1, keepdims=True) * (1.0 / L)


def norm(y):
    center = y - row_mean(y)
    scale = lax.rsqrt(row_mean(center * center) + EPS)
    return center * scale, scale


def norm_back(u, scale, g):
    return scale * (g - row_mean(g) - u * row_mean(g * u))


def silu_parts(z):
    s = jax.nn.sigmoid(z)
    return (z * s).astype(BF), s * (1.0 + z * (1.0 - s))


def body(
    x_ref, src_ref, ncot_ref, block_ref, host_ref, remote_ref,
    es_hbm, ecot_hbm, wei_hbm, weo_hbm, wni_hbm, wno_hbm, wci_hbm, wco_hbm,
    node_out_hbm, edge_out_hbm, node_grad_hbm, edge_grad_hbm, node_hbm, contact_hbm, edge_hbm,
    es, ecot, wei, weo, wni, wno, wci, wco,
    plane, hs, hr, sbuf, rbuf, dz_near, dz_far, r2h, r2, r3, r3src,
    gsend, g1h, g1, g2src, g2, g3, gout, node_out, edge_out, node_grad, edge_grad,
    halo, rim_out, rim_in, xext, onehot,
    meta_v, meta_s, table_v, table_s,
    e_u, e_r, e_h, e_a, e_dy, e_dz, mesh_sum,
    c_x, c_u, c_r, c_h, c_a, c_dy, p_own, csum, dzown, tsum, nbuf, dcon, dmesh,
    local_sem, ss, rs,
):
    me = lax.axis_index("dom")
    coord = {"y": lax.div(me, 16), "x": lax.rem(lax.div(me, 4), 4), "z": lax.rem(me, 4)}

    def around(axis, off):
        return lax.rem(coord[axis] + off, SIDE)

    def peer(axis, off):
        return me + (around(axis, off) - coord[axis]) * STRIDE[axis]

    up, down = lax.rem(me + 1, DOM), lax.rem(me + DOM - 1, DOM)

    def remote(src, dst, to, at, dev):
        return pltpu.make_async_remote_copy(
            src_ref=src, dst_ref=dst, send_sem=ss.at[to], recv_sem=rs.at[at],
            device_id={"dom": dev}, device_id_type=MESH,
        )

    def arrived(ref, sem):
        remote(ref, ref, 0, sem, up).wait_recv()

    def sent(ref, sem):
        remote(ref, ref, sem, 0, up).wait_send()

    def send(*args):
        remote(*args).start()

    loads = [
        pltpu.make_async_copy(src, dst, local_sem.at[i])
        for i, (src, dst) in enumerate(
            [(wci_hbm, wci), (es_hbm, es), (wei_hbm, wei), (weo_hbm, weo), (wco_hbm, wco),
             (wni_hbm, wni), (wno_hbm, wno), (ecot_hbm, ecot)]
        )
    ]
    for load in loads:
        load.start()

    outs = []

    def write(src, dst, i):
        out = pltpu.make_async_copy(src, dst, local_sem.at[i])
        out.start()
        outs.append(out)

    barrier = pltpu.get_barrier_semaphore()
    for axis in AXES:
        for off in (1, 2, 3):
            pl.semaphore_signal(barrier, inc=1, device_id={"dom": peer(axis, off)}, device_id_type=MESH)
    pl.semaphore_signal(barrier, inc=1, device_id={"dom": up}, device_id_type=MESH)
    pl.semaphore_signal(barrier, inc=1, device_id={"dom": down}, device_id_type=MESH)

    x = x_ref[...]
    place = lax.broadcasted_iota(jnp.int32, (1, 128), 1)
    for c in range(ROWS):
        host = host_ref[c]
        at = {"y": lax.div(host, 16), "x": lax.rem(lax.div(host, 4), 4), "z": lax.rem(host, 4)}
        code = [((at[a3] * SIDE + at[a2]) * SIDE + at[a1]) * 2 + remote_ref[c] for a1, a2, a3 in ORDERS]
        line = jnp.where(place < 32, code[0], jnp.where(place < 64, code[1], code[2]))
        line = jnp.where(place < 96, line, block_ref[c])
        for i in range(3):
            meta_v[i, 0, c:c + 1] = line
    for k, (a1, a2, a3) in enumerate(ORDERS):
        own = (coord[a2] * SIDE + coord[a1]) * 2
        for b in range(2):
            plane[k, own + b] = x_ref[b * BLOCK:(b + 1) * BLOCK, k * COLS:(k + 1) * COLS]
    pl.semaphore_wait(barrier, 11)

    for k, (a1, a2, a3) in enumerate(ORDERS):
        own = (coord[a2] * SIDE + coord[a1]) * 2
        for off in (1, 2, 3):
            part = plane.at[k, pl.ds(own, 2)]
            send(part, part, S_F1, R_F1 + k, peer(a1, off))
        part = plane.at[k, pl.ds(own, 2)]
        send(part, part, S_F2, R_F2 + k, peer(a2, 1))
        send(part, part, S_F2, R_F2 + k, peer(a2, 3))
    send(x_ref.at[pl.ds(NODES - RIM, RIM)], halo.at[0], S_HALO, R_HALO, up)
    send(x_ref.at[pl.ds(0, RIM)], halo.at[1], S_HALO, R_HALO, down)
    for i, axis in enumerate(AXES):
        for off in (1, 2, 3):
            send(meta_v.at[i, 0], meta_v.at[i, SIDE - off], S_META, R_META, peer(axis, off))

    lanes = lax.broadcasted_iota(jnp.int32, (BLOCK, L), 1)
    idx = jnp.concatenate([src_ref[...].astype(F32)] * 16, axis=0).T
    for j in range(EDGES // BLOCK):
        col = idx[:, j:j + 1].astype(jnp.int32)
        onehot[j * BLOCK:(j + 1) * BLOCK, :] = jnp.where(col == lanes, 1.0, 0.0).astype(BF)
    for k in range(COLORS):
        for j in range(3):
            dz_near[k, j, ROWS] = jnp.zeros((BLOCK, COLS), BF)
        dz_far[k, ROWS] = jnp.zeros((BLOCK, COLS), BF)
    csum[...] = jnp.zeros_like(csum)
    dzown[...] = jnp.zeros_like(dzown)
    loads[0].wait()
    p_own[...] = mm(x, wci[0:L]).reshape(2, BLOCK, L)

    for k, (a1, a2, a3) in enumerate(ORDERS):
        arrived(plane.at[k, pl.ds(0, 6)], R_F1 + k)
        for off in (1, 2, 3):
            part = plane.at[k, pl.ds((coord[a2] * SIDE + around(a1, off)) * 2, 2)]
            send(part, part, S_F2, R_F2 + k, peer(a2, 1))
            send(part, part, S_F2, R_F2 + k, peer(a2, 3))

    arrived(halo, R_HALO)
    has_low = (me > 0).astype(F32)
    has_high = (me < DOM - 1).astype(F32)
    xext[0:RIM] = (halo[0].astype(F32) * has_low).astype(BF)
    xext[RIM:RIM + NODES] = x
    xext[RIM + NODES:] = (halo[1].astype(F32) * has_high).astype(BF)

    arrived(meta_v.at[:, pl.ds(1, 3)], R_META)
    mine = [coord[a3] * 32 for a1, a2, a3 in ORDERS]
    sought = lax.rem(place, 32) + jnp.where(place < 32, mine[0], jnp.where(place < 64, mine[1], mine[2]))
    wide = lax.broadcasted_iota(jnp.int32, (ROWS, 128), 1)
    for j in range(SIDE):
        asked = [meta_v[AXES.index(a3), j] for a1, a2, a3 in ORDERS]
        asked = jnp.where(wide < 32, asked[0], jnp.where(wide < 64, asked[1], asked[2]))
        first = second = jnp.full((1, 128), ROWS, jnp.int32)
        for c in reversed(range(ROWS)):
            hit = asked[c:c + 1] == sought
            second = jnp.where(hit, first, second)
            first = jnp.where(hit, c, first)
        table_v[2 * j:2 * j + 1] = first
        table_v[2 * j + 1:2 * j + 2] = second
    to_smem = [
        pltpu.make_async_copy(meta_v, meta_s, local_sem.at[8]),
        pltpu.make_async_copy(table_v, table_s, local_sem.at[9]),
    ]
    for copy in to_smem:
        copy.start()

    for load in loads[1:4]:
        load.wait()

    quarter = TILE // EPN
    fan = jnp.where(
        lax.div(lax.broadcasted_iota(jnp.int32, (TILE, quarter), 0), EPN)
        == lax.broadcasted_iota(jnp.int32, (TILE, quarter), 1), 1.0, 0.0,
    ).astype(BF)

    def edge_forward(t):
        rows = pl.ds(pl.multiple_of(t * TILE, TILE), TILE)
        nodes = pl.ds(pl.multiple_of(t * quarter, quarter), quarter)
        state = es[rows]
        src = mm(onehot[rows], xext[...]).astype(BF)
        tgt = mm(fan, x_ref[nodes]).astype(BF)
        z = mm(state, wei[0:L]) + mm(src, wei[L:2 * L]) + mm(tgt, wei[2 * L:])
        a, h = silu_parts(z)
        u, r = norm(mm(a, weo[...]))
        out = (state.astype(F32) + u).astype(BF)
        edge_out[rows] = out
        mesh_sum[nodes] = mm_tn(fan, out).astype(BF)
        e_a[rows] = a
        e_h[rows] = h
        e_u[rows] = u.astype(BF)
        e_r[rows] = r

    for k, (a1, a2, a3) in enumerate(ORDERS):
        arrived(plane.at[k, pl.ds(0, 16)], R_F2 + k)
        part = plane.at[k, pl.ds(around(a2, 3) * 8, 4)]
        send(part, part, S_F2B, R_F2B, peer(a2, 1))
        part = plane.at[k, pl.ds(around(a2, 1) * 8 + 4, 4)]
        send(part, part, S_F2B, R_F2B, peer(a2, 3))

    edge_forward(0)

    for copy in to_smem:
        copy.wait()
    arrived(plane.at[:, pl.ds(0, 8)], R_F2B)

    def request(k, j, c):
        code = meta_s[AXES.index(ORDERS[k][2]), j, c, k * 32]
        return lax.rem(code, 32), lax.div(code, 32)

    for q in range(N_CHUNK):
        for k, (a1, a2, a3) in enumerate(ORDERS):
            for c in range(CHUNK):
                slot, _ = request(k, 2, q * CHUNK + c)
                hs[k, 0, q * CHUNK + c] = plane[k, slot, 0:HALF]
                hs[k, 1, q * CHUNK + c] = plane[k, slot, HALF:]
            part = pl.ds(q * CHUNK, CHUNK)
            send(hs.at[k, 0, part], hr[q].at[k, 0], S_H, R_H + q, peer(a3, 3))
            send(hs.at[k, 1, part], hr[q].at[k, 1], S_H, R_H + q, peer(a3, 1))
    for q in range(N_CHUNK):
        arrived(hr[q], R_H + q)
        for k, (a1, a2, a3) in enumerate(ORDERS):
            for c in range(CHUNK):
                row = q * CHUNK + c
                slot, where = request(k, 3, row)
                own = where == coord[a3]
                sbuf[k, 0, row, 0:HALF] = jnp.where(own, plane[k, slot, 0:HALF], hr[q][k, 0, c])
                sbuf[k, 0, row, HALF:] = plane[k, slot, HALF:]
                slot, where = request(k, 1, row)
                own = where == coord[a3]
                sbuf[k, 1, row, 0:HALF] = plane[k, slot, 0:HALF]
                sbuf[k, 1, row, HALF:] = jnp.where(own, plane[k, slot, HALF:], hr[q][k, 1, c])
            part = pl.ds(q * CHUNK, CHUNK)
            send(sbuf.at[k, 0, part], rbuf[q].at[k, 1], S_F3, R_F3 + q, peer(a3, 3))
            send(sbuf.at[k, 1, part], rbuf[q].at[k, 2], S_F3, R_F3 + q, peer(a3, 1))
        for k in range(COLORS):
            for c in range(CHUNK):
                rbuf[q][k, 0, c] = plane[k, request(k, 0, q * CHUNK + c)[0]]
        if q < 3:
            edge_forward(q + 1)

    loads[4].wait()
    for q in range(N_CHUNK):
        arrived(rbuf[q].at[:, pl.ds(1, 2)], R_F3 + q)

        @pl.loop(0, CHUNK // 2)
        def _(p):
            parts, owns, weights = [], [], []
            for s in range(2):
                c = q * CHUNK + 2 * p + s
                cols = []
                for k, (a1, a2, a3) in enumerate(ORDERS):
                    away = lax.rem(request(k, 0, c)[1] - coord[a3] + SIDE, SIDE)
                    cols.append(jnp.concatenate([
                        rbuf[q][k, lax.div(away + 1, 2), 2 * p + s, 0:HALF],
                        rbuf[q][k, jnp.minimum(away, 2), 2 * p + s, HALF:],
                    ], axis=0))
                parts.append(jnp.concatenate(cols, axis=1))
                block = meta_s[0, 0, c, 96]
                owns.append(p_own[block])
                weights.append(block.astype(F32))
            rows = pl.ds(pl.multiple_of(q * CHUNK * BLOCK + p * TILE, TILE), TILE)
            remote_rows = jnp.concatenate(parts, axis=0)
            c_x[rows] = remote_rows
            z = mm(remote_rows, wci[L:]) + jnp.concatenate(owns, axis=0)
            a, h = silu_parts(z)
            u, r = norm(mm(a, wco[...]))
            c_a[rows] = a
            c_h[rows] = h
            message = u.astype(BF)
            c_u[rows] = message
            c_r[rows] = r
            message = message.astype(F32)
            for s in range(2):
                m = message[s * BLOCK:(s + 1) * BLOCK]
                csum[1] += m * weights[s]
                csum[0] += m * (1.0 - weights[s])

    loads[5].wait()
    loads[6].wait()
    nbuf[:, 0:L] = x
    nbuf[:, L:2 * L] = mesh_sum[...]
    nbuf[:, 2 * L:] = csum[...].reshape(NODES, L).astype(BF)
    a, h = silu_parts(mm(nbuf[...], wni[...]))
    u, r = norm(mm(a, wno[...]))
    node_out[...] = (x.astype(F32) + u).astype(BF)
    write(node_out, node_out_hbm, 10)
    write(edge_out, edge_out_hbm, 11)
    ncot = ncot_ref[...].astype(F32)
    n_dy = norm_back(u, r, ncot).astype(BF)
    n_dz = (mm_nt(n_dy, wno[...]) * h).astype(BF)
    dcon[...] = mm_nt(n_dz, wni[2 * L:]).astype(BF).reshape(2, BLOCK, L)

    @pl.loop(0, ROWS // 2)
    def _(t):
        rows = pl.ds(pl.multiple_of(t * TILE, TILE), TILE)
        blocks = [meta_s[0, 0, 2 * t + s, 96] for s in range(2)]
        g = jnp.concatenate([dcon[b] for b in blocks], axis=0).astype(F32)
        dy = norm_back(c_u[rows].astype(F32), c_r[rows], g).astype(BF)
        c_dy[rows] = dy
        dz = (mm_nt(dy, wco[...]) * c_h[rows]).astype(BF)
        for s in range(2):
            part = dz[s * BLOCK:(s + 1) * BLOCK]
            weight = blocks[s].astype(F32)
            dzown[1] += part.astype(F32) * weight
            dzown[0] += part.astype(F32) * (1.0 - weight)
            for k in range(COLORS):
                dz_near[k, 0, 2 * t + s] = part[:, k * COLS:(k + 1) * COLS]

        @pl.when(lax.rem(t, 2) == 1)
        def _():
            four = pl.ds(2 * t - 2, 4)
            for k, (a1, a2, a3) in enumerate(ORDERS):
                chunk = lax.div(t, 2)
                send(dz_near.at[k, 0, four], dz_near.at[k, 2, four], S_B1, R_B1 + chunk, peer(a3, 1))
                send(dz_near.at[k, 0, four], dz_near.at[k, 1, four], S_B1, R_B1 + chunk, peer(a3, 3))

    def put(group, row, value):
        value = value.astype(BF)
        for k in range(COLORS):
            gsend[group][k, row:row + L] = value[:, k * COLS:(k + 1) * COLS]

    def sums_1(n):
        size = GROUPS[n] // 4
        half = size // 2
        for k, (a1, a2, a3) in enumerate(ORDERS):
            far = around(a3, 2) * size
            send(gsend[n].at[k, pl.ds(far, half)], g1h[n].at[k, 0], S_G + 7 * n, R_G + 7 * n, peer(a3, 1))
            send(gsend[n].at[k, pl.ds(far + half, half)], g1h[n].at[k, 1], S_G + 7 * n, R_G + 7 * n, peer(a3, 3))

    def sums_1b(n):
        size = GROUPS[n] // 4
        half = size // 2
        arrived(g1h[n], R_G + 7 * n)
        for k, (a1, a2, a3) in enumerate(ORDERS):
            for i, off in enumerate((1, 3)):
                start = around(a3, off) * size
                rows = pl.ds(pl.multiple_of(start + i * half, 16), half)
                total = gsend[n][k, rows].astype(F32) + g1h[n][k, i].astype(F32)
                gsend[n][k, rows] = total.astype(BF)
                send(
                    gsend[n].at[k, pl.ds(start, size)], g1[n].at[k, i],
                    S_G + 7 * n + 1, R_G + 7 * n + 1, peer(a3, off),
                )

    def sums_2(n):
        size = GROUPS[n] // 4
        piece = size // 4
        arrived(g1[n], R_G + 7 * n + 1)
        for k, (a1, a2, a3) in enumerate(ORDERS):
            @pl.loop(0, 4)
            def _(t):
                rows = pl.ds(pl.multiple_of(t * piece, 16), piece)
                total = gsend[n][k, pl.ds(pl.multiple_of(coord[a3] * size + t * piece, 16), piece)].astype(F32)
                for o in range(2):
                    total += g1[n][k, o, rows].astype(F32)
                g2src[n][k, t] = total.astype(BF)

            for off in (2, 1, 3):
                send(
                    g2src[n].at[k, around(a2, off)], g2[n].at[k, off - 1],
                    S_G + 7 * n + 2, R_G + 7 * n + 2, peer(a2, off),
                )

    def sums_3(n):
        arrived(g2[n], R_G + 7 * n + 2)
        for k, (a1, a2, a3) in enumerate(ORDERS):
            total = g2src[n][k, coord[a2]].astype(F32)
            for o in range(3):
                total += g2[n][k, o].astype(F32)
            g3[n][k, coord[a1]] = total.astype(BF)
            part = g3[n].at[k, coord[a1]]
            for off in (2, 1, 3):
                send(part, part, S_G + 7 * n + 3, R_G + 7 * n + 3, peer(a1, off))

    def sums_4(n):
        arrived(g2[n], R_G + 7 * n + 3)
        for k, (a1, a2, a3) in enumerate(ORDERS):
            total = g3[n][k, 0].astype(F32)
            for o in range(1, SIDE):
                total += g3[n][k, o].astype(F32)
            gout[n][k, coord[a3], coord[a2]] = total.astype(BF)
            part = gout[n].at[k, coord[a3], coord[a2]]
            for off in (2, 1, 3):
                send(part, part, S_G + 7 * n + 4, R_G + 7 * n + 4, peer(a2, off))

    def sums_5(n):
        arrived(g2[n], R_G + 7 * n + 4)
        for k, (a1, a2, a3) in enumerate(ORDERS):
            part = gout[n].at[k, coord[a3]]
            send(part, part, S_G + 7 * n + 5, R_G + 7 * n + 5, peer(a3, 1))
            send(part, part, S_G + 7 * n + 5, R_G + 7 * n + 5, peer(a3, 3))

    def keep(n, off):
        for k, (a1, a2, a3) in enumerate(ORDERS):
            at = around(a3, off)
            write(gout[n].at[k, at], (node_hbm, contact_hbm, edge_hbm)[n].at[k, at], 14 + (n * 3 + k) * 4 + off)

    def sums_6(n):
        arrived(gout[n].at[:, pl.ds(0, 2)], R_G + 7 * n + 5)
        for k, (a1, a2, a3) in enumerate(ORDERS):
            part = gout[n].at[k, around(a3, 3), pl.ds(0, 2)]
            send(part, part, S_G + 7 * n + 6, R_G + 7 * n + 6, peer(a3, 1))
            part = gout[n].at[k, around(a3, 1), pl.ds(2, 2)]
            send(part, part, S_G + 7 * n + 6, R_G + 7 * n + 6, peer(a3, 3))
        for off in (0, 1, 3):
            keep(n, off)

    def sums_7(n):
        arrived(gout[n].at[:, 0], R_G + 7 * n + 6)
        keep(n, 2)

    for k in range(COLORS):
        gsend[CONTACT_G][k, 3 * L:] = jnp.zeros((GROUPS[CONTACT_G] - 3 * L, COLS), BF)
    dmesh[...] = mm_nt(n_dz, wni[L:2 * L]).astype(BF)
    loads[7].wait()

    def edge_backward(t):
        rows = pl.ds(pl.multiple_of(t * TILE, TILE), TILE)
        nodes = pl.ds(pl.multiple_of(t * quarter, quarter), quarter)
        g = ecot[rows].astype(F32) + mm(fan, dmesh[nodes])
        dy = norm_back(e_u[rows].astype(F32), e_r[rows], g).astype(BF)
        dz = (mm_nt(dy, weo[...]) * e_h[rows]).astype(BF)
        edge_grad[rows] = (g + mm_nt(dz, wei[0:L])).astype(BF)
        tsum[nodes] = mm_tn(fan, dz).astype(BF)
        e_dy[rows] = dy
        e_dz[rows] = dz

    def pass_on(chunk):
        arrived(dz_near.at[:, pl.ds(0, 2), pl.ds(0, 4)], R_B1 + chunk)
        for k, (a1, a2, a3) in enumerate(ORDERS):
            even, odd = pl.ds(4 * chunk, 2), pl.ds(4 * chunk + 2, 2)
            send(dz_near.at[k, 2, even], dz_far.at[k, even], S_B1B, R_B1B, peer(a3, 1))
            send(dz_near.at[k, 1, odd], dz_far.at[k, odd], S_B1B, R_B1B, peer(a3, 3))

    pl.loop(0, 2)(edge_backward)
    pass_on(0)
    pl.loop(2, 4)(edge_backward)
    pass_on(1)
    write(edge_grad, edge_grad_hbm, 12)
    put(NODE_G, 3 * L, mm_tn(a, n_dy))
    for i in range(3):
        put(NODE_G, i * L, mm_tn(nbuf[:, i * L:(i + 1) * L], n_dz))
    sums_1(NODE_G)
    pass_on(2)
    spread = mm_tn(onehot[...], e_dz[...])
    spread_low = spread.astype(BF)
    rim_out[0] = spread_low[0:RIM]
    rim_out[1] = spread_low[RIM + NODES:]
    send(rim_out.at[0], rim_in.at[0], S_RIM, R_RIM, down)
    send(rim_out.at[1], rim_in.at[1], S_RIM, R_RIM, up)
    put(EDGE_G, L, mm_tn(xext[...], spread_low))
    put(EDGE_G, 0, mm_tn(es[...], e_dz[...]))
    put(EDGE_G, 2 * L, mm_tn(x, tsum[...]))
    put(EDGE_G, 3 * L, mm_tn(e_a[...], e_dy[...]))
    sums_1(EDGE_G)
    sums_1b(NODE_G)
    pass_on(3)
    own_low = dzown[...].reshape(NODES, L).astype(BF)
    put(CONTACT_G, 0, mm_tn(x, own_low))
    hidden = jnp.concatenate(
        [dz_near[k, 0, 0:ROWS].reshape(ROWS * BLOCK, COLS) for k in range(COLORS)], axis=1
    )
    put(CONTACT_G, L, mm_tn(c_x[...], hidden))
    put(CONTACT_G, 2 * L, mm_tn(c_a[...], c_dy[...]))
    sums_1(CONTACT_G)
    sums_1b(EDGE_G)
    sums_2(NODE_G)

    sent(plane.at[:, pl.ds(0, 16)], S_F2)
    sent(plane.at[:, pl.ds(0, 8)], S_F2B)
    sent(r3, S_F1)

    @pl.loop(0, 2 * 16)
    def _(s):
        for k in range(COLORS):
            total = jnp.zeros((BLOCK, COLS), F32)
            for at, j in enumerate((0, 1, 3)):
                for i in range(2):
                    total += dz_near[k, at, table_s[2 * j + i, k * 32 + s]].astype(F32)
            plane[k, s] = total.astype(BF)

    sums_1b(CONTACT_G)
    sums_2(EDGE_G)
    sums_3(NODE_G)
    arrived(dz_far.at[:, pl.ds(0, ROWS)], R_B1B)

    def slot_sum(k, s):
        total = plane[k, s].astype(F32)
        for i in range(2):
            total += dz_far[k, table_s[4 + i, k * 32 + s]].astype(F32)
        return total

    own, near, far, last = [[around(a2, off) * 8 for a1, a2, a3 in ORDERS] for off in range(4)]

    @pl.loop(0, 8)
    def _(s):
        for k in range(COLORS):
            plane[k, far[k] + s] = slot_sum(k, far[k] + s).astype(BF)

    for k, (a1, a2, a3) in enumerate(ORDERS):
        send(plane.at[k, pl.ds(far[k], 4)], r2h.at[k, 0], S_B2H, R_B2H, peer(a2, 1))
        send(plane.at[k, pl.ds(far[k] + 4, 4)], r2h.at[k, 1], S_B2H, R_B2H, peer(a2, 3))
    sums_2(CONTACT_G)
    sums_3(EDGE_G)
    sums_4(NODE_G)

    @pl.loop(0, 4)
    def _(s):
        for k in range(COLORS):
            plane[k, near[k] + 4 + s] = slot_sum(k, near[k] + 4 + s).astype(BF)
            plane[k, last[k] + s] = slot_sum(k, last[k] + s).astype(BF)

    arrived(r2h, R_B2H)

    @pl.loop(0, 4)
    def _(s):
        for k in range(COLORS):
            plane[k, near[k] + s] = (slot_sum(k, near[k] + s) + r2h[k, 0, s].astype(F32)).astype(BF)
            plane[k, last[k] + 4 + s] = (slot_sum(k, last[k] + 4 + s) + r2h[k, 1, s].astype(F32)).astype(BF)

    for k, (a1, a2, a3) in enumerate(ORDERS):
        send(plane.at[k, pl.ds(near[k], 8)], r2.at[k, 0], S_B2, R_B2, peer(a2, 1))
        send(plane.at[k, pl.ds(last[k], 8)], r2.at[k, 1], S_B2, R_B2, peer(a2, 3))
    sums_3(CONTACT_G)
    sums_4(EDGE_G)
    sums_5(NODE_G)

    @pl.loop(0, 8)
    def _(s):
        for k in range(COLORS):
            plane[k, own[k] + s] = slot_sum(k, own[k] + s).astype(BF)

    grad = ncot + mm_nt(n_dz, wni[0:L]) + mm_nt(tsum[...], wei[2 * L:]) + mm_nt(own_low, wci[0:L])

    sums_4(CONTACT_G)
    sums_5(EDGE_G)
    sums_6(NODE_G)
    arrived(r2, R_B2)
    for k, (a1, a2, a3) in enumerate(ORDERS):
        @pl.loop(0, 8)
        def _(s):
            total = plane[k, coord[a2] * 8 + s].astype(F32)
            for o in range(2):
                total += r2[k, o, s].astype(F32)
            r3src[k, s] = total.astype(BF)

        for off in (1, 2, 3):
            send(
                r3src.at[k, pl.ds(around(a1, off) * 2, 2)], r3.at[k, off - 1],
                S_B3, R_B3, peer(a1, off),
            )
    sums_5(CONTACT_G)
    sums_6(EDGE_G)
    sums_7(NODE_G)
    arrived(rim_in, R_RIM)
    first = spread[RIM:2 * RIM] + rim_in[1].astype(F32) * has_low
    last = spread[NODES:NODES + RIM] + rim_in[0].astype(F32) * has_high
    own_spread = jnp.concatenate([first, spread[2 * RIM:NODES], last], axis=0).astype(BF)
    grad += mm_nt(own_spread, wei[L:2 * L])
    arrived(r3, R_B3)
    cols = []
    for k, (a1, a2, a3) in enumerate(ORDERS):
        halves = [r3src[k, coord[a1] * 2 + b].astype(F32) for b in range(2)]
        for off in (1, 2, 3):
            halves = [halves[b] + r3[k, off - 1, b].astype(F32) for b in range(2)]
        cols.append(jnp.concatenate(halves, axis=0).astype(BF))
    s_rem = jnp.concatenate(cols, axis=1)
    node_grad[...] = (grad + mm_nt(s_rem, wci[L:])).astype(BF)
    write(node_grad, node_grad_hbm, 13)
    sums_6(CONTACT_G)
    sums_7(EDGE_G)
    sums_7(CONTACT_G)


    for ref, sem in (
        (meta_v.at[:, pl.ds(1, 3)], S_META), (halo, S_HALO), (rim_in, S_RIM), (hs, S_H), (sbuf, S_F3), (sbuf, S_B1),
        (dz_far.at[:, pl.ds(0, ROWS)], S_B1B), (r2h, S_B2H), (r2, S_B2), (r3, S_B3),
    ):
        sent(ref, sem)
    for n in range(3):
        refs = (g1h[n], g1[n], g2[n], g2[n], g2[n], gout[n].at[:, pl.ds(0, 2)], gout[n].at[:, 0])
        for i, ref in enumerate(refs):
            sent(ref, S_G + 7 * n + i)
    for out in outs:
        out.wait()


def dma(*shape):
    return pltpu.SemaphoreType.DMA(shape)


def vm(shape, dtype):
    return pltpu.VMEM(shape, dtype)


def fused(x, src, ncot, block, host, remote, es, ecot, wei, weo, wni, wno, wci, wco):
    tile = (BLOCK, COLS)
    pieces = [rows // 16 for rows in GROUPS]
    scratch = [
        vm((EDGES, L), BF), vm((EDGES, L), BF), vm((3 * L, L), BF), vm((L, L), BF), vm((3 * L, L), BF),
        vm((L, L), BF), vm((2 * L, L), BF), vm((L, L), BF),
        vm((COLORS, 32) + tile, BF),
        vm((COLORS, 2, ROWS, HALF, COLS), BF),
        [vm((COLORS, 2, CHUNK, HALF, COLS), BF) for _ in range(N_CHUNK)],
        vm((COLORS, 2, ROWS) + tile, BF),
        [vm((COLORS, 3, CHUNK) + tile, BF) for _ in range(N_CHUNK)],
        vm((COLORS, 3, ROWS + 1) + tile, BF), vm((COLORS, ROWS + 1) + tile, BF),
        vm((COLORS, 2, 4) + tile, BF), vm((COLORS, 2, 8) + tile, BF), vm((COLORS, 3, 2) + tile, BF), vm((COLORS, 8) + tile, BF),
        [vm((COLORS, rows, COLS), BF) for rows in GROUPS],
        [vm((COLORS, 2, rows // 8, COLS), BF) for rows in GROUPS],
        [vm((COLORS, 2, rows // 4, COLS), BF) for rows in GROUPS],
        [vm((COLORS, SIDE, piece, COLS), BF) for piece in pieces],
        [vm((COLORS, 3, piece, COLS), BF) for piece in pieces],
        [vm((COLORS, SIDE, piece, COLS), BF) for piece in pieces],
        [vm((COLORS, SIDE, SIDE, piece, COLS), BF) for piece in pieces],
        vm((NODES, L), BF), vm((EDGES, L), BF), vm((NODES, L), BF), vm((EDGES, L), BF),
        vm((2, RIM, L), BF), vm((2, RIM, L), BF), vm((2, RIM, L), BF), vm((NODES + 2 * RIM, L), BF), vm((EDGES, L), BF),
        vm((3, SIDE, ROWS, 128), jnp.int32), pltpu.SMEM((3, SIDE, ROWS, 128), jnp.int32),
        vm((8, 128), jnp.int32), pltpu.SMEM((8, 128), jnp.int32),
        vm((EDGES, L), BF), vm((EDGES, 1), F32), vm((EDGES, L), F32), vm((EDGES, L), BF),
        vm((EDGES, L), BF), vm((EDGES, L), BF), vm((NODES, L), BF),
        vm((ROWS * BLOCK, L), BF), vm((ROWS * BLOCK, L), BF), vm((ROWS * BLOCK, 1), F32), vm((ROWS * BLOCK, L), F32),
        vm((ROWS * BLOCK, L), BF),
        vm((ROWS * BLOCK, L), BF), vm((2, BLOCK, L), F32), vm((2, BLOCK, L), F32), vm((2, BLOCK, L), F32),
        vm((NODES, L), BF), vm((NODES, 3 * L), BF), vm((2, BLOCK, L), BF), vm((NODES, L), BF),
        dma(50), dma(S_G + 21), dma(R_G + 21),
    ]
    here = pl.BlockSpec(memory_space=pltpu.VMEM)
    there = pl.BlockSpec(memory_space=pl.ANY)
    scalars = pl.BlockSpec(memory_space=pltpu.SMEM)
    return pl.pallas_call(
        body,
        out_shape=(
            jax.ShapeDtypeStruct((NODES, L), BF), jax.ShapeDtypeStruct((EDGES, L), BF),
            jax.ShapeDtypeStruct((NODES, L), BF), jax.ShapeDtypeStruct((EDGES, L), BF),
        ) + tuple(jax.ShapeDtypeStruct((COLORS, SIDE, SIDE, piece, COLS), BF) for piece in pieces),
        in_specs=[here] * 3 + [scalars] * 3 + [there] * 8,
        out_specs=[there] * 7,
        scratch_shapes=scratch,
        compiler_params=pltpu.CompilerParams(
            collective_id=0, has_side_effects=True, vmem_limit_bytes=63 * 1024 * 1024
        ),
        name="layer",
    )(x, src, ncot, block, host, remote, es, ecot, wei, weo, wni, wno, wci, wco)


def finish_body(*refs):
    plain_in, packed_in = refs[0:4], refs[4:7]
    plain_out, wide_out = refs[7:11], refs[11:17]
    plain, packed, wide, in_sem, out_sem = refs[17:21], refs[21:24], refs[24:27], refs[27], refs[28]
    chunks = []
    for n, count in enumerate((3, 2, 3)):
        chunks += [(n, i * L, 2 * n + i // count, i % count * L) for i in range(count + 1)]
    loads = [
        pltpu.make_async_copy(packed_in[n].at[:, pl.ds(row, L)], packed[n].at[:, pl.ds(row, L)], in_sem.at[i])
        for i, (n, row, _, _) in enumerate(chunks)
    ]
    loads += [pltpu.make_async_copy(plain_in[i], plain[i], in_sem.at[len(chunks) + i]) for i in range(4)]
    for load in loads:
        load.start()
    stores = []

    def store(src, dst):
        copy = pltpu.make_async_copy(src, dst, out_sem.at[len(stores)])
        copy.start()
        stores.append(copy)

    for i, (n, row, which, there) in enumerate(chunks):
        loads[i].wait()
        for k in range(COLORS):
            wide[n][row:row + L, k * COLS:(k + 1) * COLS] = packed[n][k, row:row + L].astype(F32)
        store(wide[n].at[pl.ds(row, L)], wide_out[which].at[pl.ds(there, L)])
    for i in range(4):
        loads[len(chunks) + i].wait()
        store(plain[i], plain_out[i])
    for copy in stores:
        copy.wait()


def finish(plain, packed):
    packed = [p.reshape(COLORS, rows, COLS) for p, rows in zip(packed, GROUPS)]
    there = pl.BlockSpec(memory_space=pl.ANY)
    shapes = [jax.ShapeDtypeStruct(p.shape, p.dtype) for p in plain]
    shapes += [jax.ShapeDtypeStruct((n * L, L), F32) for n in (3, 1, 2, 1, 3, 1)]
    return pl.pallas_call(
        finish_body,
        out_shape=shapes,
        in_specs=[there] * 7,
        out_specs=[there] * 10,
        scratch_shapes=[
            *[vm(p.shape, p.dtype) for p in plain],
            *[vm((COLORS, rows, COLS), BF) for rows in GROUPS],
            *[vm((rows, L), F32) for rows in GROUPS],
            dma(15), dma(15),
        ],
        compiler_params=pltpu.CompilerParams(vmem_limit_bytes=63 * 1024 * 1024),
        name="finish",
    )(*plain, *packed)


def on_device(
    node_state, edge_state, edge_source, contact_block, contact_host, contact_remote,
    w_edge_in, w_edge_out, w_node_in, w_node_out, w_contact_in, w_contact_out, node_cot, edge_cot,
):
    results = fused(
        node_state, edge_source.reshape(8, 128), node_cot, contact_block, contact_host.reshape(ROWS), contact_remote,
        edge_state, edge_cot, w_edge_in, w_edge_out, w_node_in, w_node_out, w_contact_in, w_contact_out,
    )
    out = finish(results[:4], results[4:])
    node_in, node_last, contact_in, contact_last, edge_in, edge_last = out[4:]
    return tuple(out[:4]) + (edge_in, edge_last, node_in, node_last, contact_in, contact_last)


def solution(mesh):
    rows = P(("rep", "dom"), None)
    flat = P(("rep", "dom"))
    weight = P("rep", None)
    return jax.shard_map(
        on_device,
        mesh=mesh,
        in_specs=(rows, rows, flat, flat, rows, flat) + (weight,) * 6 + (rows, rows),
        out_specs=(rows,) * 4 + (weight,) * 6,
        check_vma=False,
    )
```

```python
import functools

import jax
import jax.numpy as jnp
from jax import lax
from jax.experimental import pallas as pl
from jax.experimental.pallas import tpu as pltpu
from jax.sharding import PartitionSpec as P

L = 384
BLOCK = 128
EPN = 4
RIM = 64
NODES = 256
EDGES = 1024
ROWS = 16
TILE = 256
COLORS = 3
COLS = 128
SIDE = 4
DOM = 64
EPS = 1e-05
BF = jnp.bfloat16
F32 = jnp.float32
MESH = pl.DeviceIdType.MESH

GROUPS = (1536, 1280, 1536)
NODE_G, CONTACT_G, EDGE_G = 0, 1, 2

ORDERS = (("z", "x", "y"), ("x", "y", "z"), ("y", "z", "x"))
STRIDE = {"y": 16, "x": 4, "z": 1}
AXES = ("y", "x", "z")
N_CHUNK = 4
S_META, S_HALO, S_RIM, S_F1, S_F2, S_F2B, S_H, S_F3, S_B1, S_B1B, S_B2H, S_B2, S_B3, S_G = range(14)
R_META, R_HALO, R_RIM, R_F1, R_F2, R_F2B, R_H, R_F3, R_B1, R_B1B, R_B2H, R_B2, R_B3, R_G = (
    0, 1, 2, 3, 6, 9, 10, 14, 18, 26, 27, 28, 29, 30
)
CHUNK = ROWS // N_CHUNK
HALF = BLOCK // 2


def mm(a, b):
    return lax.dot_general(a, b, (((1,), (0,)), ((), ())), preferred_element_type=F32)


def mm_nt(a, b):
    return lax.dot_general(a, b, (((1,), (1,)), ((), ())), preferred_element_type=F32)


def mm_tn(a, b):
    return lax.dot_general(a, b, (((0,), (0,)), ((), ())), preferred_element_type=F32)


def row_mean(v):
    return jnp.sum(v, axis=-1, keepdims=True) * (1.0 / L)


def norm(y):
    center = y - row_mean(y)
    scale = lax.rsqrt(row_mean(center * center) + EPS)
    return center * scale, scale


def norm_back(u, scale, g):
    return scale * (g - row_mean(g) - u * row_mean(g * u))


def silu_parts(z):
    s = jax.nn.sigmoid(z)
    return (z * s).astype(BF), s * (1.0 + z * (1.0 - s))


def body(
    x_hbm, src_hbm, ncot_hbm, block_hbm, host_hbm, remote_hbm,
    es_hbm, ecot_hbm, wei_hbm, weo_hbm, wni_hbm, wno_hbm, wci_hbm, wco_hbm,
    node_out_hbm, edge_out_hbm, node_grad_hbm, edge_grad_hbm, node_hbm, contact_hbm, edge_hbm,
    es, ecot, wei, weo, wni, wno, wci, wco,
    plane, hs, hr, sbuf, rbuf, dz_near, dz_far, r2h, r2, r3, r3src,
    gsend, g1h, g1, g2src, g2, g3, gout, node_out, edge_out, node_grad, edge_grad,
    halo, rim_out, rim_in, xext, onehot,
    meta_v, meta_s, table_v, table_s,
    e_u, e_r, e_h, e_a, e_dy, e_dz, mesh_sum,
    c_x, c_u, c_r, c_h, c_a, c_dy, p_own, csum, dzown, tsum, nbuf, dcon, dmesh,
    local_sem, ss, rs,
    x_ref, src_ref, ncot_ref, block_ref, host_ref, remote_ref,
):
    me = lax.axis_index("dom")
    coord = {"y": lax.div(me, 16), "x": lax.rem(lax.div(me, 4), 4), "z": lax.rem(me, 4)}

    def around(axis, off):
        return lax.rem(coord[axis] + off, SIDE)

    def peer(axis, off):
        return me + (around(axis, off) - coord[axis]) * STRIDE[axis]

    up, down = lax.rem(me + 1, DOM), lax.rem(me + DOM - 1, DOM)

    def remote(src, dst, to, at, dev):
        return pltpu.make_async_remote_copy(
            src_ref=src, dst_ref=dst, send_sem=ss.at[to], recv_sem=rs.at[at],
            device_id={"dom": dev}, device_id_type=MESH,
        )

    def arrived(ref, sem):
        remote(ref, ref, 0, sem, up).wait_recv()

    def sent(ref, sem):
        remote(ref, ref, sem, 0, up).wait_send()

    def send(*args):
        remote(*args).start()

    barrier = pltpu.get_barrier_semaphore()
    for axis in AXES:
        for off in (1, 2, 3):
            pl.semaphore_signal(barrier, inc=1, device_id={"dom": peer(axis, off)}, device_id_type=MESH)
    pl.semaphore_signal(barrier, inc=1, device_id={"dom": up}, device_id_type=MESH)
    pl.semaphore_signal(barrier, inc=1, device_id={"dom": down}, device_id_type=MESH)

    early = [
        pltpu.make_async_copy(src, dst, local_sem.at[50 + i])
        for i, (src, dst) in enumerate(
            [(x_hbm, x_ref), (block_hbm, block_ref), (host_hbm, host_ref), (remote_hbm, remote_ref),
             (src_hbm, src_ref), (ncot_hbm, ncot_ref)]
        )
    ]
    for load in early:
        load.start()
    loads = [
        pltpu.make_async_copy(src, dst, local_sem.at[i])
        for i, (src, dst) in enumerate(
            [(wci_hbm, wci), (es_hbm, es), (wei_hbm, wei), (weo_hbm, weo), (wco_hbm, wco),
             (wni_hbm, wni), (wno_hbm, wno), (ecot_hbm, ecot)]
        )
    ]
    for load in loads:
        load.start()

    outs = []

    def write(src, dst, i):
        out = pltpu.make_async_copy(src, dst, local_sem.at[i])
        out.start()
        outs.append(out)

    for load in early[0:4]:
        load.wait()
    x = x_ref[...]
    place = lax.broadcasted_iota(jnp.int32, (1, 128), 1)
    for c in range(ROWS):
        host = host_ref[c]
        at = {"y": lax.div(host, 16), "x": lax.rem(lax.div(host, 4), 4), "z": lax.rem(host, 4)}
        code = [((at[a3] * SIDE + at[a2]) * SIDE + at[a1]) * 2 + remote_ref[c] for a1, a2, a3 in ORDERS]
        line = jnp.where(place < 32, code[0], jnp.where(place < 64, code[1], code[2]))
        line = jnp.where(place < 96, line, block_ref[c])
        for i in range(3):
            meta_v[i, 0, c:c + 1] = line
    for k, (a1, a2, a3) in enumerate(ORDERS):
        own = (coord[a2] * SIDE + coord[a1]) * 2
        for b in range(2):
            plane[k, own + b] = x_ref[b * BLOCK:(b + 1) * BLOCK, k * COLS:(k + 1) * COLS]
    pl.semaphore_wait(barrier, 11)

    for k, (a1, a2, a3) in enumerate(ORDERS):
        own = (coord[a2] * SIDE + coord[a1]) * 2
        for off in (1, 2, 3):
            part = plane.at[k, pl.ds(own, 2)]
            send(part, part, S_F1, R_F1 + k, peer(a1, off))
        part = plane.at[k, pl.ds(own, 2)]
        send(part, part, S_F2, R_F2 + k, peer(a2, 1))
        send(part, part, S_F2, R_F2 + k, peer(a2, 3))
    send(x_ref.at[pl.ds(NODES - RIM, RIM)], halo.at[0], S_HALO, R_HALO, up)
    send(x_ref.at[pl.ds(0, RIM)], halo.at[1], S_HALO, R_HALO, down)
    for i, axis in enumerate(AXES):
        for off in (1, 2, 3):
            send(meta_v.at[i, 0], meta_v.at[i, SIDE - off], S_META, R_META, peer(axis, off))

    lanes = lax.broadcasted_iota(jnp.int32, (BLOCK, L), 1)
    early[4].wait()
    idx = jnp.concatenate([src_ref[...].astype(F32)] * 16, axis=0).T
    for j in range(EDGES // BLOCK):
        col = idx[:, j:j + 1].astype(jnp.int32)
        onehot[j * BLOCK:(j + 1) * BLOCK, :] = jnp.where(col == lanes, 1.0, 0.0).astype(BF)
    for k in range(COLORS):
        for j in range(3):
            dz_near[k, j, ROWS] = jnp.zeros((BLOCK, COLS), BF)
        dz_far[k, ROWS] = jnp.zeros((BLOCK, COLS), BF)
    csum[...] = jnp.zeros_like(csum)
    dzown[...] = jnp.zeros_like(dzown)
    loads[0].wait()
    p_own[...] = mm(x, wci[0:L]).reshape(2, BLOCK, L)

    for k, (a1, a2, a3) in enumerate(ORDERS):
        arrived(plane.at[k, pl.ds(0, 6)], R_F1 + k)
        for off in (1, 2, 3):
            part = plane.at[k, pl.ds((coord[a2] * SIDE + around(a1, off)) * 2, 2)]
            send(part, part, S_F2, R_F2 + k, peer(a2, 1))
            send(part, part, S_F2, R_F2 + k, peer(a2, 3))

    arrived(halo, R_HALO)
    has_low = (me > 0).astype(F32)
    has_high = (me < DOM - 1).astype(F32)
    xext[0:RIM] = (halo[0].astype(F32) * has_low).astype(BF)
    xext[RIM:RIM + NODES] = x
    xext[RIM + NODES:] = (halo[1].astype(F32) * has_high).astype(BF)

    arrived(meta_v.at[:, pl.ds(1, 3)], R_META)
    mine = [coord[a3] * 32 for a1, a2, a3 in ORDERS]
    sought = lax.rem(place, 32) + jnp.where(place < 32, mine[0], jnp.where(place < 64, mine[1], mine[2]))
    wide = lax.broadcasted_iota(jnp.int32, (ROWS, 128), 1)
    for j in range(SIDE):
        asked = [meta_v[AXES.index(a3), j] for a1, a2, a3 in ORDERS]
        asked = jnp.where(wide < 32, asked[0], jnp.where(wide < 64, asked[1], asked[2]))
        first = second = jnp.full((1, 128), ROWS, jnp.int32)
        for c in reversed(range(ROWS)):
            hit = asked[c:c + 1] == sought
            second = jnp.where(hit, first, second)
            first = jnp.where(hit, c, first)
        table_v[2 * j:2 * j + 1] = first
        table_v[2 * j + 1:2 * j + 2] = second
    to_smem = [
        pltpu.make_async_copy(meta_v, meta_s, local_sem.at[8]),
        pltpu.make_async_copy(table_v, table_s, local_sem.at[9]),
    ]
    for copy in to_smem:
        copy.start()

    for load in loads[1:4]:
        load.wait()

    quarter = TILE // EPN
    fan = jnp.where(
        lax.div(lax.broadcasted_iota(jnp.int32, (TILE, quarter), 0), EPN)
        == lax.broadcasted_iota(jnp.int32, (TILE, quarter), 1), 1.0, 0.0,
    ).astype(BF)

    def edge_forward(t):
        rows = pl.ds(pl.multiple_of(t * TILE, TILE), TILE)
        nodes = pl.ds(pl.multiple_of(t * quarter, quarter), quarter)
        state = es[rows]
        src = mm(onehot[rows], xext[...]).astype(BF)
        tgt = mm(fan, x_ref[nodes]).astype(BF)
        z = mm(state, wei[0:L]) + mm(src, wei[L:2 * L]) + mm(tgt, wei[2 * L:])
        a, h = silu_parts(z)
        u, r = norm(mm(a, weo[...]))
        out = (state.astype(F32) + u).astype(BF)
        edge_out[rows] = out
        mesh_sum[nodes] = mm_tn(fan, out).astype(BF)
        e_a[rows] = a
        e_h[rows] = h
        e_u[rows] = u.astype(BF)
        e_r[rows] = r

    for k, (a1, a2, a3) in enumerate(ORDERS):
        arrived(plane.at[k, pl.ds(0, 16)], R_F2 + k)
        part = plane.at[k, pl.ds(around(a2, 3) * 8, 4)]
        send(part, part, S_F2B, R_F2B, peer(a2, 1))
        part = plane.at[k, pl.ds(around(a2, 1) * 8 + 4, 4)]
        send(part, part, S_F2B, R_F2B, peer(a2, 3))

    edge_forward(0)

    for copy in to_smem:
        copy.wait()
    arrived(plane.at[:, pl.ds(0, 8)], R_F2B)

    def request(k, j, c):
        code = meta_s[AXES.index(ORDERS[k][2]), j, c, k * 32]
        return lax.rem(code, 32), lax.div(code, 32)

    for q in range(N_CHUNK):
        for k, (a1, a2, a3) in enumerate(ORDERS):
            for c in range(CHUNK):
                slot, _ = request(k, 2, q * CHUNK + c)
                hs[k, 0, q * CHUNK + c] = plane[k, slot, 0:HALF]
                hs[k, 1, q * CHUNK + c] = plane[k, slot, HALF:]
            part = pl.ds(q * CHUNK, CHUNK)
            send(hs.at[k, 0, part], hr[q].at[k, 0], S_H, R_H + q, peer(a3, 3))
            send(hs.at[k, 1, part], hr[q].at[k, 1], S_H, R_H + q, peer(a3, 1))
    for q in range(N_CHUNK):
        arrived(hr[q], R_H + q)
        for k, (a1, a2, a3) in enumerate(ORDERS):
            for c in range(CHUNK):
                row = q * CHUNK + c
                slot, where = request(k, 3, row)
                own = where == coord[a3]
                sbuf[k, 0, row, 0:HALF] = jnp.where(own, plane[k, slot, 0:HALF], hr[q][k, 0, c])
                sbuf[k, 0, row, HALF:] = plane[k, slot, HALF:]
                slot, where = request(k, 1, row)
                own = where == coord[a3]
                sbuf[k, 1, row, 0:HALF] = plane[k, slot, 0:HALF]
                sbuf[k, 1, row, HALF:] = jnp.where(own, plane[k, slot, HALF:], hr[q][k, 1, c])
            part = pl.ds(q * CHUNK, CHUNK)
            send(sbuf.at[k, 0, part], rbuf[q].at[k, 1], S_F3, R_F3 + q, peer(a3, 3))
            send(sbuf.at[k, 1, part], rbuf[q].at[k, 2], S_F3, R_F3 + q, peer(a3, 1))
        for k in range(COLORS):
            for c in range(CHUNK):
                rbuf[q][k, 0, c] = plane[k, request(k, 0, q * CHUNK + c)[0]]
        if q < 3:
            edge_forward(q + 1)

    loads[4].wait()
    for q in range(N_CHUNK):
        arrived(rbuf[q].at[:, pl.ds(1, 2)], R_F3 + q)

        @pl.loop(0, CHUNK // 2)
        def _(p):
            parts, owns, weights = [], [], []
            for s in range(2):
                c = q * CHUNK + 2 * p + s
                cols = []
                for k, (a1, a2, a3) in enumerate(ORDERS):
                    away = lax.rem(request(k, 0, c)[1] - coord[a3] + SIDE, SIDE)
                    cols.append(jnp.concatenate([
                        rbuf[q][k, lax.div(away + 1, 2), 2 * p + s, 0:HALF],
                        rbuf[q][k, jnp.minimum(away, 2), 2 * p + s, HALF:],
                    ], axis=0))
                parts.append(jnp.concatenate(cols, axis=1))
                block = meta_s[0, 0, c, 96]
                owns.append(p_own[block])
                weights.append(block.astype(F32))
            rows = pl.ds(pl.multiple_of(q * CHUNK * BLOCK + p * TILE, TILE), TILE)
            remote_rows = jnp.concatenate(parts, axis=0)
            c_x[rows] = remote_rows
            z = mm(remote_rows, wci[L:]) + jnp.concatenate(owns, axis=0)
            a, h = silu_parts(z)
            u, r = norm(mm(a, wco[...]))
            c_a[rows] = a
            c_h[rows] = h
            message = u.astype(BF)
            c_u[rows] = message
            c_r[rows] = r
            message = message.astype(F32)
            for s in range(2):
                m = message[s * BLOCK:(s + 1) * BLOCK]
                csum[1] += m * weights[s]
                csum[0] += m * (1.0 - weights[s])

    loads[5].wait()
    loads[6].wait()
    nbuf[:, 0:L] = x
    nbuf[:, L:2 * L] = mesh_sum[...]
    nbuf[:, 2 * L:] = csum[...].reshape(NODES, L).astype(BF)
    a, h = silu_parts(mm(nbuf[...], wni[...]))
    u, r = norm(mm(a, wno[...]))
    node_out[...] = (x.astype(F32) + u).astype(BF)
    write(node_out, node_out_hbm, 10)
    write(edge_out, edge_out_hbm, 11)
    early[5].wait()
    ncot = ncot_ref[...].astype(F32)
    n_dy = norm_back(u, r, ncot).astype(BF)
    n_dz = (mm_nt(n_dy, wno[...]) * h).astype(BF)
    dcon[...] = mm_nt(n_dz, wni[2 * L:]).astype(BF).reshape(2, BLOCK, L)

    @pl.loop(0, ROWS // 2)
    def _(t):
        rows = pl.ds(pl.multiple_of(t * TILE, TILE), TILE)
        blocks = [meta_s[0, 0, 2 * t + s, 96] for s in range(2)]
        g = jnp.concatenate([dcon[b] for b in blocks], axis=0).astype(F32)
        dy = norm_back(c_u[rows].astype(F32), c_r[rows], g).astype(BF)
        c_dy[rows] = dy
        dz = (mm_nt(dy, wco[...]) * c_h[rows]).astype(BF)
        for s in range(2):
            part = dz[s * BLOCK:(s + 1) * BLOCK]
            weight = blocks[s].astype(F32)
            dzown[1] += part.astype(F32) * weight
            dzown[0] += part.astype(F32) * (1.0 - weight)
            for k in range(COLORS):
                dz_near[k, 0, 2 * t + s] = part[:, k * COLS:(k + 1) * COLS]

        @pl.when(lax.rem(t, 2) == 1)
        def _():
            four = pl.ds(2 * t - 2, 4)
            for k, (a1, a2, a3) in enumerate(ORDERS):
                chunk = lax.div(t, 2)
                send(dz_near.at[k, 0, four], dz_near.at[k, 2, four], S_B1, R_B1 + chunk, peer(a3, 1))
                send(dz_near.at[k, 0, four], dz_near.at[k, 1, four], S_B1, R_B1 + chunk, peer(a3, 3))

    def put(group, row, value):
        value = value.astype(BF)
        for k in range(COLORS):
            gsend[group][k, row:row + L] = value[:, k * COLS:(k + 1) * COLS]

    def sums_1(n):
        size = GROUPS[n] // 4
        half = size // 2
        for k, (a1, a2, a3) in enumerate(ORDERS):
            far = around(a3, 2) * size
            send(gsend[n].at[k, pl.ds(far, half)], g1h[n].at[k, 0], S_G + 7 * n, R_G + 7 * n, peer(a3, 1))
            send(gsend[n].at[k, pl.ds(far + half, half)], g1h[n].at[k, 1], S_G + 7 * n, R_G + 7 * n, peer(a3, 3))

    def sums_1b(n):
        size = GROUPS[n] // 4
        half = size // 2
        arrived(g1h[n], R_G + 7 * n)
        for k, (a1, a2, a3) in enumerate(ORDERS):
            for i, off in enumerate((1, 3)):
                start = around(a3, off) * size
                rows = pl.ds(pl.multiple_of(start + i * half, 16), half)
                total = gsend[n][k, rows].astype(F32) + g1h[n][k, i].astype(F32)
                gsend[n][k, rows] = total.astype(BF)
                send(
                    gsend[n].at[k, pl.ds(start, size)], g1[n].at[k, i],
                    S_G + 7 * n + 1, R_G + 7 * n + 1, peer(a3, off),
                )

    def sums_2(n):
        size = GROUPS[n] // 4
        piece = size // 4
        arrived(g1[n], R_G + 7 * n + 1)
        for k, (a1, a2, a3) in enumerate(ORDERS):
            @pl.loop(0, 4)
            def _(t):
                rows = pl.ds(pl.multiple_of(t * piece, 16), piece)
                total = gsend[n][k, pl.ds(pl.multiple_of(coord[a3] * size + t * piece, 16), piece)].astype(F32)
                for o in range(2):
                    total += g1[n][k, o, rows].astype(F32)
                g2src[n][k, t] = total.astype(BF)

            for off in (2, 1, 3):
                send(
                    g2src[n].at[k, around(a2, off)], g2[n].at[k, off - 1],
                    S_G + 7 * n + 2, R_G + 7 * n + 2, peer(a2, off),
                )

    def sums_3(n):
        arrived(g2[n], R_G + 7 * n + 2)
        for k, (a1, a2, a3) in enumerate(ORDERS):
            total = g2src[n][k, coord[a2]].astype(F32)
            for o in range(3):
                total += g2[n][k, o].astype(F32)
            g3[n][k, coord[a1]] = total.astype(BF)
            part = g3[n].at[k, coord[a1]]
            for off in (2, 1, 3):
                send(part, part, S_G + 7 * n + 3, R_G + 7 * n + 3, peer(a1, off))

    def sums_4(n):
        arrived(g2[n], R_G + 7 * n + 3)
        for k, (a1, a2, a3) in enumerate(ORDERS):
            total = g3[n][k, 0].astype(F32)
            for o in range(1, SIDE):
                total += g3[n][k, o].astype(F32)
            gout[n][k, coord[a3], coord[a2]] = total.astype(BF)
            part = gout[n].at[k, coord[a3], coord[a2]]
            for off in (2, 1, 3):
                send(part, part, S_G + 7 * n + 4, R_G + 7 * n + 4, peer(a2, off))

    def sums_5(n):
        arrived(g2[n], R_G + 7 * n + 4)
        for k, (a1, a2, a3) in enumerate(ORDERS):
            part = gout[n].at[k, coord[a3]]
            send(part, part, S_G + 7 * n + 5, R_G + 7 * n + 5, peer(a3, 1))
            send(part, part, S_G + 7 * n + 5, R_G + 7 * n + 5, peer(a3, 3))

    def keep(n, off):
        for k, (a1, a2, a3) in enumerate(ORDERS):
            at = around(a3, off)
            write(gout[n].at[k, at], (node_hbm, contact_hbm, edge_hbm)[n].at[k, at], 14 + (n * 3 + k) * 4 + off)

    def sums_6(n):
        arrived(gout[n].at[:, pl.ds(0, 2)], R_G + 7 * n + 5)
        for k, (a1, a2, a3) in enumerate(ORDERS):
            part = gout[n].at[k, around(a3, 3), pl.ds(0, 2)]
            send(part, part, S_G + 7 * n + 6, R_G + 7 * n + 6, peer(a3, 1))
            part = gout[n].at[k, around(a3, 1), pl.ds(2, 2)]
            send(part, part, S_G + 7 * n + 6, R_G + 7 * n + 6, peer(a3, 3))
        for off in (0, 1, 3):
            keep(n, off)

    def sums_7(n):
        arrived(gout[n].at[:, 0], R_G + 7 * n + 6)
        keep(n, 2)

    for k in range(COLORS):
        gsend[CONTACT_G][k, 3 * L:] = jnp.zeros((GROUPS[CONTACT_G] - 3 * L, COLS), BF)
    dmesh[...] = mm_nt(n_dz, wni[L:2 * L]).astype(BF)
    loads[7].wait()

    def edge_backward(t):
        rows = pl.ds(pl.multiple_of(t * TILE, TILE), TILE)
        nodes = pl.ds(pl.multiple_of(t * quarter, quarter), quarter)
        g = ecot[rows].astype(F32) + mm(fan, dmesh[nodes])
        dy = norm_back(e_u[rows].astype(F32), e_r[rows], g).astype(BF)
        dz = (mm_nt(dy, weo[...]) * e_h[rows]).astype(BF)
        edge_grad[rows] = (g + mm_nt(dz, wei[0:L])).astype(BF)
        tsum[nodes] = mm_tn(fan, dz).astype(BF)
        e_dy[rows] = dy
        e_dz[rows] = dz

    def pass_on(chunk):
        arrived(dz_near.at[:, pl.ds(0, 2), pl.ds(0, 4)], R_B1 + chunk)
        for k, (a1, a2, a3) in enumerate(ORDERS):
            even, odd = pl.ds(4 * chunk, 2), pl.ds(4 * chunk + 2, 2)
            send(dz_near.at[k, 2, even], dz_far.at[k, even], S_B1B, R_B1B, peer(a3, 1))
            send(dz_near.at[k, 1, odd], dz_far.at[k, odd], S_B1B, R_B1B, peer(a3, 3))

    pl.loop(0, 2)(edge_backward)
    pass_on(0)
    pl.loop(2, 4)(edge_backward)
    pass_on(1)
    write(edge_grad, edge_grad_hbm, 12)
    put(NODE_G, 3 * L, mm_tn(a, n_dy))
    for i in range(3):
        put(NODE_G, i * L, mm_tn(nbuf[:, i * L:(i + 1) * L], n_dz))
    sums_1(NODE_G)
    pass_on(2)
    spread = mm_tn(onehot[...], e_dz[...])
    spread_low = spread.astype(BF)
    rim_out[0] = spread_low[0:RIM]
    rim_out[1] = spread_low[RIM + NODES:]
    send(rim_out.at[0], rim_in.at[0], S_RIM, R_RIM, down)
    send(rim_out.at[1], rim_in.at[1], S_RIM, R_RIM, up)
    put(EDGE_G, L, mm_tn(xext[...], spread_low))
    put(EDGE_G, 0, mm_tn(es[...], e_dz[...]))
    put(EDGE_G, 2 * L, mm_tn(x, tsum[...]))
    put(EDGE_G, 3 * L, mm_tn(e_a[...], e_dy[...]))
    sums_1(EDGE_G)
    sums_1b(NODE_G)
    pass_on(3)
    own_low = dzown[...].reshape(NODES, L).astype(BF)
    put(CONTACT_G, 0, mm_tn(x, own_low))
    hidden = jnp.concatenate(
        [dz_near[k, 0, 0:ROWS].reshape(ROWS * BLOCK, COLS) for k in range(COLORS)], axis=1
    )
    put(CONTACT_G, L, mm_tn(c_x[...], hidden))
    put(CONTACT_G, 2 * L, mm_tn(c_a[...], c_dy[...]))
    sums_1(CONTACT_G)
    sums_1b(EDGE_G)
    sums_2(NODE_G)

    sent(plane.at[:, pl.ds(0, 16)], S_F2)
    sent(plane.at[:, pl.ds(0, 8)], S_F2B)
    sent(r3, S_F1)

    @pl.loop(0, 2 * 16)
    def _(s):
        for k in range(COLORS):
            total = jnp.zeros((BLOCK, COLS), F32)
            for at, j in enumerate((0, 1, 3)):
                for i in range(2):
                    total += dz_near[k, at, table_s[2 * j + i, k * 32 + s]].astype(F32)
            plane[k, s] = total.astype(BF)

    sums_1b(CONTACT_G)
    sums_2(EDGE_G)
    sums_3(NODE_G)
    arrived(dz_far.at[:, pl.ds(0, ROWS)], R_B1B)

    def slot_sum(k, s):
        total = plane[k, s].astype(F32)
        for i in range(2):
            total += dz_far[k, table_s[4 + i, k * 32 + s]].astype(F32)
        return total

    own, near, far, last = [[around(a2, off) * 8 for a1, a2, a3 in ORDERS] for off in range(4)]

    @pl.loop(0, 8)
    def _(s):
        for k in range(COLORS):
            plane[k, far[k] + s] = slot_sum(k, far[k] + s).astype(BF)

    for k, (a1, a2, a3) in enumerate(ORDERS):
        send(plane.at[k, pl.ds(far[k], 4)], r2h.at[k, 0], S_B2H, R_B2H, peer(a2, 1))
        send(plane.at[k, pl.ds(far[k] + 4, 4)], r2h.at[k, 1], S_B2H, R_B2H, peer(a2, 3))
    sums_2(CONTACT_G)
    sums_3(EDGE_G)
    sums_4(NODE_G)

    @pl.loop(0, 4)
    def _(s):
        for k in range(COLORS):
            plane[k, near[k] + 4 + s] = slot_sum(k, near[k] + 4 + s).astype(BF)
            plane[k, last[k] + s] = slot_sum(k, last[k] + s).astype(BF)

    arrived(r2h, R_B2H)

    @pl.loop(0, 4)
    def _(s):
        for k in range(COLORS):
            plane[k, near[k] + s] = (slot_sum(k, near[k] + s) + r2h[k, 0, s].astype(F32)).astype(BF)
            plane[k, last[k] + 4 + s] = (slot_sum(k, last[k] + 4 + s) + r2h[k, 1, s].astype(F32)).astype(BF)

    for k, (a1, a2, a3) in enumerate(ORDERS):
        send(plane.at[k, pl.ds(near[k], 8)], r2.at[k, 0], S_B2, R_B2, peer(a2, 1))
        send(plane.at[k, pl.ds(last[k], 8)], r2.at[k, 1], S_B2, R_B2, peer(a2, 3))
    sums_3(CONTACT_G)
    sums_4(EDGE_G)
    sums_5(NODE_G)

    @pl.loop(0, 8)
    def _(s):
        for k in range(COLORS):
            plane[k, own[k] + s] = slot_sum(k, own[k] + s).astype(BF)

    grad = ncot + mm_nt(n_dz, wni[0:L]) + mm_nt(tsum[...], wei[2 * L:]) + mm_nt(own_low, wci[0:L])

    sums_4(CONTACT_G)
    sums_5(EDGE_G)
    sums_6(NODE_G)
    arrived(r2, R_B2)
    for k, (a1, a2, a3) in enumerate(ORDERS):
        @pl.loop(0, 8)
        def _(s):
            total = plane[k, coord[a2] * 8 + s].astype(F32)
            for o in range(2):
                total += r2[k, o, s].astype(F32)
            r3src[k, s] = total.astype(BF)

        for off in (1, 2, 3):
            send(
                r3src.at[k, pl.ds(around(a1, off) * 2, 2)], r3.at[k, off - 1],
                S_B3, R_B3, peer(a1, off),
            )
    sums_5(CONTACT_G)
    sums_6(EDGE_G)
    sums_7(NODE_G)
    arrived(rim_in, R_RIM)
    first = spread[RIM:2 * RIM] + rim_in[1].astype(F32) * has_low
    last = spread[NODES:NODES + RIM] + rim_in[0].astype(F32) * has_high
    own_spread = jnp.concatenate([first, spread[2 * RIM:NODES], last], axis=0).astype(BF)
    grad += mm_nt(own_spread, wei[L:2 * L])
    arrived(r3, R_B3)
    cols = []
    for k, (a1, a2, a3) in enumerate(ORDERS):
        halves = [r3src[k, coord[a1] * 2 + b].astype(F32) for b in range(2)]
        for off in (1, 2, 3):
            halves = [halves[b] + r3[k, off - 1, b].astype(F32) for b in range(2)]
        cols.append(jnp.concatenate(halves, axis=0).astype(BF))
    s_rem = jnp.concatenate(cols, axis=1)
    node_grad[...] = (grad + mm_nt(s_rem, wci[L:])).astype(BF)
    write(node_grad, node_grad_hbm, 13)
    sums_6(CONTACT_G)
    sums_7(EDGE_G)
    sums_7(CONTACT_G)


    for ref, sem in (
        (meta_v.at[:, pl.ds(1, 3)], S_META), (halo, S_HALO), (rim_in, S_RIM), (hs, S_H), (sbuf, S_F3), (sbuf, S_B1),
        (dz_far.at[:, pl.ds(0, ROWS)], S_B1B), (r2h, S_B2H), (r2, S_B2), (r3, S_B3),
    ):
        sent(ref, sem)
    for n in range(3):
        refs = (g1h[n], g1[n], g2[n], g2[n], g2[n], gout[n].at[:, pl.ds(0, 2)], gout[n].at[:, 0])
        for i, ref in enumerate(refs):
            sent(ref, S_G + 7 * n + i)
    for out in outs:
        out.wait()


def dma(*shape):
    return pltpu.SemaphoreType.DMA(shape)


def vm(shape, dtype):
    return pltpu.VMEM(shape, dtype)


def fused(x, src, ncot, block, host, remote, es, ecot, wei, weo, wni, wno, wci, wco):
    tile = (BLOCK, COLS)
    pieces = [rows // 16 for rows in GROUPS]
    scratch = [
        vm((EDGES, L), BF), vm((EDGES, L), BF), vm((3 * L, L), BF), vm((L, L), BF), vm((3 * L, L), BF),
        vm((L, L), BF), vm((2 * L, L), BF), vm((L, L), BF),
        vm((COLORS, 32) + tile, BF),
        vm((COLORS, 2, ROWS, HALF, COLS), BF),
        [vm((COLORS, 2, CHUNK, HALF, COLS), BF) for _ in range(N_CHUNK)],
        vm((COLORS, 2, ROWS) + tile, BF),
        [vm((COLORS, 3, CHUNK) + tile, BF) for _ in range(N_CHUNK)],
        vm((COLORS, 3, ROWS + 1) + tile, BF), vm((COLORS, ROWS + 1) + tile, BF),
        vm((COLORS, 2, 4) + tile, BF), vm((COLORS, 2, 8) + tile, BF), vm((COLORS, 3, 2) + tile, BF), vm((COLORS, 8) + tile, BF),
        [vm((COLORS, rows, COLS), BF) for rows in GROUPS],
        [vm((COLORS, 2, rows // 8, COLS), BF) for rows in GROUPS],
        [vm((COLORS, 2, rows // 4, COLS), BF) for rows in GROUPS],
        [vm((COLORS, SIDE, piece, COLS), BF) for piece in pieces],
        [vm((COLORS, 3, piece, COLS), BF) for piece in pieces],
        [vm((COLORS, SIDE, piece, COLS), BF) for piece in pieces],
        [vm((COLORS, SIDE, SIDE, piece, COLS), BF) for piece in pieces],
        vm((NODES, L), BF), vm((EDGES, L), BF), vm((NODES, L), BF), vm((EDGES, L), BF),
        vm((2, RIM, L), BF), vm((2, RIM, L), BF), vm((2, RIM, L), BF), vm((NODES + 2 * RIM, L), BF), vm((EDGES, L), BF),
        vm((3, SIDE, ROWS, 128), jnp.int32), pltpu.SMEM((3, SIDE, ROWS, 128), jnp.int32),
        vm((8, 128), jnp.int32), pltpu.SMEM((8, 128), jnp.int32),
        vm((EDGES, L), BF), vm((EDGES, 1), F32), vm((EDGES, L), F32), vm((EDGES, L), BF),
        vm((EDGES, L), BF), vm((EDGES, L), BF), vm((NODES, L), BF),
        vm((ROWS * BLOCK, L), BF), vm((ROWS * BLOCK, L), BF), vm((ROWS * BLOCK, 1), F32), vm((ROWS * BLOCK, L), F32),
        vm((ROWS * BLOCK, L), BF),
        vm((ROWS * BLOCK, L), BF), vm((2, BLOCK, L), F32), vm((2, BLOCK, L), F32), vm((2, BLOCK, L), F32),
        vm((NODES, L), BF), vm((NODES, 3 * L), BF), vm((2, BLOCK, L), BF), vm((NODES, L), BF),
        dma(56), dma(S_G + 21), dma(R_G + 21),
        vm((NODES, L), BF), vm((8, 128), jnp.int32), vm((NODES, L), BF),
        *[pltpu.SMEM((ROWS,), jnp.int32) for _ in range(3)],
    ]
    there = pl.BlockSpec(memory_space=pl.ANY)
    return pl.pallas_call(
        body,
        out_shape=(
            jax.ShapeDtypeStruct((NODES, L), BF), jax.ShapeDtypeStruct((EDGES, L), BF),
            jax.ShapeDtypeStruct((NODES, L), BF), jax.ShapeDtypeStruct((EDGES, L), BF),
        ) + tuple(jax.ShapeDtypeStruct((COLORS, SIDE, SIDE, piece, COLS), BF) for piece in pieces),
        in_specs=[there] * 14,
        out_specs=[there] * 7,
        scratch_shapes=scratch,
        compiler_params=pltpu.CompilerParams(
            collective_id=0, has_side_effects=True, vmem_limit_bytes=63 * 1024 * 1024
        ),
        name="layer",
    )(x, src, ncot, block, host, remote, es, ecot, wei, weo, wni, wno, wci, wco)


def finish_body(*refs):
    plain_in, packed_in = refs[0:4], refs[4:7]
    plain_out, wide_out = refs[7:11], refs[11:17]
    plain, packed, wide, in_sem, out_sem = refs[17:21], refs[21:24], refs[24:27], refs[27], refs[28]
    chunks = []
    for n, count in enumerate((3, 2, 3)):
        chunks += [(n, i * L, 2 * n + i // count, i % count * L) for i in range(count + 1)]
    loads = [
        pltpu.make_async_copy(packed_in[n].at[:, pl.ds(row, L)], packed[n].at[:, pl.ds(row, L)], in_sem.at[i])
        for i, (n, row, _, _) in enumerate(chunks)
    ]
    loads += [pltpu.make_async_copy(plain_in[i], plain[i], in_sem.at[len(chunks) + i]) for i in range(4)]
    for load in loads:
        load.start()
    stores = []

    def store(src, dst):
        copy = pltpu.make_async_copy(src, dst, out_sem.at[len(stores)])
        copy.start()
        stores.append(copy)

    for i, (n, row, which, there) in enumerate(chunks):
        loads[i].wait()
        for k in range(COLORS):
            wide[n][row:row + L, k * COLS:(k + 1) * COLS] = packed[n][k, row:row + L].astype(F32)
        store(wide[n].at[pl.ds(row, L)], wide_out[which].at[pl.ds(there, L)])
    for i in range(4):
        loads[len(chunks) + i].wait()
        store(plain[i], plain_out[i])
    for copy in stores:
        copy.wait()


def finish(plain, packed):
    packed = [p.reshape(COLORS, rows, COLS) for p, rows in zip(packed, GROUPS)]
    there = pl.BlockSpec(memory_space=pl.ANY)
    shapes = [jax.ShapeDtypeStruct(p.shape, p.dtype) for p in plain]
    shapes += [jax.ShapeDtypeStruct((n * L, L), F32) for n in (3, 1, 2, 1, 3, 1)]
    return pl.pallas_call(
        finish_body,
        out_shape=shapes,
        in_specs=[there] * 7,
        out_specs=[there] * 10,
        scratch_shapes=[
            *[vm(p.shape, p.dtype) for p in plain],
            *[vm((COLORS, rows, COLS), BF) for rows in GROUPS],
            *[vm((rows, L), F32) for rows in GROUPS],
            dma(15), dma(15),
        ],
        compiler_params=pltpu.CompilerParams(vmem_limit_bytes=63 * 1024 * 1024),
        name="finish",
    )(*plain, *packed)


def on_device(
    node_state, edge_state, edge_source, contact_block, contact_host, contact_remote,
    w_edge_in, w_edge_out, w_node_in, w_node_out, w_contact_in, w_contact_out, node_cot, edge_cot,
):
    results = fused(
        node_state, edge_source.reshape(8, 128), node_cot, contact_block, contact_host.reshape(ROWS), contact_remote,
        edge_state, edge_cot, w_edge_in, w_edge_out, w_node_in, w_node_out, w_contact_in, w_contact_out,
    )
    out = finish(results[:4], results[4:])
    node_in, node_last, contact_in, contact_last, edge_in, edge_last = out[4:]
    return tuple(out[:4]) + (edge_in, edge_last, node_in, node_last, contact_in, contact_last)


def solution(mesh):
    rows = P(("rep", "dom"), None)
    flat = P(("rep", "dom"))
    weight = P("rep", None)
    return jax.shard_map(
        on_device,
        mesh=mesh,
        in_specs=(rows, rows, flat, flat, rows, flat) + (weight,) * 6 + (rows, rows),
        out_specs=(rows,) * 4 + (weight,) * 6,
        check_vma=False,
    )
```
